32 devices in a mesh: slab: 8 (over z, x), hodlr: 4 (over y, core).
Axes of the slice: x: 2, y: 2, z: 4, core: 2. Of those that a mesh axis runs over, the one named last changes fastest.
Arguments:
- sources: bfloat16 [8, 32, 16384], P('slab', None, 'hodlr'), may hold values from -2 to 2
- leaves: bfloat16 [8, 16, 1024, 1024], P('slab', 'hodlr'), may hold values from -1 to 2
- v_rows: bfloat16 [8, 4, 64, 16384], P('slab', None, None, 'hodlr'), may hold values from -0.0625 to 0.0625
- u_rows: bfloat16 [8, 4, 64, 16384], P('slab', None, None, 'hodlr'), may hold values from -0.1875 to 0.1875
Outputs:
- fronts: bfloat16 [8, 32, 16384], P('slab', None, 'hodlr')
The draws below stay inside these ranges and needn't reach their ends.
All inputs are finite; a program needn't handle non-finite values.
Results may differ from the reference program's by a relative error of at most 0.025.
Values may be sent and summed in bfloat16 or wider, within the bound.
No kernel may reach another device: no remote copies, remote signals or barrier semaphores. Data moves between devices by JAX's collectives and lax.ppermute only.
A program may use at most 64 MiB of HBM per device.

```python
import math
import jax
import jax.numpy as jnp
from jax import lax

LEAF = 1024
BLOCK_RANK = 64
LEVELS = 4
SHOTS = 32
SLABS = 8
INTERFACE_SIZE = 16384
NLEAF = 16


def draw_leaves(key, part):
    shape = (SLABS, NLEAF, LEAF, LEAF)
    spread = jax.random.truncated_normal(key, -4.0, 4.0, shape, jnp.float32)
    unit = jnp.eye(LEAF, dtype=jnp.float32)
    return (0.85 * unit + 0.3 * spread / math.sqrt(LEAF)).astype(jnp.bfloat16)


def shard_levels(key, dims, cuts, smallest, largest):
    loudness = 1.0
    for dim, shards_of in cuts:
        steps = jax.random.uniform(jax.random.fold_in(jax.random.fold_in(key, 6), dim), (shards_of,), jnp.float32, smallest / len(cuts), largest / len(cuts))
        loudness = loudness * jnp.repeat(jnp.exp(steps), dims[dim] // shards_of).reshape((-1,) + (1,) * (len(dims) - 1 - dim))
    return loudness


def normal_values(own_key, dims, scale, most, split=(), held_as=jnp.bfloat16):
    result = jax.random.normal(own_key, dims, jnp.float32) * scale
    if len(split) > 0:
        result = shard_levels(own_key, dims, split, -0.22, 0.18) * result
    return jnp.clip(result, min=-most, max=most).astype(held_as)


def setup_inputs(seed: int = 0) -> dict:
    arg_keys = jax.random.split(jax.random.key(seed), 5)
    return {
        "sources": normal_values(arg_keys[0], (SLABS, SHOTS, INTERFACE_SIZE), 0.3, 2.0, ((0, 8), (2, 4))),
        "leaves": draw_leaves(jax.random.fold_in(arg_keys[4], 71), 0),
        "v_rows": normal_values(arg_keys[2], (SLABS, LEVELS, BLOCK_RANK, INTERFACE_SIZE), (INTERFACE_SIZE // 2) ** -0.5, 0.0625, ((0, 8), (3, 4))),
        "u_rows": normal_values(arg_keys[3], (SLABS, LEVELS, BLOCK_RANK, INTERFACE_SIZE), (16 * BLOCK_RANK) ** -0.5, 0.1875, ((0, 8), (3, 4))),
    }


def apply_slab(w, leaf, right_factor_transposed, left_factor_transposed):
    shot_batch = w.shape[0]
    wide_rows = w.astype(jnp.float32)
    sweep_output = jnp.einsum("sbj,bjo->sbo", wide_rows.reshape(shot_batch, NLEAF, LEAF), leaf.astype(jnp.float32), precision=lax.Precision.HIGHEST).reshape(shot_batch, INTERFACE_SIZE)
    for tree_level in range(1, LEVELS + 1):
        block_list = 2 ** tree_level
        block_size = INTERFACE_SIZE // block_list
        projection_rows = jnp.einsum("kqc,vqc->kqv", wide_rows.reshape(shot_batch, block_list, block_size), right_factor_transposed[tree_level - 1].astype(jnp.float32).reshape(BLOCK_RANK, block_list, block_size), precision=lax.Precision.HIGHEST)
        projection_rows = lax.optimization_barrier(projection_rows.astype(jnp.bfloat16)).astype(jnp.float32)
        swapped_halves = projection_rows.reshape(shot_batch, block_list // 2, 2, BLOCK_RANK)[:, :, ::-1].reshape(shot_batch, block_list, BLOCK_RANK)
        sweep_output = sweep_output + jnp.einsum("cwp,pwi->cwi", swapped_halves, left_factor_transposed[tree_level - 1].astype(jnp.float32).reshape(BLOCK_RANK, block_list, block_size), precision=lax.Precision.HIGHEST).reshape(shot_batch, INTERFACE_SIZE)
    return sweep_output.astype(jnp.bfloat16)


def reference(sources, leaves, v_rows, u_rows):
    def advance(front, inputs):
        source, leaf, right_factor_transposed, left_factor_transposed = inputs
        w = (source.astype(jnp.float32) + front.astype(jnp.float32)).astype(jnp.bfloat16)
        swept = apply_slab(w, leaf, right_factor_transposed, left_factor_transposed)
        return swept, swept

    start = jnp.zeros((SHOTS, INTERFACE_SIZE), jnp.bfloat16)
    _, fronts = lax.scan(advance, start, (sources, leaves, v_rows, u_rows))
    return fronts
```

```python
import functools

import jax
import jax.numpy as jnp
from jax import lax
from jax.experimental import pallas as pl
from jax.experimental.pallas import tpu as pltpu
from jax.sharding import PartitionSpec as P

VMEM_LIMIT = 24 * 1024 * 1024
ROWS_TIMES_COLUMNS = (((1,), (0,)), ((), ()))
ROWS_TIMES_ROWS = (((1,), (1,)), ((), ()))


def dot(a, b, dims=ROWS_TIMES_COLUMNS):
    return lax.dot_general(a, b, dims, preferred_element_type=jnp.float32)


def in_vmem(x):
    return pltpu.with_memory_space_constraint(x, pltpu.VMEM)


def call(kernel, outs, args, flops, aliases=None):
    whole = pl.BlockSpec(memory_space=pltpu.VMEM)
    bytes_accessed = sum(a.size * a.dtype.itemsize for a in args)
    return pl.pallas_call(
        kernel,
        out_shape=outs,
        in_specs=[whole] * len(args),
        out_specs=[whole] * len(outs),
        input_output_aliases=aliases or {},
        compiler_params=pltpu.CompilerParams(vmem_limit_bytes=VMEM_LIMIT),
        cost_estimate=pl.CostEstimate(flops=flops, bytes_accessed=bytes_accessed, transcendentals=0),
    )(*[in_vmem(a) for a in args])


def project_kernel(w_ref, v_ref, p_ref):
    p_ref[...] = dot(w_ref[...], v_ref[...], ROWS_TIMES_ROWS)


def project(w, v):
    outs = [pltpu.VMEM((w.shape[0], v.shape[0]), jnp.float32)]
    return call(project_kernel, outs, [w, v], 2 * w.size * v.shape[0])[0]


def step_kernel(rank, cross, has_front, parts, has_next, *refs):
    refs = list(refs)
    w_ref, q_ref = refs[:2]
    del refs[:2]
    front_ref = refs.pop(0) if has_front else None
    part_refs = refs[: len(parts)]
    del refs[: len(parts)]
    leaf_ref, u_ref, vl_ref = refs[:3]
    del refs[:3]
    next_ref = refs.pop(0) if has_next else None
    out_ref, w_out, q_out = refs[:3]
    p_out = refs[3] if has_next else None

    nleaf, size, _ = leaf_ref.shape
    rows = w_ref.shape[0]
    near = vl_ref.shape[0]
    far = u_ref.shape[0] - near

    w = w_ref[...]
    if has_front:
        w = (w.astype(jnp.float32) + front_ref[...].astype(jnp.float32)).astype(jnp.bfloat16)
    w_out[...] = w
    q = q_ref[...]
    lane = lax.broadcasted_iota(jnp.int32, (rows, far), 1) // rank
    for ref, level in zip(part_refs, parts):
        q = q + jnp.where(lane == level, ref[...], 0.0)
    q_out[...] = q
    q = q.astype(jnp.bfloat16)

    pieces = [w_out[:, c * size : (c + 1) * size] for c in range(nleaf)]
    projected = [
        dot(pieces[c], vl_ref[:, c * size : (c + 1) * size], ROWS_TIMES_ROWS) for c in range(nleaf)
    ]
    near_lane = lax.broadcasted_iota(jnp.int32, (rows, near), 1) // rank
    swapped = [jnp.zeros((rows, near), jnp.float32) for _ in range(nleaf)]
    for level in range(near // rank):
        span = nleaf >> (level + 1)
        sums = [
            functools.reduce(jnp.add, projected[b * span : (b + 1) * span]) for b in range(nleaf // span)
        ]
        for c in range(nleaf):
            swapped[c] = jnp.where(near_lane == level, sums[(c // span) ^ 1], swapped[c])
    total = None
    for c in range(nleaf):
        columns = slice(c * size, (c + 1) * size)
        value = dot(pieces[c], leaf_ref[c])
        value = value + dot(q, u_ref[:far, columns])
        value = value + dot(swapped[c].astype(jnp.bfloat16), u_ref[far:, columns])
        value = value.astype(jnp.bfloat16)
        out_ref[:, columns] = value
        if has_next:
            term = dot(value, next_ref[:, columns], ROWS_TIMES_ROWS)
            total = term if total is None else total + term
    if has_next:
        p_out[...] = total


def step(w, q, front, parts, levels_of, leaf, u, vl, following, rank, cross, last):
    has_front = front is not None
    has_next = following is not None
    args = [w, q] + ([front] if has_front else []) + list(parts) + [leaf, u, vl]
    args += [following] if has_next else []
    space = jax.ShapeDtypeStruct if last else pltpu.VMEM
    outs = [
        space(w.shape, jnp.bfloat16),
        pltpu.VMEM(w.shape, jnp.bfloat16),
        pltpu.VMEM(q.shape, jnp.float32),
    ]
    outs += [pltpu.VMEM(q.shape, jnp.float32)] if has_next else []
    flops = 2 * w.shape[0] * (leaf.size + u.size + vl.size + (following.size if has_next else 0))
    kernel = functools.partial(step_kernel, rank, cross, has_front, tuple(levels_of[: len(parts)]), has_next)
    found = call(kernel, outs, args, flops, {0: 1, 1: 2})
    return found if has_next else (*found, None)


def local(groups, sources, leaves, v_rows, u_rows):
    devices = lax.axis_size("hodlr")
    chain = lax.axis_size("slab")
    cross = devices.bit_length() - 1
    source, leaf, right, left = sources[0], leaves[0], v_rows[0], u_rows[0]
    levels, rank, width = right.shape
    far_v = right[:cross].reshape(cross * rank, width)
    near_v = right[cross:].reshape((levels - cross) * rank, width)
    u = left.reshape(levels * rank, width)
    offsets = list(range(1, devices))
    levels_of = [cross - x.bit_length() for x in offsets]
    batch = source.shape[0] // groups

    def moved(x, route):
        return lax.ppermute(x, ("slab", "hodlr"), route)

    def exchanged(p, moves):
        return [
            moved(p, [(a * devices + h, b * devices + (h ^ x)) for a, b in moves for h in range(devices)])
            for x in offsets
        ]

    shifted = moved(
        far_v,
        [(k * devices + h, (k - 1) * devices + h) for k in range(2, chain) for h in range(devices)],
    )

    rows = [slice(g * batch, (g + 1) * batch) for g in range(groups)]
    w = [source[r] for r in rows]
    first = project(source, far_v)
    first = exchanged(first, [(k, k) for k in range(chain)])
    q = [jnp.zeros((batch, cross * rank), jnp.float32) for _ in rows]
    parts = [[p[r] for p in first] for r in rows]
    front = [None] * groups
    sent = [None] * groups
    for k in range(chain):
        for g in range(groups):
            if k == 1:
                parts[g] = exchanged(project(front[g], far_v), [(1, 1)])
            last = k == chain - 1
            following = shifted if 0 < k < chain - 1 else None
            out, w[g], q[g], p = step(
                w[g], q[g], front[g], parts[g], levels_of, leaf, u, near_v, following, rank, cross, last
            )
            if last:
                sent[g] = out
                continue
            front[g] = moved(
                out, [(k * devices + h, (k + 1) * devices + h) for h in range(devices)]
            )
            parts[g] = exchanged(p, [(k, k + 1)]) if following is not None else []
    swept = sent[0] if groups == 1 else jnp.concatenate(sent, axis=0)
    return swept[None]


def solution(mesh):
    in_specs = (
        P("slab", None, "hodlr"),
        P("slab", "hodlr", None, None),
        P("slab", None, None, "hodlr"),
        P("slab", None, None, "hodlr"),
    )
    out_specs = P("slab", None, "hodlr")
    return jax.shard_map(
        functools.partial(local, 1), mesh=mesh, in_specs=in_specs, out_specs=out_specs, check_vma=False
    )
```

```python
import functools

import jax
import jax.numpy as jnp
from jax import lax
from jax.experimental import pallas as pl
from jax.experimental.pallas import tpu as pltpu
from jax.sharding import PartitionSpec as P

VMEM_LIMIT = 24 * 1024 * 1024
FIRST_SHARE = 3
ROWS_TIMES_COLUMNS = (((1,), (0,)), ((), ()))
ROWS_TIMES_ROWS = (((1,), (1,)), ((), ()))


def dot(a, b, dims=ROWS_TIMES_COLUMNS):
    return lax.dot_general(a, b, dims, preferred_element_type=jnp.float32)


def call(kernel, outs, args, aliases=None, scratch=(), from_hbm=()):
    whole = pl.BlockSpec(memory_space=pltpu.VMEM)
    remote = pl.BlockSpec(memory_space=pl.ANY)
    placed = [
        pltpu.with_memory_space_constraint(a, pltpu.HBM if i in from_hbm else pltpu.VMEM)
        for i, a in enumerate(args)
    ]
    return pl.pallas_call(
        kernel,
        out_shape=outs,
        in_specs=[remote if i in from_hbm else whole for i in range(len(args))],
        out_specs=[whole] * len(outs),
        scratch_shapes=scratch,
        input_output_aliases=aliases or {},
        compiler_params=pltpu.CompilerParams(vmem_limit_bytes=VMEM_LIMIT),
        cost_estimate=pl.CostEstimate(flops=0, bytes_accessed=0, transcendentals=0),
    )(*placed)


def open_kernel(spans, source_ref, v_ref, p_ref, far_ref, *refs):
    parts, sems = refs[: len(spans)], refs[len(spans)]
    copies = [pltpu.make_async_copy(v_ref.at[pl.ds(0, far_ref.shape[0])], far_ref, sems.at[len(spans)])]
    for i, (ref, (start, stop)) in enumerate(zip(parts, spans)):
        columns = pl.ds(start, stop - start)
        copies.append(pltpu.make_async_copy(source_ref.at[:, columns], ref, sems.at[i]))
    for copy in copies:
        copy.start()
    for copy in copies:
        copy.wait()
    far = far_ref[...].reshape(-1, far_ref.shape[2])
    total = None
    for ref, (start, stop) in zip(parts, spans):
        term = dot(ref[...], far[:, start:stop], ROWS_TIMES_ROWS)
        total = term if total is None else total + term
    p_ref[...] = total


def open_sweep(spans, cross, source, v):
    shots, width = source.shape
    rank = v.shape[1]
    outs = [
        pltpu.VMEM((shots, cross * rank), jnp.float32),
        pltpu.VMEM((cross, rank, width), v.dtype),
    ] + [pltpu.VMEM((shots, stop - start), source.dtype) for start, stop in spans]
    found = call(
        functools.partial(open_kernel, spans),
        outs,
        [source, v],
        scratch=[pltpu.SemaphoreType.DMA((len(spans) + 1,))],
        from_hbm=(0, 1),
    )
    return found[0], found[1].reshape(cross * rank, width), list(found[2:])


def leaves_of(span, size):
    return range(span[0] // size, span[1] // size)


def first_kernel(spans, cross, *refs):
    n = len(spans)
    w_refs, (leaf_ref, u_ref, v_ref) = refs[:n], refs[n : n + 3]
    leaf_out, u_out, near_out = refs[n + 3 : n + 6]
    sum_refs, p_refs, sems = refs[n + 6 : 2 * n + 6], refs[2 * n + 6 : 3 * n + 6], refs[3 * n + 6]
    nleaf, size, _ = leaf_out.shape
    near_copy = pltpu.make_async_copy(v_ref.at[pl.ds(cross, near_out.shape[0])], near_out, sems.at[0])
    u_copy = pltpu.make_async_copy(u_ref, u_out, sems.at[1])
    leaf_copies = [
        pltpu.make_async_copy(leaf_ref.at[c], leaf_out.at[c], sems.at[2 + c]) for c in range(nleaf)
    ]
    for copy in [near_copy, *leaf_copies, u_copy]:
        copy.start()
    near_copy.wait()
    near = near_out[...].reshape(-1, near_out.shape[2])
    for i, span in enumerate(spans):
        for j, c in enumerate(leaves_of(span, size)):
            columns = slice(j * size, (j + 1) * size)
            p_refs[i][j] = dot(w_refs[i][:, columns], near[:, c * size : (c + 1) * size], ROWS_TIMES_ROWS)
    for i, span in enumerate(spans):
        for j, c in enumerate(leaves_of(span, size)):
            leaf_copies[c].wait()
            columns = slice(j * size, (j + 1) * size)
            sum_refs[i][:, columns] = dot(w_refs[i][:, columns], leaf_out[c])
    u_copy.wait()


def first_part(spans, cross, w, leaf, u, v):
    levels, rank, width = v.shape
    nleaf, size, _ = leaf.shape
    rows = w[0].shape[0]
    near = (levels - cross) * rank
    outs = [
        pltpu.VMEM(leaf.shape, leaf.dtype),
        pltpu.VMEM(u.shape, u.dtype),
        pltpu.VMEM((levels - cross, rank, width), v.dtype),
    ]
    outs += [pltpu.VMEM(x.shape, jnp.float32) for x in w]
    outs += [pltpu.VMEM((x.shape[1] // size, rows, near), jnp.float32) for x in w]
    n = len(w)
    found = call(
        functools.partial(first_kernel, spans, cross),
        outs,
        [*w, leaf, u, v],
        scratch=[pltpu.SemaphoreType.DMA((2 + nleaf,))],
        from_hbm=(n, n + 1, n + 2),
    )
    leaf, u, near_v = found[:3]
    u, near_v = u.reshape(levels * rank, width), near_v.reshape(near, width)
    return leaf, u, near_v, list(found[3 : 3 + n]), list(found[3 + n :])


def project_kernel(spans, *refs):
    fronts, v_ref, p_ref = refs[: len(spans)], refs[len(spans)], refs[len(spans) + 1]
    total = None
    for ref, (start, stop) in zip(fronts, spans):
        term = dot(ref[...], v_ref[:, start:stop], ROWS_TIMES_ROWS)
        total = term if total is None else total + term
    p_ref[...] = total


def project(spans, fronts, v):
    outs = [pltpu.VMEM((fronts[0].shape[0], v.shape[0]), jnp.float32)]
    return call(functools.partial(project_kernel, spans), outs, [*fronts, v])[0]


def near_kernel(span, w_ref, front_ref, leaf_ref, v_ref, *refs):
    w_out, sum_out, p_out = refs[-3:]
    size = leaf_ref.shape[1]
    for j, c in enumerate(leaves_of(span, size)):
        columns = slice(j * size, (j + 1) * size)
        w = w_ref[:, columns] + front_ref[:, columns]
        w_out[:, columns] = w
        p_out[j] = dot(w, v_ref[:, c * size : (c + 1) * size], ROWS_TIMES_ROWS)
        sum_out[:, columns] = dot(w, leaf_ref[c])


def near_part(span, w, front, leaf, near_v, behind):
    outs = [
        pltpu.VMEM(w.shape, w.dtype),
        pltpu.VMEM(w.shape, jnp.float32),
        pltpu.VMEM((w.shape[1] // leaf.shape[1], w.shape[0], near_v.shape[0]), jnp.float32),
    ]
    return call(functools.partial(near_kernel, span), outs, [w, front, leaf, near_v, *behind], {0: 0})


def far_kernel(rank, size, spans, chosen, levels_of, has_next, has_before, *refs):
    refs = list(refs)
    sum_refs = [refs.pop(0) for _ in chosen]
    p_refs = [refs.pop(0) for _ in spans]
    q_ref = refs.pop(0)
    part_refs = [refs.pop(0) for _ in levels_of]
    u_ref = refs.pop(0)
    next_ref = refs.pop(0) if has_next else None
    before_ref = refs.pop(0) if has_before else None
    out_ref, q_out = refs[:2]
    rows, far = q_ref.shape
    near = u_ref.shape[0] - far

    q = q_ref[...]
    if levels_of:
        lane = lax.broadcasted_iota(jnp.int32, (rows, far), 1) // rank
        for ref, level in zip(part_refs, levels_of):
            q = q + jnp.where(lane == level, ref[...], 0.0)
    q_out[...] = q

    projected = [ref[j] for ref in p_refs for j in range(ref.shape[0])]
    nleaf = len(projected)
    lane = lax.broadcasted_iota(jnp.int32, (rows, near), 1) // rank
    sums = []
    for level in range(near // rank):
        block = nleaf >> (level + 1)
        sums.append(
            [
                functools.reduce(jnp.add, projected[b * block : (b + 1) * block])
                for b in range(nleaf // block)
            ]
        )
    total = before_ref[...] if has_before else None
    place = 0
    for i, ref in zip(chosen, sum_refs):
        for j, c in enumerate(leaves_of(spans[i], size)):
            swapped = sums[0][(c // (nleaf >> 1)) ^ 1]
            for level in range(1, near // rank):
                swapped = jnp.where(lane == level, sums[level][(c // (nleaf >> (level + 1))) ^ 1], swapped)
            columns = slice(c * size, (c + 1) * size)
            value = ref[:, j * size : (j + 1) * size]
            value = value + dot(q.astype(jnp.bfloat16), u_ref[:far, columns])
            value = value + dot(swapped.astype(jnp.bfloat16), u_ref[far:, columns])
            value = value.astype(jnp.bfloat16)
            out_ref[:, place : place + size] = value
            place += size
            if has_next:
                term = dot(value, next_ref[:, columns], ROWS_TIMES_ROWS)
                total = term if total is None else total + term
    if has_next:
        refs[2][...] = total


def far_part(rank, size, spans, chosen, sums, projected, q, parts, levels_of, u, following, before, last):
    has_next, has_before = following is not None, before is not None
    args = [*[sums[i] for i in chosen], *projected, q, *parts, u]
    args += ([following] if has_next else []) + ([before] if has_before else [])
    width = sum(sums[i].shape[1] for i in chosen)
    space = jax.ShapeDtypeStruct if last else pltpu.VMEM
    outs = [space((q.shape[0], width), jnp.bfloat16), pltpu.VMEM(q.shape, jnp.float32)]
    outs += [pltpu.VMEM(q.shape, jnp.float32)] if has_next else []
    levels_of = tuple(levels_of) if parts else ()
    kernel = functools.partial(far_kernel, rank, size, spans, chosen, levels_of, has_next, has_before)
    found = call(kernel, outs, args, {len(chosen) + len(projected): 1})
    return found if has_next else (*found, None)


def local(sources, leaves, v_rows, u_rows):
    devices = lax.axis_size("hodlr")
    chain = lax.axis_size("slab")
    cross = devices.bit_length() - 1
    source, right = sources[0], v_rows[0]
    levels, rank, width = right.shape
    nleaf, size = leaves.shape[1:3]
    cut = max(nleaf * FIRST_SHARE // 4, 1) * size
    spans = ((0, cut), (cut, width))
    offsets = list(range(1, devices))
    levels_of = [cross - x.bit_length() for x in offsets]

    def moved(x, moves, offset=0):
        route = [(a * devices + h, b * devices + (h ^ offset)) for a, b in moves for h in range(devices)]
        return lax.ppermute(x, ("slab", "hodlr"), route)

    def exchanged(p, moves):
        return [moved(p, moves, x) for x in offsets]

    p, far_v, w = open_sweep(spans, cross, source, right)
    parts = exchanged(p, [(k, k) for k in range(chain)])
    shifted = moved(far_v, [(k, k - 1) for k in range(2, chain)])
    leaf, u, near_v, sums, projected = first_part(spans, cross, w, leaves[0], u_rows[0], right)

    q = jnp.zeros(p.shape, jnp.float32)
    front = [None] * len(spans)
    for k in range(chain):
        if k == 1:
            parts = exchanged(project(spans, front, far_v), [(1, 1)])
        if k > 0:
            for i, span in enumerate(spans):
                behind = projected[i - 1 : i] if i else []
                w[i], sums[i], projected[i] = near_part(span, w[i], front[i], leaf, near_v, behind)
        far = functools.partial(far_part, rank, size, spans)
        if k == chain - 1:
            out, _, _ = far((0, 1), sums, projected, q, parts, levels_of, u, None, None, True)
            return out[None]
        following = shifted if k > 0 else None
        p = None
        for i in range(len(spans)):
            given = parts if i == 0 else []
            out, q, p = far((i,), sums, projected, q, given, levels_of, u, following, p, False)
            front[i] = moved(out, [(k, k + 1)])
        parts = exchanged(p, [(k, k + 1)]) if k > 0 else []


def solution(mesh):
    in_specs = (
        P("slab", None, "hodlr"),
        P("slab", "hodlr", None, None),
        P("slab", None, None, "hodlr"),
        P("slab", None, None, "hodlr"),
    )
    out_specs = P("slab", None, "hodlr")
    return jax.shard_map(local, mesh=mesh, in_specs=in_specs, out_specs=out_specs, check_vma=False)
```

```python
import functools

import jax
import jax.numpy as jnp
from jax import lax
from jax.experimental import pallas as pl
from jax.experimental.pallas import tpu as pltpu
from jax.sharding import PartitionSpec as P

VMEM_LIMIT = 24 * 1024 * 1024
FIRST_SHARE = 2
ROWS_TIMES_COLUMNS = (((1,), (0,)), ((), ()))
ROWS_TIMES_ROWS = (((1,), (1,)), ((), ()))


def dot(a, b, dims=ROWS_TIMES_COLUMNS):
    return lax.dot_general(a, b, dims, preferred_element_type=jnp.float32)


def call(kernel, outs, args, aliases=None, scratch=(), from_hbm=(), scalars=()):
    whole = pl.BlockSpec(memory_space=pltpu.VMEM)
    remote = pl.BlockSpec(memory_space=pl.ANY)
    scalar = pl.BlockSpec(memory_space=pltpu.SMEM)
    placed = [
        a if i in scalars else pltpu.with_memory_space_constraint(a, pltpu.HBM if i in from_hbm else pltpu.VMEM)
        for i, a in enumerate(args)
    ]
    return pl.pallas_call(
        kernel,
        out_shape=outs,
        in_specs=[
            scalar if i in scalars else remote if i in from_hbm else whole for i in range(len(args))
        ],
        out_specs=[whole] * len(outs),
        scratch_shapes=scratch,
        input_output_aliases=aliases or {},
        compiler_params=pltpu.CompilerParams(vmem_limit_bytes=VMEM_LIMIT),
        cost_estimate=pl.CostEstimate(flops=0, bytes_accessed=0, transcendentals=0),
    )(*placed)


def open_kernel(spans, source_ref, v_ref, p_ref, far_ref, *refs):
    parts, sems = refs[: len(spans)], refs[len(spans)]
    copies = [pltpu.make_async_copy(v_ref.at[pl.ds(0, far_ref.shape[0])], far_ref, sems.at[len(spans)])]
    for i, (ref, (start, stop)) in enumerate(zip(parts, spans)):
        columns = pl.ds(start, stop - start)
        copies.append(pltpu.make_async_copy(source_ref.at[:, columns], ref, sems.at[i]))
    for copy in copies:
        copy.start()
    for copy in copies:
        copy.wait()
    far = far_ref[...].reshape(-1, far_ref.shape[2])
    total = None
    for ref, (start, stop) in zip(parts, spans):
        term = dot(ref[...], far[:, start:stop], ROWS_TIMES_ROWS)
        total = term if total is None else total + term
    p_ref[...] = total


def open_sweep(spans, cross, source, v):
    shots, width = source.shape
    rank = v.shape[1]
    outs = [
        pltpu.VMEM((shots, cross * rank), jnp.float32),
        pltpu.VMEM((cross, rank, width), v.dtype),
    ] + [pltpu.VMEM((shots, stop - start), source.dtype) for start, stop in spans]
    found = call(
        functools.partial(open_kernel, spans),
        outs,
        [source, v],
        scratch=[pltpu.SemaphoreType.DMA((len(spans) + 1,))],
        from_hbm=(0, 1),
    )
    return found[0], found[1].reshape(cross * rank, width), list(found[2:])


def leaves_of(span, size):
    return range(span[0] // size, span[1] // size)


def first_kernel(spans, cross, *refs):
    n = len(spans)
    w_refs, (leaf_ref, u_ref, v_ref) = refs[:n], refs[n : n + 3]
    leaf_out, u_out, near_out = refs[n + 3 : n + 6]
    sum_refs, p_refs, sems = refs[n + 6 : 2 * n + 6], refs[2 * n + 6 : 3 * n + 6], refs[3 * n + 6]
    nleaf, size, _ = leaf_out.shape
    near_copy = pltpu.make_async_copy(v_ref.at[pl.ds(cross, near_out.shape[0])], near_out, sems.at[0])
    u_copy = pltpu.make_async_copy(u_ref, u_out, sems.at[1])
    leaf_copies = [
        pltpu.make_async_copy(leaf_ref.at[c], leaf_out.at[c], sems.at[2 + c]) for c in range(nleaf)
    ]
    for copy in [near_copy, *leaf_copies, u_copy]:
        copy.start()
    near_copy.wait()
    near = near_out[...].reshape(-1, near_out.shape[2])
    for i, span in enumerate(spans):
        for j, c in enumerate(leaves_of(span, size)):
            columns = slice(j * size, (j + 1) * size)
            p_refs[i][j] = dot(w_refs[i][:, columns], near[:, c * size : (c + 1) * size], ROWS_TIMES_ROWS)
    for i, span in enumerate(spans):
        for j, c in enumerate(leaves_of(span, size)):
            leaf_copies[c].wait()
            columns = slice(j * size, (j + 1) * size)
            sum_refs[i][:, columns] = dot(w_refs[i][:, columns], leaf_out[c])
    u_copy.wait()


def first_part(spans, cross, w, leaf, u, v):
    levels, rank, width = v.shape
    nleaf, size, _ = leaf.shape
    rows = w[0].shape[0]
    near = (levels - cross) * rank
    outs = [
        pltpu.VMEM(leaf.shape, leaf.dtype),
        pltpu.VMEM(u.shape, u.dtype),
        pltpu.VMEM((levels - cross, rank, width), v.dtype),
    ]
    outs += [pltpu.VMEM(x.shape, jnp.float32) for x in w]
    outs += [pltpu.VMEM((x.shape[1] // size, rows, near), jnp.float32) for x in w]
    n = len(w)
    found = call(
        functools.partial(first_kernel, spans, cross),
        outs,
        [*w, leaf, u, v],
        scratch=[pltpu.SemaphoreType.DMA((2 + nleaf,))],
        from_hbm=(n, n + 1, n + 2),
    )
    leaf, u, near_v = found[:3]
    u, near_v = u.reshape(levels * rank, width), near_v.reshape(near, width)
    return leaf, u, near_v, list(found[3 : 3 + n]), list(found[3 + n :])


def project_kernel(spans, *refs):
    fronts, v_ref, p_ref = refs[: len(spans)], refs[len(spans)], refs[len(spans) + 1]
    total = None
    for ref, (start, stop) in zip(fronts, spans):
        term = dot(ref[...], v_ref[:, start:stop], ROWS_TIMES_ROWS)
        total = term if total is None else total + term
    p_ref[...] = total


def project(spans, fronts, v):
    outs = [pltpu.VMEM((fronts[0].shape[0], v.shape[0]), jnp.float32)]
    return call(functools.partial(project_kernel, spans), outs, [*fronts, v])[0]


def near_kernel(span, start, w_ref, front_ref, leaf_ref, v_ref, *refs):
    w_out, sum_out, p_out = refs[-3:]
    size = leaf_ref.shape[1]
    for j, c in enumerate(leaves_of(span, size)):
        columns = slice(j * size, (j + 1) * size)
        w = w_ref[:, columns] + front_ref[:, start + j * size : start + (j + 1) * size]
        w_out[:, columns] = w
        p_out[j] = dot(w, v_ref[:, c * size : (c + 1) * size], ROWS_TIMES_ROWS)
        sum_out[:, columns] = dot(w, leaf_ref[c])


def near_part(span, start, w, front, leaf, near_v, behind):
    outs = [
        pltpu.VMEM(w.shape, w.dtype),
        pltpu.VMEM(w.shape, jnp.float32),
        pltpu.VMEM((w.shape[1] // leaf.shape[1], w.shape[0], near_v.shape[0]), jnp.float32),
    ]
    return call(functools.partial(near_kernel, span, start), outs, [w, front, leaf, near_v, *behind], {0: 0})


def far_kernel(rank, size, spans, chosen, levels_of, gathered, has_next, has_before, *refs):
    refs = list(refs)
    member_ref = refs.pop(0) if gathered else None
    sum_refs = [refs.pop(0) for _ in chosen]
    p_refs = [refs.pop(0) for _ in spans]
    q_ref = refs.pop(0)
    part_refs = [refs.pop(0) for _ in range(1 if gathered else len(levels_of))]
    u_ref = refs.pop(0)
    next_ref = refs.pop(0) if has_next else None
    before_ref = refs.pop(0) if has_before else None
    out_ref, q_out = refs[:2]
    rows, far = q_ref.shape
    near = u_ref.shape[0] - far

    q = q_ref[...]
    lane = lax.broadcasted_iota(jnp.int32, (rows, far), 1) // rank
    if gathered:
        all_ref = part_refs[0]
        devices = all_ref.shape[0] // rows
        cross = far // rank
        for h in range(devices):
            apart = jnp.bitwise_xor(member_ref[0], h)
            level = cross - sum((apart >= 2**b).astype(jnp.int32) for b in range(cross))
            q = q + jnp.where(lane == level, all_ref[h * rows : (h + 1) * rows, :], 0.0)
    else:
        for ref, level in zip(part_refs, levels_of):
            q = q + jnp.where(lane == level, ref[...], 0.0)
    q_out[...] = q

    projected = [ref[j] for ref in p_refs for j in range(ref.shape[0])]
    nleaf = len(projected)
    lane = lax.broadcasted_iota(jnp.int32, (rows, near), 1) // rank
    sums = []
    for level in range(near // rank):
        block = nleaf >> (level + 1)
        sums.append(
            [
                functools.reduce(jnp.add, projected[b * block : (b + 1) * block])
                for b in range(nleaf // block)
            ]
        )
    total = before_ref[...] if has_before else None
    place = 0
    for i, ref in zip(chosen, sum_refs):
        for j, c in enumerate(leaves_of(spans[i], size)):
            swapped = sums[0][(c // (nleaf >> 1)) ^ 1]
            for level in range(1, near // rank):
                swapped = jnp.where(lane == level, sums[level][(c // (nleaf >> (level + 1))) ^ 1], swapped)
            columns = slice(c * size, (c + 1) * size)
            value = ref[:, j * size : (j + 1) * size]
            value = value + dot(q.astype(jnp.bfloat16), u_ref[:far, columns])
            value = value + dot(swapped.astype(jnp.bfloat16), u_ref[far:, columns])
            value = value.astype(jnp.bfloat16)
            out_ref[:, place : place + size] = value
            place += size
            if has_next:
                term = dot(value, next_ref[:, columns], ROWS_TIMES_ROWS)
                total = term if total is None else total + term
    if has_next:
        refs[2][...] = total


def far_part(rank, size, spans, chosen, sums, projected, q, parts, levels_of, u, following, before, last, member=None):
    has_next, has_before = following is not None, before is not None
    gathered = member is not None
    args = [member] if gathered else []
    args += [*[sums[i] for i in chosen], *projected, q, *parts, u]
    args += ([following] if has_next else []) + ([before] if has_before else [])
    width = sum(sums[i].shape[1] for i in chosen)
    space = jax.ShapeDtypeStruct if last else pltpu.VMEM
    outs = [space((q.shape[0], width), jnp.bfloat16), pltpu.VMEM(q.shape, jnp.float32)]
    outs += [pltpu.VMEM(q.shape, jnp.float32)] if has_next else []
    levels_of = tuple(levels_of) if parts else ()
    kernel = functools.partial(far_kernel, rank, size, spans, chosen, levels_of, gathered, has_next, has_before)
    scalars = (0,) if gathered else ()
    found = call(kernel, outs, args, {len(scalars) + len(chosen) + len(projected): 1}, scalars=scalars)
    return found if has_next else (*found, None)


def local(sources, leaves, v_rows, u_rows):
    devices = lax.axis_size("hodlr")
    chain = lax.axis_size("slab")
    cross = devices.bit_length() - 1
    source, right = sources[0], v_rows[0]
    levels, rank, width = right.shape
    nleaf, size = leaves.shape[1:3]
    cut = max(nleaf * FIRST_SHARE // 4, 1) * size
    spans = ((0, cut), (cut, width))
    offsets = list(range(1, devices))
    levels_of = [cross - x.bit_length() for x in offsets]

    def moved(x, moves, offset=0):
        route = [(a * devices + h, b * devices + (h ^ offset)) for a, b in moves for h in range(devices)]
        return lax.ppermute(x, ("slab", "hodlr"), route)

    def exchanged(p, moves):
        return [moved(p, moves, x) for x in offsets]

    p, far_v, w = open_sweep(spans, cross, source, right)
    parts = exchanged(p, [(k, k) for k in range(chain)])
    shifted = moved(far_v, [(k, k - 1) for k in range(2, chain)])
    leaf, u, near_v, sums, projected = first_part(spans, cross, w, leaves[0], u_rows[0], right)

    q = jnp.zeros(p.shape, jnp.float32)
    front = [None] * len(spans)
    member = jnp.full((1,), lax.axis_index("hodlr"), jnp.int32)
    far = functools.partial(far_part, rank, size, spans)
    out, q, _ = far((0, 1), sums, projected, q, parts, levels_of, u, None, None, False)
    joined = moved(out, [(0, 1)])
    gathered = lax.all_gather(project(((0, width),), [joined], far_v), "hodlr", axis=0, tiled=True)
    for k in range(1, chain):
        for i, span in enumerate(spans):
            behind = projected[i - 1 : i] if i else []
            given, start = (joined, span[0]) if k == 1 else (front[i], 0)
            w[i], sums[i], projected[i] = near_part(span, start, w[i], given, leaf, near_v, behind)
        if k == 1:
            parts = [gathered]
        first = member if k == 1 else None
        if k == chain - 1:
            out, _, _ = far((0, 1), sums, projected, q, parts, levels_of, u, None, None, True, first)
            return out[None]
        p = None
        for i in range(len(spans)):
            given = parts if i == 0 else []
            out, q, p = far((i,), sums, projected, q, given, levels_of, u, shifted, p, False, first)
            first = None
            front[i] = moved(out, [(k, k + 1)])
        parts = exchanged(p, [(k, k + 1)])


def solution(mesh):
    in_specs = (
        P("slab", None, "hodlr"),
        P("slab", "hodlr", None, None),
        P("slab", None, None, "hodlr"),
        P("slab", None, None, "hodlr"),
    )
    out_specs = P("slab", None, "hodlr")
    return jax.shard_map(local, mesh=mesh, in_specs=in_specs, out_specs=out_specs, check_vma=False)
```

```python
import functools

import jax
import jax.numpy as jnp
from jax import lax
from jax.experimental import pallas as pl
from jax.experimental.pallas import tpu as pltpu
from jax.sharding import PartitionSpec as P

VMEM_LIMIT = 24 * 1024 * 1024
FIRST_SHARE = 2
SPLIT_HOPS = 3
ROWS_TIMES_COLUMNS = (((1,), (0,)), ((), ()))
ROWS_TIMES_ROWS = (((1,), (1,)), ((), ()))


def dot(a, b, dims=ROWS_TIMES_COLUMNS):
    return lax.dot_general(a, b, dims, preferred_element_type=jnp.float32)


def call(kernel, outs, args, aliases=None, scratch=(), from_hbm=()):
    whole = pl.BlockSpec(memory_space=pltpu.VMEM)
    remote = pl.BlockSpec(memory_space=pl.ANY)
    placed = [
        pltpu.with_memory_space_constraint(a, pltpu.HBM if i in from_hbm else pltpu.VMEM)
        for i, a in enumerate(args)
    ]
    return pl.pallas_call(
        kernel,
        out_shape=outs,
        in_specs=[remote if i in from_hbm else whole for i in range(len(args))],
        out_specs=[whole] * len(outs),
        scratch_shapes=scratch,
        input_output_aliases=aliases or {},
        compiler_params=pltpu.CompilerParams(vmem_limit_bytes=VMEM_LIMIT),
        cost_estimate=pl.CostEstimate(flops=0, bytes_accessed=0, transcendentals=0),
    )(*placed)


def on_factors(value, v_refs, columns):
    return jnp.concatenate([dot(value, ref[:, columns], ROWS_TIMES_ROWS) for ref in v_refs], axis=1)


def fetch_kernel(v_ref, *refs):
    outs, sems = refs[:-1], refs[-1]
    copies, level = [], 0
    for i, out in enumerate(outs):
        copies.append(pltpu.make_async_copy(v_ref.at[pl.ds(level, out.shape[0])], out, sems.at[i]))
        level += out.shape[0]
    for copy in copies:
        copy.start()
    for copy in copies:
        copy.wait()


def fetch(shares, v):
    _, rank, width = v.shape
    outs = [pltpu.VMEM((n, rank, width), v.dtype) for n in shares]
    found = call(fetch_kernel, outs, [v], scratch=[pltpu.SemaphoreType.DMA((len(shares),))], from_hbm=(0,))
    return [f.reshape(-1, width) for f in found]


def open_kernel(spans, factors, source_ref, *refs):
    v_refs, p_ref = refs[:factors], refs[factors]
    parts, sems = refs[factors + 1 : -1], refs[-1]
    copies = []
    for i, (ref, (start, stop)) in enumerate(zip(parts, spans)):
        copies.append(pltpu.make_async_copy(source_ref.at[:, pl.ds(start, stop - start)], ref, sems.at[i]))
    for copy in copies:
        copy.start()
    total = None
    for ref, copy, (start, stop) in zip(parts, copies, spans):
        copy.wait()
        term = on_factors(ref[...], v_refs, slice(start, stop))
        total = term if total is None else total + term
    p_ref[...] = total


def open_sweep(spans, source, far_v):
    shots = source.shape[0]
    outs = [pltpu.VMEM((shots, sum(v.shape[0] for v in far_v)), jnp.float32)]
    outs += [pltpu.VMEM((shots, stop - start), source.dtype) for start, stop in spans]
    found = call(
        functools.partial(open_kernel, spans, len(far_v)),
        outs,
        [source, *far_v],
        scratch=[pltpu.SemaphoreType.DMA((len(spans),))],
        from_hbm=(0,),
    )
    return found[0], list(found[1:])


def leaves_of(span, size):
    return range(span[0] // size, span[1] // size)


def first_kernel(spans, cross, *refs):
    n = len(spans)
    w_refs, (leaf_ref, u_ref, v_ref) = refs[:n], refs[n : n + 3]
    leaf_out, u_out, near_out = refs[n + 3 : n + 6]
    sum_refs, p_refs, sems = refs[n + 6 : 2 * n + 6], refs[2 * n + 6 : 3 * n + 6], refs[3 * n + 6]
    nleaf, size, _ = leaf_out.shape
    near_copy = pltpu.make_async_copy(v_ref.at[pl.ds(cross, near_out.shape[0])], near_out, sems.at[0])
    u_copy = pltpu.make_async_copy(u_ref, u_out, sems.at[1])
    leaf_copies = [
        pltpu.make_async_copy(leaf_ref.at[c], leaf_out.at[c], sems.at[2 + c]) for c in range(nleaf)
    ]
    for copy in [near_copy, *leaf_copies, u_copy]:
        copy.start()
    near_copy.wait()
    near = near_out[...].reshape(-1, near_out.shape[2])
    for i, span in enumerate(spans):
        for j, c in enumerate(leaves_of(span, size)):
            columns = slice(j * size, (j + 1) * size)
            p_refs[i][j] = dot(w_refs[i][:, columns], near[:, c * size : (c + 1) * size], ROWS_TIMES_ROWS)
    for i, span in enumerate(spans):
        for j, c in enumerate(leaves_of(span, size)):
            leaf_copies[c].wait()
            columns = slice(j * size, (j + 1) * size)
            sum_refs[i][:, columns] = dot(w_refs[i][:, columns], leaf_out[c])
    u_copy.wait()


def first_part(spans, cross, w, leaf, u, v):
    levels, rank, width = v.shape
    nleaf, size, _ = leaf.shape
    rows = w[0].shape[0]
    near = (levels - cross) * rank
    outs = [
        pltpu.VMEM(leaf.shape, leaf.dtype),
        pltpu.VMEM(u.shape, u.dtype),
        pltpu.VMEM((levels - cross, rank, width), v.dtype),
    ]
    outs += [pltpu.VMEM(x.shape, jnp.float32) for x in w]
    outs += [pltpu.VMEM((x.shape[1] // size, rows, near), jnp.float32) for x in w]
    n = len(w)
    found = call(
        functools.partial(first_kernel, spans, cross),
        outs,
        [*w, leaf, u, v],
        scratch=[pltpu.SemaphoreType.DMA((2 + nleaf,))],
        from_hbm=(n, n + 1, n + 2),
    )
    leaf, u, near_v = found[:3]
    u, near_v = u.reshape(levels * rank, width), near_v.reshape(near, width)
    return leaf, u, near_v, list(found[3 : 3 + n]), list(found[3 + n :])


def project_kernel(before, front_ref, v_ref, *refs):
    p_ref = refs[-1]
    rows, ranks = p_ref.shape
    term = dot(front_ref[...], v_ref[...], ROWS_TIMES_ROWS)
    after = ranks - before - term.shape[1]
    pieces = [jnp.zeros((rows, before), jnp.float32)] if before else []
    pieces += [term] + ([jnp.zeros((rows, after), jnp.float32)] if after else [])
    p_ref[...] = jnp.concatenate(pieces, axis=1) if len(pieces) > 1 else term


def project(front, v, before, ranks, behind=()):
    outs = [pltpu.VMEM((front.shape[0], ranks), jnp.float32)]
    return call(functools.partial(project_kernel, before), outs, [front, v, *behind])[0]


def near_kernel(span, start, w_ref, front_ref, leaf_ref, v_ref, *refs):
    w_out, sum_out, p_out = refs[-3:]
    size = leaf_ref.shape[1]
    for j, c in enumerate(leaves_of(span, size)):
        columns = slice(j * size, (j + 1) * size)
        w = w_ref[:, columns] + front_ref[:, start + j * size : start + (j + 1) * size]
        w_out[:, columns] = w
        p_out[j] = dot(w, v_ref[:, c * size : (c + 1) * size], ROWS_TIMES_ROWS)
        sum_out[:, columns] = dot(w, leaf_ref[c])


def near_part(span, start, w, front, leaf, near_v, behind):
    outs = [
        pltpu.VMEM(w.shape, w.dtype),
        pltpu.VMEM(w.shape, jnp.float32),
        pltpu.VMEM((w.shape[1] // leaf.shape[1], w.shape[0], near_v.shape[0]), jnp.float32),
    ]
    return call(functools.partial(near_kernel, span, start), outs, [w, front, leaf, near_v, *behind], {0: 0})


def far_kernel(rank, size, spans, chosen, levels_of, nexts, has_before, *refs):
    refs = list(refs)
    sum_refs = [refs.pop(0) for _ in chosen]
    p_refs = [refs.pop(0) for _ in spans]
    q_ref = refs.pop(0)
    part_refs = [refs.pop(0) for _ in levels_of]
    u_ref = refs.pop(0)
    next_refs = [refs.pop(0) for _ in range(nexts)]
    before_ref = refs.pop(0) if has_before else None
    out_ref, q_out = refs[:2]
    rows, far = q_ref.shape
    near = u_ref.shape[0] - far

    q = q_ref[...]
    lane = lax.broadcasted_iota(jnp.int32, (rows, far), 1) // rank
    for ref, level in zip(part_refs, levels_of):
        q = q + jnp.where(lane == level, ref[...], 0.0)
    q_out[...] = q

    projected = [ref[j] for ref in p_refs for j in range(ref.shape[0])]
    nleaf = len(projected)
    lane = lax.broadcasted_iota(jnp.int32, (rows, near), 1) // rank
    sums = []
    for level in range(near // rank):
        block = nleaf >> (level + 1)
        sums.append(
            [
                functools.reduce(jnp.add, projected[b * block : (b + 1) * block])
                for b in range(nleaf // block)
            ]
        )
    total = before_ref[...] if has_before else None
    place = 0
    for i, ref in zip(chosen, sum_refs):
        for j, c in enumerate(leaves_of(spans[i], size)):
            swapped = sums[0][(c // (nleaf >> 1)) ^ 1]
            for level in range(1, near // rank):
                swapped = jnp.where(lane == level, sums[level][(c // (nleaf >> (level + 1))) ^ 1], swapped)
            columns = slice(c * size, (c + 1) * size)
            value = ref[:, j * size : (j + 1) * size]
            value = value + dot(q.astype(jnp.bfloat16), u_ref[:far, columns])
            value = value + dot(swapped.astype(jnp.bfloat16), u_ref[far:, columns])
            value = value.astype(jnp.bfloat16)
            out_ref[:, place : place + size] = value
            place += size
            if nexts:
                term = on_factors(value, next_refs, columns)
                total = term if total is None else total + term
    if nexts:
        refs[2][...] = total


def far_part(rank, size, spans, chosen, sums, projected, q, parts, levels_of, u, following, before, last):
    has_next, has_before = len(following) > 0, before is not None
    args = [*[sums[i] for i in chosen], *projected, q, *parts, u]
    args += following + ([before] if has_before else [])
    width = sum(sums[i].shape[1] for i in chosen)
    space = jax.ShapeDtypeStruct if last else pltpu.VMEM
    outs = [space((q.shape[0], width), jnp.bfloat16), pltpu.VMEM(q.shape, jnp.float32)]
    outs += [pltpu.VMEM(q.shape, jnp.float32)] if has_next else []
    levels_of = tuple(levels_of) if parts else ()
    kernel = functools.partial(far_kernel, rank, size, spans, chosen, levels_of, len(following), has_before)
    found = call(kernel, outs, args, {len(chosen) + len(projected): 1})
    return found if has_next else (*found, None)


def local(sources, leaves, v_rows, u_rows):
    devices = lax.axis_size("hodlr")
    chain = lax.axis_size("slab")
    cross = devices.bit_length() - 1
    source, right = sources[0], v_rows[0]
    levels, rank, width = right.shape
    nleaf, size = leaves.shape[1:3]
    cut = max(nleaf * FIRST_SHARE // 4, 1) * size
    spans = ((0, cut), (cut, width))
    offsets = list(range(1, devices))
    levels_of = [cross - x.bit_length() for x in offsets]

    def moved(x, moves, offset=0):
        route = [(a * devices + h, b * devices + (h ^ offset)) for a, b in moves for h in range(devices)]
        return lax.ppermute(x, ("slab", "hodlr"), route)

    def exchanged(p, moves):
        return [moved(p, moves, x) for x in offsets]

    shares = [n for n in (cross - 1, 1) if n]
    far_v = fetch(shares, right)
    shifted = [
        moved(v, [(k, k - 1) for k in range(2 if v is far_v[-1] else 1, chain)]) for v in far_v
    ]
    p, w = open_sweep(spans, source, far_v)
    parts = exchanged(p, [(k, k) for k in range(chain)])
    leaf, u, near_v, sums, projected = first_part(spans, cross, w, leaves[0], u_rows[0], right)

    ranks = cross * rank
    q = jnp.zeros(p.shape, jnp.float32)
    every = tuple(range(len(spans)))
    far = functools.partial(far_part, rank, size, spans)
    out, q, _ = far(every, sums, projected, q, parts, levels_of, u, [], None, False)
    front = [moved(out, [(0, 1)])]
    ahead = [project(out, shifted[0], 0, ranks)] if cross > 1 else []
    parts = [moved(ahead[0], [(0, 1)], x) for x in offsets[1:]]
    nearby = project(front[0], far_v[-1], ranks - rank, ranks, ahead)
    parts = [moved(nearby, [(1, 1)], offsets[0])] + parts
    for k in range(1, chain):
        for i, span in enumerate(spans):
            behind = projected[i - 1 : i] if i else []
            given, start = (front[0], span[0]) if len(front) == 1 else (front[i], 0)
            w[i], sums[i], projected[i] = near_part(span, start, w[i], given, leaf, near_v, behind)
        if k == chain - 1:
            out, _, _ = far(every, sums, projected, q, parts, levels_of, u, [], None, True)
            return out[None]
        p, front = None, []
        for chosen in [(i,) for i in every] if k >= chain - 1 - SPLIT_HOPS else [every]:
            given = [] if front else parts
            out, q, p = far(chosen, sums, projected, q, given, levels_of, u, shifted, p, False)
            front.append(moved(out, [(k, k + 1)]))
        parts = exchanged(p, [(k, k + 1)])


def solution(mesh):
    in_specs = (
        P("slab", None, "hodlr"),
        P("slab", "hodlr", None, None),
        P("slab", None, None, "hodlr"),
        P("slab", None, None, "hodlr"),
    )
    out_specs = P("slab", None, "hodlr")
    return jax.shard_map(local, mesh=mesh, in_specs=in_specs, out_specs=out_specs, check_vma=False)
```

```python
import functools

import jax
import jax.numpy as jnp
from jax import lax
from jax.experimental import pallas as pl
from jax.experimental.pallas import tpu as pltpu
from jax.sharding import PartitionSpec as P

VMEM_LIMIT = 24 * 1024 * 1024
FIRST_SHARE = 2
SPLIT_HOPS = 3
IN_PLACE = 2
ROWS_TIMES_COLUMNS = (((1,), (0,)), ((), ()))
ROWS_TIMES_ROWS = (((1,), (1,)), ((), ()))


def dot(a, b, dims=ROWS_TIMES_COLUMNS):
    return lax.dot_general(a, b, dims, preferred_element_type=jnp.float32)


def call(kernel, outs, args, aliases=None, scratch=(), from_hbm=()):
    whole = pl.BlockSpec(memory_space=pltpu.VMEM)
    remote = pl.BlockSpec(memory_space=pl.ANY)
    placed = [
        pltpu.with_memory_space_constraint(a, pltpu.HBM if i in from_hbm else pltpu.VMEM)
        for i, a in enumerate(args)
    ]
    return pl.pallas_call(
        kernel,
        out_shape=outs,
        in_specs=[remote if i in from_hbm else whole for i in range(len(args))],
        out_specs=[whole] * len(outs),
        scratch_shapes=scratch,
        input_output_aliases=aliases or {},
        compiler_params=pltpu.CompilerParams(vmem_limit_bytes=VMEM_LIMIT),
        cost_estimate=pl.CostEstimate(flops=0, bytes_accessed=0, transcendentals=0),
    )(*placed)


def on_factors(value, v_refs, columns, ranks):
    pieces = [dot(value, ref[:, columns], ROWS_TIMES_ROWS) for ref in v_refs]
    missing = ranks - sum(ref.shape[0] for ref in v_refs)
    if missing:
        pieces.append(jnp.zeros((value.shape[0], missing), jnp.float32))
    return jnp.concatenate(pieces, axis=1)


def fetch_kernel(spans, factors, source_ref, v_ref, *refs):
    v_outs, w_outs, sems = refs[:factors], refs[factors:-1], refs[-1]
    copies, level = [], 0
    for out in v_outs:
        copies.append((v_ref.at[pl.ds(level, out.shape[0])], out))
        level += out.shape[0]
    for out, (start, stop) in zip(w_outs, spans):
        copies.append((source_ref.at[:, pl.ds(start, stop - start)], out))
    copies = [pltpu.make_async_copy(a, b, sems.at[i]) for i, (a, b) in enumerate(copies)]
    for copy in copies:
        copy.start()
    for copy in copies:
        copy.wait()


def fetch(spans, shares, source, v):
    _, rank, width = v.shape
    outs = [pltpu.VMEM((n, rank, width), v.dtype) for n in shares]
    outs += [pltpu.VMEM((source.shape[0], stop - start), source.dtype) for start, stop in spans]
    found = call(
        functools.partial(fetch_kernel, spans, len(shares)),
        outs,
        [source, v],
        scratch=[pltpu.SemaphoreType.DMA((len(outs),))],
        from_hbm=(0, 1),
    )
    return [f.reshape(-1, width) for f in found[: len(shares)]], list(found[len(shares) :])


def open_kernel(spans, factors, *refs):
    v_refs, parts, p_ref = refs[:factors], refs[factors:-1], refs[-1]
    total = None
    for ref, (start, stop) in zip(parts, spans):
        term = on_factors(ref[...], v_refs, slice(start, stop), p_ref.shape[1])
        total = term if total is None else total + term
    p_ref[...] = total


def open_sweep(spans, w, far_v):
    outs = [pltpu.VMEM((w[0].shape[0], sum(v.shape[0] for v in far_v)), jnp.float32)]
    return call(functools.partial(open_kernel, spans, len(far_v)), outs, [*far_v, *w])[0]


def leaves_of(span, size):
    return range(span[0] // size, span[1] // size)


def first_kernel(spans, cross, *refs):
    n = len(spans)
    w_refs, (leaf_ref, u_ref, v_ref) = refs[:n], refs[n : n + 3]
    leaf_out, u_out, near_out = refs[n + 3 : n + 6]
    sum_refs, p_refs, sems = refs[n + 6 : 2 * n + 6], refs[2 * n + 6 : 3 * n + 6], refs[3 * n + 6]
    nleaf, size, _ = leaf_out.shape
    near_copy = pltpu.make_async_copy(v_ref.at[pl.ds(cross, near_out.shape[0])], near_out, sems.at[0])
    u_copy = pltpu.make_async_copy(u_ref, u_out, sems.at[1])
    leaf_copies = [
        pltpu.make_async_copy(leaf_ref.at[c], leaf_out.at[c], sems.at[2 + c]) for c in range(nleaf)
    ]
    for copy in [near_copy, *leaf_copies, u_copy]:
        copy.start()
    near_copy.wait()
    near = near_out[...].reshape(-1, near_out.shape[2])
    for i, span in enumerate(spans):
        for j, c in enumerate(leaves_of(span, size)):
            columns = slice(j * size, (j + 1) * size)
            p_refs[i][j] = dot(w_refs[i][:, columns], near[:, c * size : (c + 1) * size], ROWS_TIMES_ROWS)
    for i, span in enumerate(spans):
        for j, c in enumerate(leaves_of(span, size)):
            leaf_copies[c].wait()
            columns = slice(j * size, (j + 1) * size)
            sum_refs[i][:, columns] = dot(w_refs[i][:, columns], leaf_out[c])
    u_copy.wait()


def first_part(spans, cross, w, leaf, u, v):
    levels, rank, width = v.shape
    nleaf, size, _ = leaf.shape
    rows = w[0].shape[0]
    near = (levels - cross) * rank
    outs = [
        pltpu.VMEM(leaf.shape, leaf.dtype),
        pltpu.VMEM(u.shape, u.dtype),
        pltpu.VMEM((levels - cross, rank, width), v.dtype),
    ]
    outs += [pltpu.VMEM(x.shape, jnp.float32) for x in w]
    outs += [pltpu.VMEM((x.shape[1] // size, rows, near), jnp.float32) for x in w]
    n = len(w)
    found = call(
        functools.partial(first_kernel, spans, cross),
        outs,
        [*w, leaf, u, v],
        scratch=[pltpu.SemaphoreType.DMA((2 + nleaf,))],
        from_hbm=(n, n + 1, n + 2),
    )
    leaf, u, near_v = found[:3]
    u, near_v = u.reshape(levels * rank, width), near_v.reshape(near, width)
    return leaf, u, near_v, list(found[3 : 3 + n]), list(found[3 + n :])


def project_kernel(before, front_ref, v_ref, *refs):
    p_ref = refs[-1]
    rows, ranks = p_ref.shape
    term = dot(front_ref[...], v_ref[...], ROWS_TIMES_ROWS)
    after = ranks - before - term.shape[1]
    pieces = [jnp.zeros((rows, before), jnp.float32)] if before else []
    pieces += [term] + ([jnp.zeros((rows, after), jnp.float32)] if after else [])
    p_ref[...] = jnp.concatenate(pieces, axis=1) if len(pieces) > 1 else term


def project(front, v, before, ranks, behind=()):
    outs = [pltpu.VMEM((front.shape[0], ranks), jnp.float32)]
    return call(functools.partial(project_kernel, before), outs, [front, v, *behind])[0]


def near_kernel(span, start, w_ref, front_ref, leaf_ref, v_ref, *refs):
    w_out, sum_out, p_out = refs[-3:]
    size = leaf_ref.shape[1]
    for j, c in enumerate(leaves_of(span, size)):
        columns = slice(j * size, (j + 1) * size)
        w = w_ref[:, columns] + front_ref[:, start + j * size : start + (j + 1) * size]
        w_out[:, columns] = w
        p_out[j] = dot(w, v_ref[:, c * size : (c + 1) * size], ROWS_TIMES_ROWS)
        sum_out[:, columns] = dot(w, leaf_ref[c])


def near_part(span, start, w, front, leaf, near_v, behind):
    outs = [
        pltpu.VMEM(w.shape, w.dtype),
        pltpu.VMEM(w.shape, jnp.float32),
        pltpu.VMEM((w.shape[1] // leaf.shape[1], w.shape[0], near_v.shape[0]), jnp.float32),
    ]
    return call(functools.partial(near_kernel, span, start), outs, [w, front, leaf, near_v, *behind], {0: 0})


def far_kernel(rank, size, spans, chosen, levels_of, nexts, has_before, *refs):
    refs = list(refs)
    sum_refs = [refs.pop(0) for _ in chosen]
    p_refs = [refs.pop(0) for _ in spans]
    q_ref = refs.pop(0)
    part_refs = [refs.pop(0) for _ in levels_of]
    u_ref = refs.pop(0)
    next_refs = [refs.pop(0) for _ in range(nexts)]
    before_ref = refs.pop(0) if has_before else None
    out_ref, q_out = refs[:2]
    rows, far = q_ref.shape
    near = u_ref.shape[0] - far

    q = q_ref[...]
    lane = lax.broadcasted_iota(jnp.int32, (rows, far), 1) // rank
    for ref, level in zip(part_refs, levels_of):
        q = q + jnp.where(lane == level, ref[...], 0.0)
    q_out[...] = q

    projected = [ref[j] for ref in p_refs for j in range(ref.shape[0])]
    nleaf = len(projected)
    lane = lax.broadcasted_iota(jnp.int32, (rows, near), 1) // rank
    sums = []
    for level in range(near // rank):
        block = nleaf >> (level + 1)
        sums.append(
            [
                functools.reduce(jnp.add, projected[b * block : (b + 1) * block])
                for b in range(nleaf // block)
            ]
        )
    total = before_ref[...] if has_before else None
    place = 0
    for i, ref in zip(chosen, sum_refs):
        for j, c in enumerate(leaves_of(spans[i], size)):
            swapped = sums[0][(c // (nleaf >> 1)) ^ 1]
            for level in range(1, near // rank):
                swapped = jnp.where(lane == level, sums[level][(c // (nleaf >> (level + 1))) ^ 1], swapped)
            columns = slice(c * size, (c + 1) * size)
            value = ref[:, j * size : (j + 1) * size]
            value = value + dot(q.astype(jnp.bfloat16), u_ref[:far, columns])
            value = value + dot(swapped.astype(jnp.bfloat16), u_ref[far:, columns])
            value = value.astype(jnp.bfloat16)
            out_ref[:, place : place + size] = value
            place += size
            if nexts:
                term = on_factors(value, next_refs, columns, far)
                total = term if total is None else total + term
    if nexts:
        refs[2][...] = total


def far_part(rank, size, spans, chosen, sums, projected, q, parts, levels_of, u, following, before, last):
    has_next, has_before = len(following) > 0, before is not None
    args = [*[sums[i] for i in chosen], *projected, q, *parts, u]
    args += following + ([before] if has_before else [])
    width = sum(sums[i].shape[1] for i in chosen)
    space = jax.ShapeDtypeStruct if last else pltpu.VMEM
    outs = [space((q.shape[0], width), jnp.bfloat16), pltpu.VMEM(q.shape, jnp.float32)]
    outs += [pltpu.VMEM(q.shape, jnp.float32)] if has_next else []
    levels_of = tuple(levels_of) if parts else ()
    kernel = functools.partial(far_kernel, rank, size, spans, chosen, levels_of, len(following), has_before)
    found = call(kernel, outs, args, {len(chosen) + len(projected): 1})
    return found if has_next else (*found, None)


def local(sources, leaves, v_rows, u_rows):
    devices = lax.axis_size("hodlr")
    chain = lax.axis_size("slab")
    cross = devices.bit_length() - 1
    source, right = sources[0], v_rows[0]
    levels, rank, width = right.shape
    nleaf, size = leaves.shape[1:3]
    cut = max(nleaf * FIRST_SHARE // 4, 1) * size
    spans = ((0, cut), (cut, width))
    offsets = list(range(1, devices))
    levels_of = [cross - x.bit_length() for x in offsets]

    def moved(x, moves, offset=0):
        route = [(a * devices + h, b * devices + (h ^ offset)) for a, b in moves for h in range(devices)]
        return lax.ppermute(x, ("slab", "hodlr"), route)

    def exchanged(p, moves):
        return [moved(p, moves, x) for x in offsets]

    shares = [n for n in (cross - 1, 1) if n]
    far_v, w = fetch(spans, shares, source, right)
    shifted = [
        moved(v, [(k, k - 1) for k in range(IN_PLACE + 1 if v is far_v[-1] else 1, chain)]) for v in far_v
    ]
    p = open_sweep(spans, w, far_v)
    parts = exchanged(p, [(k, k) for k in range(chain)])
    leaf, u, near_v, sums, projected = first_part(spans, cross, w, leaves[0], u_rows[0], right)

    ranks = cross * rank
    q = jnp.zeros(p.shape, jnp.float32)
    every = tuple(range(len(spans)))
    far = functools.partial(far_part, rank, size, spans)
    out, q, _ = far(every, sums, projected, q, parts, levels_of, u, [], None, False)
    front = [moved(out, [(0, 1)])]
    ahead = [project(out, shifted[0], 0, ranks)] if cross > 1 else []
    parts = [moved(ahead[0], [(0, 1)], x) for x in offsets[1:]]
    for k in range(1, chain):
        if k <= IN_PLACE:
            nearby = project(front[0], far_v[-1], ranks - rank, ranks, parts)
            parts = [moved(nearby, [(k, k)], offsets[0])] + parts
        for i, span in enumerate(spans):
            behind = projected[i - 1 : i] if i else []
            given, start = (front[0], span[0]) if len(front) == 1 else (front[i], 0)
            w[i], sums[i], projected[i] = near_part(span, start, w[i], given, leaf, near_v, behind)
        if k == chain - 1:
            out, _, _ = far(every, sums, projected, q, parts, levels_of, u, [], None, True)
            return out[None]
        p, front = None, []
        following = shifted[:-1] if k < IN_PLACE else shifted
        for chosen in [(i,) for i in every] if k >= chain - 1 - SPLIT_HOPS else [every]:
            given = [] if front else parts
            out, q, p = far(chosen, sums, projected, q, given, levels_of, u, following, p, False)
            front.append(moved(out, [(k, k + 1)]))
        parts = [moved(p, [(k, k + 1)], x) for x in offsets[1 if k < IN_PLACE else 0 :]]


def solution(mesh):
    in_specs = (
        P("slab", None, "hodlr"),
        P("slab", "hodlr", None, None),
        P("slab", None, None, "hodlr"),
        P("slab", None, None, "hodlr"),
    )
    out_specs = P("slab", None, "hodlr")
    return jax.shard_map(local, mesh=mesh, in_specs=in_specs, out_specs=out_specs, check_vma=False)
```

```python
import functools

import jax
import jax.numpy as jnp
from jax import lax
from jax.experimental import pallas as pl
from jax.experimental.pallas import tpu as pltpu
from jax.sharding import PartitionSpec as P

VMEM_LIMIT = 24 * 1024 * 1024
FIRST_SHARE = 2
SPLIT_HOPS = 3
IN_PLACE = 2
ROWS_TIMES_COLUMNS = (((1,), (0,)), ((), ()))
ROWS_TIMES_ROWS = (((1,), (1,)), ((), ()))


def dot(a, b, dims=ROWS_TIMES_COLUMNS):
    return lax.dot_general(a, b, dims, preferred_element_type=jnp.float32)


def call(kernel, outs, args, aliases=None, scratch=(), from_hbm=()):
    whole = pl.BlockSpec(memory_space=pltpu.VMEM)
    remote = pl.BlockSpec(memory_space=pl.ANY)
    placed = [
        pltpu.with_memory_space_constraint(a, pltpu.HBM if i in from_hbm else pltpu.VMEM)
        for i, a in enumerate(args)
    ]
    return pl.pallas_call(
        kernel,
        out_shape=outs,
        in_specs=[remote if i in from_hbm else whole for i in range(len(args))],
        out_specs=[whole] * len(outs),
        scratch_shapes=scratch,
        input_output_aliases=aliases or {},
        compiler_params=pltpu.CompilerParams(vmem_limit_bytes=VMEM_LIMIT),
        cost_estimate=pl.CostEstimate(flops=0, bytes_accessed=0, transcendentals=0),
    )(*placed)


def on_factors(value, v_refs, columns, ranks):
    pieces = [dot(value, ref[:, columns], ROWS_TIMES_ROWS) for ref in v_refs]
    missing = ranks - sum(ref.shape[0] for ref in v_refs)
    if missing:
        pieces.append(jnp.zeros((value.shape[0], missing), jnp.float32))
    return jnp.concatenate(pieces, axis=1)


def fetch_kernel(spans, factors, source_ref, v_ref, *refs):
    v_outs, w_outs, sems = refs[:factors], refs[factors:-1], refs[-1]
    copies, level = [], 0
    for out in v_outs:
        copies.append((v_ref.at[pl.ds(level, out.shape[0])], out))
        level += out.shape[0]
    for out, (start, stop) in zip(w_outs, spans):
        copies.append((source_ref.at[:, pl.ds(start, stop - start)], out))
    copies = [pltpu.make_async_copy(a, b, sems.at[i]) for i, (a, b) in enumerate(copies)]
    for copy in copies:
        copy.start()
    for copy in copies:
        copy.wait()


def fetch(spans, shares, source, v):
    _, rank, width = v.shape
    outs = [pltpu.VMEM((n, rank, width), v.dtype) for n in shares]
    outs += [pltpu.VMEM((source.shape[0], stop - start), source.dtype) for start, stop in spans]
    found = call(
        functools.partial(fetch_kernel, spans, len(shares)),
        outs,
        [source, v],
        scratch=[pltpu.SemaphoreType.DMA((len(outs),))],
        from_hbm=(0, 1),
    )
    return [f.reshape(-1, width) for f in found[: len(shares)]], list(found[len(shares) :])


def project_kernel(spans, factors, *refs):
    v_refs, parts, p_ref = refs[:factors], refs[factors:-1], refs[-1]
    total = None
    for ref, (start, stop) in zip(parts, spans):
        term = on_factors(ref[...], v_refs, slice(start, stop), p_ref.shape[1])
        total = term if total is None else total + term
    p_ref[...] = total


def project(spans, w, far_v, ranks):
    outs = [pltpu.VMEM((w[0].shape[0], ranks), jnp.float32)]
    return call(functools.partial(project_kernel, spans, len(far_v)), outs, [*far_v, *w])[0]


def leaves_of(span, size):
    return range(span[0] // size, span[1] // size)


def first_kernel(spans, cross, *refs):
    n = len(spans)
    w_refs, (leaf_ref, u_ref, v_ref) = refs[:n], refs[n : n + 3]
    leaf_out, u_out, near_out = refs[n + 3 : n + 6]
    sum_refs, p_refs, (near_rows, sems) = refs[n + 6 : 2 * n + 6], refs[2 * n + 6 : 3 * n + 6], refs[3 * n + 6 :]
    nleaf, size, _ = leaf_out.shape
    near_copy = pltpu.make_async_copy(v_ref.at[pl.ds(cross, near_rows.shape[0])], near_rows, sems.at[0])
    u_copy = pltpu.make_async_copy(u_ref, u_out, sems.at[1])
    leaf_copies = [
        pltpu.make_async_copy(leaf_ref.at[c], leaf_out.at[c], sems.at[2 + c]) for c in range(nleaf)
    ]
    for copy in [near_copy, *leaf_copies, u_copy]:
        copy.start()
    near_copy.wait()
    near = near_rows[...].reshape(-1, near_rows.shape[2])
    for i, span in enumerate(spans):
        for j, c in enumerate(leaves_of(span, size)):
            columns = slice(j * size, (j + 1) * size)
            turned = near[:, c * size : (c + 1) * size].T
            near_out[c * size : (c + 1) * size, :] = turned
            p_refs[i][j] = dot(w_refs[i][:, columns], turned)
    for i, span in enumerate(spans):
        for j, c in enumerate(leaves_of(span, size)):
            leaf_copies[c].wait()
            columns = slice(j * size, (j + 1) * size)
            sum_refs[i][:, columns] = dot(w_refs[i][:, columns], leaf_out[c])
    u_copy.wait()


def first_part(spans, cross, w, leaf, u, v):
    levels, rank, width = v.shape
    nleaf, size, _ = leaf.shape
    rows = w[0].shape[0]
    near = (levels - cross) * rank
    outs = [
        pltpu.VMEM(leaf.shape, leaf.dtype),
        pltpu.VMEM(u.shape, u.dtype),
        pltpu.VMEM((width, near), v.dtype),
    ]
    outs += [pltpu.VMEM(x.shape, jnp.float32) for x in w]
    outs += [pltpu.VMEM((x.shape[1] // size, rows, near), jnp.float32) for x in w]
    n = len(w)
    found = call(
        functools.partial(first_kernel, spans, cross),
        outs,
        [*w, leaf, u, v],
        scratch=[
            pltpu.VMEM((levels - cross, rank, width), v.dtype),
            pltpu.SemaphoreType.DMA((2 + nleaf,)),
        ],
        from_hbm=(n, n + 1, n + 2),
    )
    leaf, u, near_v = found[:3]
    u = u.reshape(levels * rank, width)
    return leaf, u, near_v, list(found[3 : 3 + n]), list(found[3 + n :])


def nearby_kernel(front_ref, v_ref, *refs):
    p_ref = refs[-1]
    term = dot(front_ref[...], v_ref[...], ROWS_TIMES_ROWS)
    before = p_ref.shape[1] - term.shape[1]
    if before:
        term = jnp.concatenate([jnp.zeros((term.shape[0], before), jnp.float32), term], axis=1)
    p_ref[...] = term


def nearby_part(front, v, ranks, behind):
    outs = [pltpu.VMEM((front.shape[0], ranks), jnp.float32)]
    return call(nearby_kernel, outs, [front, v, *behind])[0]


def near_kernel(span, start, w_ref, front_ref, leaf_ref, v_ref, *refs):
    w_out, sum_out, p_out = refs[-3:]
    size = leaf_ref.shape[1]
    for j, c in enumerate(leaves_of(span, size)):
        columns = slice(j * size, (j + 1) * size)
        w = w_ref[:, columns] + front_ref[:, start + j * size : start + (j + 1) * size]
        w_out[:, columns] = w
        p_out[j] = dot(w, v_ref[c * size : (c + 1) * size, :])
        sum_out[:, columns] = dot(w, leaf_ref[c])


def near_part(span, start, w, front, leaf, near_v, behind):
    outs = [
        pltpu.VMEM(w.shape, w.dtype),
        pltpu.VMEM(w.shape, jnp.float32),
        pltpu.VMEM((w.shape[1] // leaf.shape[1], w.shape[0], near_v.shape[1]), jnp.float32),
    ]
    return call(functools.partial(near_kernel, span, start), outs, [w, front, leaf, near_v, *behind], {0: 0})


def far_kernel(rank, size, spans, chosen, levels_of, *refs):
    refs = list(refs)
    sum_refs = [refs.pop(0) for _ in chosen]
    p_refs = [refs.pop(0) for _ in spans]
    q_ref = refs.pop(0)
    part_refs = [refs.pop(0) for _ in levels_of]
    u_ref = refs.pop(0)
    out_ref, q_out = refs[:2]
    rows, far = q_ref.shape
    near = u_ref.shape[0] - far

    q = q_ref[...]
    lane = lax.broadcasted_iota(jnp.int32, (rows, far), 1) // rank
    for ref, level in zip(part_refs, levels_of):
        q = q + jnp.where(lane == level, ref[...], 0.0)
    q_out[...] = q

    projected = [ref[j] for ref in p_refs for j in range(ref.shape[0])]
    nleaf = len(projected)
    lane = lax.broadcasted_iota(jnp.int32, (rows, near), 1) // rank
    sums = []
    for level in range(near // rank):
        block = nleaf >> (level + 1)
        sums.append(
            [
                functools.reduce(jnp.add, projected[b * block : (b + 1) * block])
                for b in range(nleaf // block)
            ]
        )
    place = 0
    for i, ref in zip(chosen, sum_refs):
        for j, c in enumerate(leaves_of(spans[i], size)):
            swapped = sums[0][(c // (nleaf >> 1)) ^ 1]
            for level in range(1, near // rank):
                swapped = jnp.where(lane == level, sums[level][(c // (nleaf >> (level + 1))) ^ 1], swapped)
            columns = slice(c * size, (c + 1) * size)
            value = ref[:, j * size : (j + 1) * size]
            value = value + dot(q.astype(jnp.bfloat16), u_ref[:far, columns])
            value = value + dot(swapped.astype(jnp.bfloat16), u_ref[far:, columns])
            out_ref[:, place : place + size] = value.astype(jnp.bfloat16)
            place += size


def far_part(rank, size, spans, chosen, sums, projected, q, parts, levels_of, u, last):
    args = [*[sums[i] for i in chosen], *projected, q, *parts, u]
    width = sum(sums[i].shape[1] for i in chosen)
    space = jax.ShapeDtypeStruct if last else pltpu.VMEM
    outs = [space((q.shape[0], width), jnp.bfloat16), pltpu.VMEM(q.shape, jnp.float32)]
    kernel = functools.partial(far_kernel, rank, size, spans, chosen, tuple(levels_of) if parts else ())
    return call(kernel, outs, args, {len(chosen) + len(projected): 1})


def local(sources, leaves, v_rows, u_rows):
    devices = lax.axis_size("hodlr")
    chain = lax.axis_size("slab")
    cross = devices.bit_length() - 1
    source, right = sources[0], v_rows[0]
    levels, rank, width = right.shape
    nleaf, size = leaves.shape[1:3]
    cut = max(nleaf * FIRST_SHARE // 4, 1) * size
    spans = ((0, cut), (cut, width))
    offsets = list(range(1, devices))
    levels_of = [cross - x.bit_length() for x in offsets]

    def moved(x, moves, offset=0):
        route = [(a * devices + h, b * devices + (h ^ offset)) for a, b in moves for h in range(devices)]
        return lax.ppermute(x, ("slab", "hodlr"), route)

    def exchanged(p, moves):
        return [moved(p, moves, x) for x in offsets]

    shares = [n for n in (cross - 1, 1) if n]
    far_v, w = fetch(spans, shares, source, right)
    shifted = [
        moved(v, [(k, k - 1) for k in range(IN_PLACE + 1 if v is far_v[-1] else 1, chain)]) for v in far_v
    ]
    ranks = cross * rank
    whole = ((0, width),)
    p = project(spans, w, far_v, ranks)
    parts = exchanged(p, [(k, k) for k in range(chain)])
    leaf, u, near_v, sums, projected = first_part(spans, cross, w, leaves[0], u_rows[0], right)

    q = jnp.zeros(p.shape, jnp.float32)
    every = tuple(range(len(spans)))
    far = functools.partial(far_part, rank, size, spans)
    out, q = far(every, sums, projected, q, parts, levels_of, u, False)
    front = [moved(out, [(0, 1)])]
    ahead = [project(whole, [out], shifted[:-1], ranks)] if cross > 1 else []
    parts = [moved(ahead[0], [(0, 1)], x) for x in offsets[1:]]
    for k in range(1, chain):
        if k <= IN_PLACE:
            behind = parts + (shifted[-1:] if k == IN_PLACE else [])
            nearby = nearby_part(front[0], far_v[-1], ranks, behind)
            parts = [moved(nearby, [(k, k)], offsets[0])] + parts
        for i, span in enumerate(spans):
            behind = projected[i - 1 : i] if i else []
            given, start = (front[0], span[0]) if len(front) == 1 else (front[i], 0)
            w[i], sums[i], projected[i] = near_part(span, start, w[i], given, leaf, near_v, behind)
        if k == chain - 1:
            out, _ = far(every, sums, projected, q, parts, levels_of, u, True)
            return out[None]
        split = k >= chain - 1 - SPLIT_HOPS
        outs, front = [], []
        for chosen in [(i,) for i in every] if split else [every]:
            out, q = far(chosen, sums, projected, q, [] if front else parts, levels_of, u, False)
            outs.append(out)
            front.append(moved(out, [(k, k + 1)]))
        following = shifted[:-1] if k < IN_PLACE else shifted
        p = project(spans if split else whole, outs, following, ranks)
        parts = [moved(p, [(k, k + 1)], x) for x in offsets[1 if k < IN_PLACE else 0 :]]


def solution(mesh):
    in_specs = (
        P("slab", None, "hodlr"),
        P("slab", "hodlr", None, None),
        P("slab", None, None, "hodlr"),
        P("slab", None, None, "hodlr"),
    )
    out_specs = P("slab", None, "hodlr")
    return jax.shard_map(local, mesh=mesh, in_specs=in_specs, out_specs=out_specs, check_vma=False)
```

```python
import functools

import jax
import jax.numpy as jnp
from jax import lax
from jax.experimental import pallas as pl
from jax.experimental.pallas import tpu as pltpu
from jax.sharding import PartitionSpec as P

VMEM_LIMIT = 24 * 1024 * 1024
FIRST_SHARE = 2
SPLIT_HOPS = 3
IN_PLACE = 2
OPEN_FLOPS = 4 * 10**9
ROWS_TIMES_COLUMNS = (((1,), (0,)), ((), ()))
ROWS_TIMES_ROWS = (((1,), (1,)), ((), ()))


def dot(a, b, dims=ROWS_TIMES_COLUMNS):
    return lax.dot_general(a, b, dims, preferred_element_type=jnp.float32)


def call(kernel, outs, args, aliases=None, scratch=(), from_hbm=(), flops=0):
    whole = pl.BlockSpec(memory_space=pltpu.VMEM)
    remote = pl.BlockSpec(memory_space=pl.ANY)
    placed = [
        pltpu.with_memory_space_constraint(a, pltpu.HBM if i in from_hbm else pltpu.VMEM)
        for i, a in enumerate(args)
    ]
    return pl.pallas_call(
        kernel,
        out_shape=outs,
        in_specs=[remote if i in from_hbm else whole for i in range(len(args))],
        out_specs=[whole] * len(outs),
        scratch_shapes=scratch,
        input_output_aliases=aliases or {},
        compiler_params=pltpu.CompilerParams(vmem_limit_bytes=VMEM_LIMIT),
        cost_estimate=pl.CostEstimate(flops=flops, bytes_accessed=0, transcendentals=0),
    )(*placed)


def on_factors(value, v_refs, columns, ranks):
    pieces = [dot(value, ref[:, columns], ROWS_TIMES_ROWS) for ref in v_refs]
    missing = ranks - sum(ref.shape[0] for ref in v_refs)
    if missing:
        pieces.append(jnp.zeros((value.shape[0], missing), jnp.float32))
    return jnp.concatenate(pieces, axis=1)


def fetch_kernel(spans, factors, source_ref, v_ref, *refs):
    v_outs, w_outs, sems = refs[:factors], refs[factors:-1], refs[-1]
    copies, level = [], 0
    for out in v_outs:
        copies.append((v_ref.at[pl.ds(level, out.shape[0])], out))
        level += out.shape[0]
    for out, (start, stop) in zip(w_outs, spans):
        copies.append((source_ref.at[:, pl.ds(start, stop - start)], out))
    copies = [pltpu.make_async_copy(a, b, sems.at[i]) for i, (a, b) in enumerate(copies)]
    for copy in copies:
        copy.start()
    for copy in copies:
        copy.wait()


def fetch(spans, shares, source, v):
    _, rank, width = v.shape
    outs = [pltpu.VMEM((n, rank, width), v.dtype) for n in shares]
    outs += [pltpu.VMEM((source.shape[0], stop - start), source.dtype) for start, stop in spans]
    found = call(
        functools.partial(fetch_kernel, spans, len(shares)),
        outs,
        [source, v],
        scratch=[pltpu.SemaphoreType.DMA((len(outs),))],
        from_hbm=(0, 1),
    )
    return [f.reshape(-1, width) for f in found[: len(shares)]], list(found[len(shares) :])


def project_kernel(spans, factors, *refs):
    v_refs, parts, p_ref = refs[:factors], refs[factors:-1], refs[-1]
    total = None
    for ref, (start, stop) in zip(parts, spans):
        term = on_factors(ref[...], v_refs, slice(start, stop), p_ref.shape[1])
        total = term if total is None else total + term
    p_ref[...] = total


def project(spans, w, far_v, ranks, flops=0):
    outs = [pltpu.VMEM((w[0].shape[0], ranks), jnp.float32)]
    return call(functools.partial(project_kernel, spans, len(far_v)), outs, [*far_v, *w], flops=flops)[0]


def leaves_of(span, size):
    return range(span[0] // size, span[1] // size)


def first_kernel(spans, cross, *refs):
    n = len(spans)
    w_refs, (leaf_ref, v_ref), near_out = refs[:n], refs[n : n + 2], refs[n + 2]
    sum_refs, p_refs = refs[n + 3 : 2 * n + 3], refs[2 * n + 3 :]
    size = leaf_ref.shape[1]
    near = near_out.shape[1]
    for i, span in enumerate(spans):
        for j, c in enumerate(leaves_of(span, size)):
            columns = slice(j * size, (j + 1) * size)
            turned = v_ref[cross:, :, c * size : (c + 1) * size].reshape(near, size).T
            near_out[c * size : (c + 1) * size, :] = turned
            p_refs[i][j] = dot(w_refs[i][:, columns], turned)
            sum_refs[i][:, columns] = dot(w_refs[i][:, columns], leaf_ref[c])


def first_part(spans, cross, w, leaf, v):
    levels, rank, width = v.shape
    size = leaf.shape[1]
    rows = w[0].shape[0]
    near = (levels - cross) * rank
    outs = [pltpu.VMEM((width, near), v.dtype)]
    outs += [pltpu.VMEM(x.shape, jnp.float32) for x in w]
    outs += [pltpu.VMEM((x.shape[1] // size, rows, near), jnp.float32) for x in w]
    n = len(w)
    found = call(functools.partial(first_kernel, spans, cross), outs, [*w, leaf, v])
    return found[0], list(found[1 : 1 + n]), list(found[1 + n :])


def nearby_kernel(front_ref, v_ref, *refs):
    p_ref = refs[-1]
    term = dot(front_ref[...], v_ref[...], ROWS_TIMES_ROWS)
    before = p_ref.shape[1] - term.shape[1]
    if before:
        term = jnp.concatenate([jnp.zeros((term.shape[0], before), jnp.float32), term], axis=1)
    p_ref[...] = term


def nearby_part(front, v, ranks, behind):
    outs = [pltpu.VMEM((front.shape[0], ranks), jnp.float32)]
    return call(nearby_kernel, outs, [front, v, *behind])[0]


def near_kernel(span, start, w_ref, front_ref, leaf_ref, v_ref, *refs):
    w_out, sum_out, p_out = refs[-3:]
    size = leaf_ref.shape[1]
    for j, c in enumerate(leaves_of(span, size)):
        columns = slice(j * size, (j + 1) * size)
        w = w_ref[:, columns] + front_ref[:, start + j * size : start + (j + 1) * size]
        w_out[:, columns] = w
        p_out[j] = dot(w, v_ref[c * size : (c + 1) * size, :])
        sum_out[:, columns] = dot(w, leaf_ref[c])


def near_part(span, start, w, front, leaf, near_v, behind):
    outs = [
        pltpu.VMEM(w.shape, w.dtype),
        pltpu.VMEM(w.shape, jnp.float32),
        pltpu.VMEM((w.shape[1] // leaf.shape[1], w.shape[0], near_v.shape[1]), jnp.float32),
    ]
    return call(functools.partial(near_kernel, span, start), outs, [w, front, leaf, near_v, *behind], {0: 0})


def far_kernel(rank, size, spans, chosen, levels_of, *refs):
    refs = list(refs)
    sum_refs = [refs.pop(0) for _ in chosen]
    p_refs = [refs.pop(0) for _ in spans]
    q_ref = refs.pop(0)
    part_refs = [refs.pop(0) for _ in levels_of]
    u_ref = refs.pop(0)
    out_ref, q_out = refs[:2]
    rows, far = q_ref.shape
    near = u_ref.shape[0] - far

    q = q_ref[...]
    lane = lax.broadcasted_iota(jnp.int32, (rows, far), 1) // rank
    for ref, level in zip(part_refs, levels_of):
        q = q + jnp.where(lane == level, ref[...], 0.0)
    q_out[...] = q

    projected = [ref[j] for ref in p_refs for j in range(ref.shape[0])]
    nleaf = len(projected)
    lane = lax.broadcasted_iota(jnp.int32, (rows, near), 1) // rank
    sums = []
    for level in range(near // rank):
        block = nleaf >> (level + 1)
        sums.append(
            [
                functools.reduce(jnp.add, projected[b * block : (b + 1) * block])
                for b in range(nleaf // block)
            ]
        )
    place = 0
    for i, ref in zip(chosen, sum_refs):
        for j, c in enumerate(leaves_of(spans[i], size)):
            swapped = sums[0][(c // (nleaf >> 1)) ^ 1]
            for level in range(1, near // rank):
                swapped = jnp.where(lane == level, sums[level][(c // (nleaf >> (level + 1))) ^ 1], swapped)
            columns = slice(c * size, (c + 1) * size)
            value = ref[:, j * size : (j + 1) * size]
            value = value + dot(q.astype(jnp.bfloat16), u_ref[:far, columns])
            value = value + dot(swapped.astype(jnp.bfloat16), u_ref[far:, columns])
            out_ref[:, place : place + size] = value.astype(jnp.bfloat16)
            place += size


def far_part(rank, size, spans, chosen, sums, projected, q, parts, levels_of, u, last):
    args = [*[sums[i] for i in chosen], *projected, q, *parts, u]
    width = sum(sums[i].shape[1] for i in chosen)
    space = jax.ShapeDtypeStruct if last else pltpu.VMEM
    outs = [space((q.shape[0], width), jnp.bfloat16), pltpu.VMEM(q.shape, jnp.float32)]
    kernel = functools.partial(far_kernel, rank, size, spans, chosen, tuple(levels_of) if parts else ())
    return call(kernel, outs, args, {len(chosen) + len(projected): 1})


def local(sources, leaves, v_rows, u_rows):
    devices = lax.axis_size("hodlr")
    chain = lax.axis_size("slab")
    cross = devices.bit_length() - 1
    source, right = sources[0], v_rows[0]
    levels, rank, width = right.shape
    nleaf, size = leaves.shape[1:3]
    cut = max(nleaf * FIRST_SHARE // 4, 1) * size
    spans = ((0, cut), (cut, width))
    offsets = list(range(1, devices))
    levels_of = [cross - x.bit_length() for x in offsets]

    def moved(x, moves, offset=0):
        route = [(a * devices + h, b * devices + (h ^ offset)) for a, b in moves for h in range(devices)]
        return lax.ppermute(x, ("slab", "hodlr"), route)

    def exchanged(p, moves):
        return [moved(p, moves, x) for x in offsets]

    shares = [n for n in (cross - 1, 1) if n]
    far_v, w = fetch(spans, shares, source, right)
    shifted = [
        moved(v, [(k, k - 1) for k in range(IN_PLACE + 1 if v is far_v[-1] else 1, chain)]) for v in far_v
    ]
    ranks = cross * rank
    whole = ((0, width),)
    p = project(spans, w, far_v, ranks, OPEN_FLOPS)
    parts = exchanged(p, [(k, k) for k in range(chain)])
    leaf, u = leaves[0], u_rows[0].reshape(levels * rank, width)
    near_v, sums, projected = first_part(spans, cross, w, leaf, right)

    q = jnp.zeros(p.shape, jnp.float32)
    every = tuple(range(len(spans)))
    far = functools.partial(far_part, rank, size, spans)
    out, q = far(every, sums, projected, q, parts, levels_of, u, False)
    front = [moved(out, [(0, 1)])]
    ahead = [project(whole, [out], shifted[:-1], ranks)] if cross > 1 else []
    parts = [moved(ahead[0], [(0, 1)], x) for x in offsets[1:]]
    for k in range(1, chain):
        first = []
        if k <= IN_PLACE:
            first = parts
            nearby = nearby_part(front[0], far_v[-1], ranks, ahead if k == 1 else shifted[-1:])
            parts = [moved(nearby, [(k, k)], offsets[0])] + parts
        for i, span in enumerate(spans):
            behind = projected[i - 1 : i] if i else first
            given, start = (front[0], span[0]) if len(front) == 1 else (front[i], 0)
            w[i], sums[i], projected[i] = near_part(span, start, w[i], given, leaf, near_v, behind)
        if k == chain - 1:
            out, _ = far(every, sums, projected, q, parts, levels_of, u, True)
            return out[None]
        split = k >= chain - 1 - SPLIT_HOPS
        outs, front = [], []
        for chosen in [(i,) for i in every] if split else [every]:
            out, q = far(chosen, sums, projected, q, [] if front else parts, levels_of, u, False)
            outs.append(out)
            front.append(moved(out, [(k, k + 1)]))
        following = shifted[:-1] if k < IN_PLACE else shifted
        p = project(spans if split else whole, outs, following, ranks)
        parts = [moved(p, [(k, k + 1)], x) for x in offsets[1 if k < IN_PLACE else 0 :]]


def solution(mesh):
    in_specs = (
        P("slab", None, "hodlr"),
        P("slab", "hodlr", None, None),
        P("slab", None, None, "hodlr"),
        P("slab", None, None, "hodlr"),
    )
    out_specs = P("slab", None, "hodlr")
    return jax.shard_map(local, mesh=mesh, in_specs=in_specs, out_specs=out_specs, check_vma=False)
```

```python
import functools

import jax
import jax.numpy as jnp
from jax import lax
from jax.experimental import pallas as pl
from jax.experimental.pallas import tpu as pltpu
from jax.sharding import PartitionSpec as P

VMEM_LIMIT = 24 * 1024 * 1024
FIRST_SHARE = 2
IN_PLACE = 2
OPEN_FLOPS = 4 * 10**9
ROWS_TIMES_COLUMNS = (((1,), (0,)), ((), ()))
ROWS_TIMES_ROWS = (((1,), (1,)), ((), ()))


def dot(a, b, dims=ROWS_TIMES_COLUMNS):
    return lax.dot_general(a, b, dims, preferred_element_type=jnp.float32)


def call(kernel, outs, args, aliases=None, scratch=(), from_hbm=(), flops=0):
    whole = pl.BlockSpec(memory_space=pltpu.VMEM)
    remote = pl.BlockSpec(memory_space=pl.ANY)
    placed = [
        pltpu.with_memory_space_constraint(a, pltpu.HBM if i in from_hbm else pltpu.VMEM)
        for i, a in enumerate(args)
    ]
    return pl.pallas_call(
        kernel,
        out_shape=outs,
        in_specs=[remote if i in from_hbm else whole for i in range(len(args))],
        out_specs=[whole] * len(outs),
        scratch_shapes=scratch,
        input_output_aliases=aliases or {},
        compiler_params=pltpu.CompilerParams(vmem_limit_bytes=VMEM_LIMIT),
        cost_estimate=pl.CostEstimate(flops=flops, bytes_accessed=0, transcendentals=0),
    )(*placed)


def on_factors(value, v_refs, columns, ranks):
    pieces = [dot(value, ref[:, columns], ROWS_TIMES_ROWS) for ref in v_refs]
    missing = ranks - sum(ref.shape[0] for ref in v_refs)
    if missing:
        pieces.append(jnp.zeros((value.shape[0], missing), jnp.float32))
    return jnp.concatenate(pieces, axis=1)


def fetch_kernel(spans, source_ref, v_ref, *refs):
    v_outs, w_outs, sems = refs[: -1 - len(spans)], refs[-1 - len(spans) : -1], refs[-1]
    copies, level = [], 0
    for out in v_outs[:-1]:
        copies.append((v_ref.at[pl.ds(level, out.shape[0])], out))
        level += out.shape[0]
    first = jnp.where(lax.axis_index("slab") == 1, 0, 1)
    copies.append((v_ref.at[pl.ds(first, v_outs[-1].shape[0])], v_outs[-1]))
    for out, (start, stop) in zip(w_outs, spans):
        copies.append((source_ref.at[:, pl.ds(start, stop - start)], out))
    copies = [pltpu.make_async_copy(a, b, sems.at[i]) for i, (a, b) in enumerate(copies)]
    for copy in copies:
        copy.start()
    for copy in copies:
        copy.wait()


def fetch(spans, cross, source, v):
    _, rank, width = v.shape
    shares = (cross - 1, 1, cross - 1)
    outs = [pltpu.VMEM((n, rank, width), v.dtype) for n in shares]
    outs += [pltpu.VMEM((source.shape[0], stop - start), source.dtype) for start, stop in spans]
    found = call(
        functools.partial(fetch_kernel, spans),
        outs,
        [source, v],
        scratch=[pltpu.SemaphoreType.DMA((len(outs),))],
        from_hbm=(0, 1),
    )
    return [f.reshape(-1, width) for f in found[: len(shares)]], list(found[len(shares) :])


def behind_kernel(x_ref, other_ref, out_ref):
    pass


def put_behind(x, other):
    return call(behind_kernel, [pltpu.VMEM(x.shape, x.dtype)], [x, other], {0: 0})[0]


def project_kernel(spans, factors, *refs):
    v_refs, parts, p_ref = refs[:factors], refs[factors:-1], refs[-1]
    total = None
    for ref, (start, stop) in zip(parts, spans):
        term = on_factors(ref[...], v_refs, slice(start, stop), p_ref.shape[1])
        total = term if total is None else total + term
    p_ref[...] = total


def project(spans, w, far_v, ranks, flops=0):
    outs = [pltpu.VMEM((w[0].shape[0], ranks), jnp.float32)]
    return call(functools.partial(project_kernel, spans, len(far_v)), outs, [*far_v, *w], flops=flops)[0]


def leaves_of(span, size):
    return range(span[0] // size, span[1] // size)


def first_kernel(spans, cross, *refs):
    n = len(spans)
    w_refs, (leaf_ref, v_ref), near_out = refs[:n], refs[n : n + 2], refs[n + 2]
    sum_refs, p_refs = refs[n + 3 : 2 * n + 3], refs[2 * n + 3 :]
    size = leaf_ref.shape[1]
    near = near_out.shape[1]
    for i, span in enumerate(spans):
        for j, c in enumerate(leaves_of(span, size)):
            columns = slice(j * size, (j + 1) * size)
            turned = v_ref[cross:, :, c * size : (c + 1) * size].reshape(near, size).T
            near_out[c * size : (c + 1) * size, :] = turned
            p_refs[i][j] = dot(w_refs[i][:, columns], turned)
            sum_refs[i][:, columns] = dot(w_refs[i][:, columns], leaf_ref[c])


def first_part(spans, cross, w, leaf, v):
    levels, rank, width = v.shape
    size = leaf.shape[1]
    rows = w[0].shape[0]
    near = (levels - cross) * rank
    outs = [pltpu.VMEM((width, near), v.dtype)]
    outs += [pltpu.VMEM(x.shape, jnp.float32) for x in w]
    outs += [pltpu.VMEM((x.shape[1] // size, rows, near), jnp.float32) for x in w]
    n = len(w)
    found = call(functools.partial(first_kernel, spans, cross), outs, [*w, leaf, v])
    return found[0], list(found[1 : 1 + n]), list(found[1 + n :])


def nearby_kernel(front_ref, v_ref, *refs):
    p_ref = refs[-1]
    term = dot(front_ref[...], v_ref[...], ROWS_TIMES_ROWS)
    before = p_ref.shape[1] - term.shape[1]
    if before:
        term = jnp.concatenate([jnp.zeros((term.shape[0], before), jnp.float32), term], axis=1)
    p_ref[...] = term


def nearby_part(front, v, ranks, behind):
    outs = [pltpu.VMEM((front.shape[0], ranks), jnp.float32)]
    return call(nearby_kernel, outs, [front, v, *behind])[0]


def near_kernel(span, start, w_ref, front_ref, leaf_ref, v_ref, *refs):
    w_out, sum_out, p_out = refs[-3:]
    size = leaf_ref.shape[1]
    for j, c in enumerate(leaves_of(span, size)):
        columns = slice(j * size, (j + 1) * size)
        w = w_ref[:, columns] + front_ref[:, start + j * size : start + (j + 1) * size]
        w_out[:, columns] = w
        p_out[j] = dot(w, v_ref[c * size : (c + 1) * size, :])
        sum_out[:, columns] = dot(w, leaf_ref[c])


def near_part(span, start, w, front, leaf, near_v, behind):
    outs = [
        pltpu.VMEM(w.shape, w.dtype),
        pltpu.VMEM(w.shape, jnp.float32),
        pltpu.VMEM((w.shape[1] // leaf.shape[1], w.shape[0], near_v.shape[1]), jnp.float32),
    ]
    return call(functools.partial(near_kernel, span, start), outs, [w, front, leaf, near_v, *behind], {0: 0})


def far_kernel(rank, size, spans, chosen, levels_of, *refs):
    refs = list(refs)
    sum_refs = [refs.pop(0) for _ in chosen]
    p_refs = [refs.pop(0) for _ in spans]
    q_ref = refs.pop(0)
    part_refs = [refs.pop(0) for _ in levels_of]
    u_ref = refs.pop(0)
    out_ref, q_out = refs[:2]
    rows, far = q_ref.shape
    near = u_ref.shape[0] - far

    q = q_ref[...]
    lane = lax.broadcasted_iota(jnp.int32, (rows, far), 1) // rank
    for ref, level in zip(part_refs, levels_of):
        q = q + jnp.where(lane == level, ref[...], 0.0)
    q_out[...] = q

    projected = [ref[j] for ref in p_refs for j in range(ref.shape[0])]
    nleaf = len(projected)
    lane = lax.broadcasted_iota(jnp.int32, (rows, near), 1) // rank
    sums = []
    for level in range(near // rank):
        block = nleaf >> (level + 1)
        sums.append(
            [
                functools.reduce(jnp.add, projected[b * block : (b + 1) * block])
                for b in range(nleaf // block)
            ]
        )
    place = 0
    for i, ref in zip(chosen, sum_refs):
        for j, c in enumerate(leaves_of(spans[i], size)):
            swapped = sums[0][(c // (nleaf >> 1)) ^ 1]
            for level in range(1, near // rank):
                swapped = jnp.where(lane == level, sums[level][(c // (nleaf >> (level + 1))) ^ 1], swapped)
            columns = slice(c * size, (c + 1) * size)
            value = ref[:, j * size : (j + 1) * size]
            value = value + dot(q.astype(jnp.bfloat16), u_ref[:far, columns])
            value = value + dot(swapped.astype(jnp.bfloat16), u_ref[far:, columns])
            out_ref[:, place : place + size] = value.astype(jnp.bfloat16)
            place += size


def far_part(rank, size, spans, chosen, sums, projected, q, parts, levels_of, u, last):
    args = [*[sums[i] for i in chosen], *projected, q, *parts, u]
    width = sum(sums[i].shape[1] for i in chosen)
    space = jax.ShapeDtypeStruct if last else pltpu.VMEM
    outs = [space((q.shape[0], width), jnp.bfloat16), pltpu.VMEM(q.shape, jnp.float32)]
    kernel = functools.partial(far_kernel, rank, size, spans, chosen, tuple(levels_of) if parts else ())
    return call(kernel, outs, args, {len(chosen) + len(projected): 1})


def local(sources, leaves, v_rows, u_rows):
    devices = lax.axis_size("hodlr")
    chain = lax.axis_size("slab")
    cross = devices.bit_length() - 1
    source, right = sources[0], v_rows[0]
    levels, rank, width = right.shape
    nleaf, size = leaves.shape[1:3]
    cut = max(nleaf * FIRST_SHARE // 4, 1) * size
    spans = ((0, cut), (cut, width))
    offsets = list(range(1, devices))
    levels_of = [cross - x.bit_length() for x in offsets]

    def moved(x, moves, offset=0):
        route = [(a * devices + h, b * devices + (h ^ offset)) for a, b in moves for h in range(devices)]
        return lax.ppermute(x, ("slab", "hodlr"), route)

    def exchanged(p, moves):
        return [moved(p, moves, x) for x in offsets]

    (coarse_v, fine_v, ahead_v), w = fetch(spans, cross, source, right)
    later = [(k, k - 1) for k in range(IN_PLACE + 1, chain)]
    early = moved(ahead_v, [(1, 0)] + later)
    ranks = cross * rank
    whole = ((0, width),)
    p = project(spans, w, [coarse_v, fine_v], ranks, OPEN_FLOPS)
    parts = exchanged(p, [(k, k) for k in range(chain)])
    leaf, u = leaves[0], u_rows[0].reshape(levels * rank, width)
    near_v, sums, projected = first_part(spans, cross, w, leaf, right)

    q = jnp.zeros(p.shape, jnp.float32)
    every = tuple(range(len(spans)))
    far = functools.partial(far_part, rank, size, spans)
    out, q = far(every, sums, projected, q, parts, levels_of, u, False)
    front = [moved(out, [(0, 1)])]
    ahead = project(whole, [out], [early], ranks)
    parts = [moved(ahead, [(0, 1)], x) for x in offsets[1:]]
    coarse = moved(put_behind(coarse_v, early), [(2, 1)] + later)
    fine = early[-rank:]
    for k in range(1, chain):
        first = []
        if k <= IN_PLACE:
            first = parts
            nearby = nearby_part(front[0], fine_v, ranks, [ahead if k == 1 else early])
            parts = [moved(nearby, [(k, k)], offsets[0])] + parts
        for i, span in enumerate(spans):
            behind = projected[i - 1 : i] if i else first
            given, start = (front[0], span[0]) if len(front) == 1 else (front[i], 0)
            w[i], sums[i], projected[i] = near_part(span, start, w[i], given, leaf, near_v, behind)
        if k == chain - 1:
            out, _ = far(every, sums, projected, q, parts, levels_of, u, True)
            return out[None]
        split = k >= IN_PLACE and k % 2 == 0
        outs, front = [], []
        for chosen in [(i,) for i in every] if split else [every]:
            out, q = far(chosen, sums, projected, q, [] if front else parts, levels_of, u, False)
            outs.append(out)
            front.append(moved(out, [(k, k + 1)]))
        following = [coarse] if k < IN_PLACE else [coarse, fine]
        p = project(spans if split else whole, outs, following, ranks)
        parts = [moved(p, [(k, k + 1)], x) for x in offsets[1 if k < IN_PLACE else 0 :]]


def solution(mesh):
    in_specs = (
        P("slab", None, "hodlr"),
        P("slab", "hodlr", None, None),
        P("slab", None, None, "hodlr"),
        P("slab", None, None, "hodlr"),
    )
    out_specs = P("slab", None, "hodlr")
    return jax.shard_map(local, mesh=mesh, in_specs=in_specs, out_specs=out_specs, check_vma=False)
```

```python
import functools

import jax
import jax.numpy as jnp
from jax import lax
from jax.experimental import pallas as pl
from jax.experimental.pallas import tpu as pltpu
from jax.sharding import PartitionSpec as P

VMEM_LIMIT = 24 * 1024 * 1024
FIRST_SHARE = 2
IN_PLACE = 2
OPEN_FLOPS = 4 * 10**9
ROWS_TIMES_COLUMNS = (((1,), (0,)), ((), ()))
ROWS_TIMES_ROWS = (((1,), (1,)), ((), ()))


def dot(a, b, dims=ROWS_TIMES_COLUMNS):
    return lax.dot_general(a, b, dims, preferred_element_type=jnp.float32)


def call(kernel, outs, args, aliases=None, scratch=(), from_hbm=(), flops=0):
    whole = pl.BlockSpec(memory_space=pltpu.VMEM)
    remote = pl.BlockSpec(memory_space=pl.ANY)
    placed = [
        pltpu.with_memory_space_constraint(a, pltpu.HBM if i in from_hbm else pltpu.VMEM)
        for i, a in enumerate(args)
    ]
    return pl.pallas_call(
        kernel,
        out_shape=outs,
        in_specs=[remote if i in from_hbm else whole for i in range(len(args))],
        out_specs=[whole] * len(outs),
        scratch_shapes=scratch,
        input_output_aliases=aliases or {},
        compiler_params=pltpu.CompilerParams(vmem_limit_bytes=VMEM_LIMIT),
        cost_estimate=pl.CostEstimate(flops=flops, bytes_accessed=0, transcendentals=0),
    )(*placed)


def on_factors(value, v_refs, columns, ranks):
    pieces = [dot(value, ref[:, columns], ROWS_TIMES_ROWS) for ref in v_refs]
    missing = ranks - sum(ref.shape[0] for ref in v_refs)
    if missing:
        pieces.append(jnp.zeros((value.shape[0], missing), jnp.float32))
    return jnp.concatenate(pieces, axis=1)


def fetch_kernel(spans, factors, source_ref, v_ref, *refs):
    v_outs, w_outs, sems = refs[:factors], refs[factors:-1], refs[-1]
    copies, level = [], 0
    for out in v_outs:
        copies.append((v_ref.at[pl.ds(level, out.shape[0])], out))
        level += out.shape[0]
    for out, (start, stop) in zip(w_outs, spans):
        copies.append((source_ref.at[:, pl.ds(start, stop - start)], out))
    copies = [pltpu.make_async_copy(a, b, sems.at[i]) for i, (a, b) in enumerate(copies)]
    for copy in copies:
        copy.start()
    for copy in copies:
        copy.wait()


def fetch(spans, shares, source, v):
    _, rank, width = v.shape
    outs = [pltpu.VMEM((n, rank, width), v.dtype) for n in shares]
    outs += [pltpu.VMEM((source.shape[0], stop - start), source.dtype) for start, stop in spans]
    found = call(
        functools.partial(fetch_kernel, spans, len(shares)),
        outs,
        [source, v],
        scratch=[pltpu.SemaphoreType.DMA((len(outs),))],
        from_hbm=(0, 1),
    )
    return [f.reshape(-1, width) for f in found[: len(shares)]], list(found[len(shares) :])


def project_kernel(spans, factors, *refs):
    v_refs, parts, p_ref = refs[:factors], refs[factors:-1], refs[-1]
    total = None
    for ref, (start, stop) in zip(parts, spans):
        term = on_factors(ref[...], v_refs, slice(start, stop), p_ref.shape[1])
        total = term if total is None else total + term
    p_ref[...] = total


def project(spans, w, far_v, ranks, flops=0):
    outs = [pltpu.VMEM((w[0].shape[0], ranks), jnp.float32)]
    return call(functools.partial(project_kernel, spans, len(far_v)), outs, [*far_v, *w], flops=flops)[0]


def leaves_of(span, size):
    return range(span[0] // size, span[1] // size)


def first_kernel(spans, cross, *refs):
    n = len(spans)
    w_refs, (leaf_ref, v_ref), near_out = refs[:n], refs[n : n + 2], refs[n + 2]
    sum_refs, p_refs = refs[n + 3 : 2 * n + 3], refs[2 * n + 3 :]
    size = leaf_ref.shape[1]
    near = p_refs[0].shape[2]
    for i, span in enumerate(spans):
        for j, c in enumerate(leaves_of(span, size)):
            columns = slice(j * size, (j + 1) * size)
            turned = v_ref[cross:, :, c * size : (c + 1) * size].reshape(near, size).T
            group = near_out.shape[2] // near
            near_out[c // group, :, c % group * near : (c % group + 1) * near] = turned
            p_refs[i][j] = dot(w_refs[i][:, columns], turned)
            sum_refs[i][:, columns] = dot(w_refs[i][:, columns], leaf_ref[c])


def first_part(spans, cross, w, leaf, v):
    levels, rank, width = v.shape
    size = leaf.shape[1]
    rows = w[0].shape[0]
    near = (levels - cross) * rank
    group = 2 if all((stop - start) // size % 2 == 0 for start, stop in spans) else 1
    outs = [pltpu.VMEM((width // size // group, size, group * near), v.dtype)]
    outs += [pltpu.VMEM(x.shape, jnp.float32) for x in w]
    outs += [pltpu.VMEM((x.shape[1] // size, rows, near), jnp.float32) for x in w]
    n = len(w)
    found = call(functools.partial(first_kernel, spans, cross), outs, [*w, leaf, v])
    return found[0], list(found[1 : 1 + n]), list(found[1 + n :])


def nearby_kernel(front_ref, v_ref, *refs):
    p_ref = refs[-1]
    term = dot(front_ref[...], v_ref[...], ROWS_TIMES_ROWS)
    before = p_ref.shape[1] - term.shape[1]
    if before:
        term = jnp.concatenate([jnp.zeros((term.shape[0], before), jnp.float32), term], axis=1)
    p_ref[...] = term


def nearby_part(front, v, ranks, behind):
    outs = [pltpu.VMEM((front.shape[0], ranks), jnp.float32)]
    return call(nearby_kernel, outs, [front, v, *behind])[0]


def near_kernel(span, start, w_ref, front_ref, leaf_ref, v_ref, *refs):
    w_out, sum_out, p_out = refs[-3:]
    size = leaf_ref.shape[1]
    rows = w_ref.shape[0]
    near = p_out.shape[2]
    group = v_ref.shape[2] // near
    members = []
    for j, c in enumerate(leaves_of(span, size)):
        columns = slice(j * size, (j + 1) * size)
        w = w_ref[:, columns] + front_ref[:, start + j * size : start + (j + 1) * size]
        w_out[:, columns] = w
        members.append(w)
        if len(members) == group:
            both = dot(jnp.concatenate(members, axis=0), v_ref[c // group])
            for i in range(group):
                p_out[j - group + 1 + i] = both[i * rows : (i + 1) * rows, i * near : (i + 1) * near]
            members = []
        sum_out[:, columns] = dot(w, leaf_ref[c])


def near_part(span, start, near, w, front, leaf, near_v, behind):
    outs = [
        pltpu.VMEM(w.shape, w.dtype),
        pltpu.VMEM(w.shape, jnp.float32),
        pltpu.VMEM((w.shape[1] // leaf.shape[1], w.shape[0], near), jnp.float32),
    ]
    return call(functools.partial(near_kernel, span, start), outs, [w, front, leaf, near_v, *behind], {0: 0})


def far_kernel(rank, size, spans, chosen, levels_of, *refs):
    refs = list(refs)
    sum_refs = [refs.pop(0) for _ in chosen]
    p_refs = [refs.pop(0) for _ in spans]
    q_ref = refs.pop(0)
    part_refs = [refs.pop(0) for _ in levels_of]
    u_ref = refs.pop(0)
    out_ref, q_out = refs[:2]
    rows, far = q_ref.shape
    near = u_ref.shape[0] - far

    q = q_ref[...]
    lane = lax.broadcasted_iota(jnp.int32, (rows, far), 1) // rank
    for ref, level in zip(part_refs, levels_of):
        q = q + jnp.where(lane == level, ref[...], 0.0)
    q_out[...] = q

    projected = [ref[j] for ref in p_refs for j in range(ref.shape[0])]
    nleaf = len(projected)
    lane = lax.broadcasted_iota(jnp.int32, (rows, near), 1) // rank
    sums = []
    for level in range(near // rank):
        block = nleaf >> (level + 1)
        sums.append(
            [
                functools.reduce(jnp.add, projected[b * block : (b + 1) * block])
                for b in range(nleaf // block)
            ]
        )
    place = 0
    for i, ref in zip(chosen, sum_refs):
        for j, c in enumerate(leaves_of(spans[i], size)):
            swapped = sums[0][(c // (nleaf >> 1)) ^ 1]
            for level in range(1, near // rank):
                swapped = jnp.where(lane == level, sums[level][(c // (nleaf >> (level + 1))) ^ 1], swapped)
            columns = slice(c * size, (c + 1) * size)
            value = ref[:, j * size : (j + 1) * size]
            value = value + dot(q.astype(jnp.bfloat16), u_ref[:far, columns])
            value = value + dot(swapped.astype(jnp.bfloat16), u_ref[far:, columns])
            out_ref[:, place : place + size] = value.astype(jnp.bfloat16)
            place += size


def far_part(rank, size, spans, chosen, sums, projected, q, parts, levels_of, u, last):
    args = [*[sums[i] for i in chosen], *projected, q, *parts, u]
    width = sum(sums[i].shape[1] for i in chosen)
    space = jax.ShapeDtypeStruct if last else pltpu.VMEM
    outs = [space((q.shape[0], width), jnp.bfloat16), pltpu.VMEM(q.shape, jnp.float32)]
    kernel = functools.partial(far_kernel, rank, size, spans, chosen, tuple(levels_of) if parts else ())
    return call(kernel, outs, args, {len(chosen) + len(projected): 1})


def local(sources, leaves, v_rows, u_rows):
    devices = lax.axis_size("hodlr")
    chain = lax.axis_size("slab")
    cross = devices.bit_length() - 1
    source, right = sources[0], v_rows[0]
    levels, rank, width = right.shape
    nleaf, size = leaves.shape[1:3]
    cut = max(nleaf * FIRST_SHARE // 4, 1) * size
    spans = ((0, cut), (cut, width))
    offsets = list(range(1, devices))
    levels_of = [cross - x.bit_length() for x in offsets]

    def moved(x, moves, offset=0):
        route = [(a * devices + h, b * devices + (h ^ offset)) for a, b in moves for h in range(devices)]
        return lax.ppermute(x, ("slab", "hodlr"), route)

    def exchanged(p, moves):
        return [moved(p, moves, x) for x in offsets]

    shares = [n for n in (cross - 1, 1) if n]
    far_v, w = fetch(spans, shares, source, right)
    shifted = [
        moved(v, [(k, k - 1) for k in range(IN_PLACE + 1 if v is far_v[-1] else 1, chain)]) for v in far_v
    ]
    ranks = cross * rank
    whole = ((0, width),)
    p = project(spans, w, far_v, ranks, OPEN_FLOPS)
    parts = exchanged(p, [(k, k) for k in range(chain)])
    leaf, u = leaves[0], u_rows[0].reshape(levels * rank, width)
    near_v, sums, projected = first_part(spans, cross, w, leaf, right)

    q = jnp.zeros(p.shape, jnp.float32)
    every = tuple(range(len(spans)))
    far = functools.partial(far_part, rank, size, spans)
    out, q = far(every, sums, projected, q, parts, levels_of, u, False)
    front = [moved(out, [(0, 1)])]
    ahead = [project(whole, [out], shifted[:-1], ranks)] if cross > 1 else []
    parts = [moved(ahead[0], [(0, 1)], x) for x in offsets[1:]]
    for k in range(1, chain):
        first = []
        if k <= IN_PLACE:
            first = parts
            nearby = nearby_part(front[0], far_v[-1], ranks, ahead if k == 1 else shifted[-1:])
            parts = [moved(nearby, [(k, k)], offsets[0])] + parts
        for i, span in enumerate(spans):
            behind = projected[i - 1 : i] if i else first
            given, start = (front[0], span[0]) if len(front) == 1 else (front[i], 0)
            w[i], sums[i], projected[i] = near_part(span, start, (levels - cross) * rank, w[i], given, leaf, near_v, behind)
        if k == chain - 1:
            out, _ = far(every, sums, projected, q, parts, levels_of, u, True)
            return out[None]
        split = k >= IN_PLACE and k % 2 == 0
        outs, front = [], []
        for chosen in [(i,) for i in every] if split else [every]:
            out, q = far(chosen, sums, projected, q, [] if front else parts, levels_of, u, False)
            outs.append(out)
            front.append(moved(out, [(k, k + 1)]))
        following = shifted[:-1] if k < IN_PLACE else shifted
        p = project(spans if split else whole, outs, following, ranks)
        parts = [moved(p, [(k, k + 1)], x) for x in offsets[1 if k < IN_PLACE else 0 :]]


def solution(mesh):
    in_specs = (
        P("slab", None, "hodlr"),
        P("slab", "hodlr", None, None),
        P("slab", None, None, "hodlr"),
        P("slab", None, None, "hodlr"),
    )
    out_specs = P("slab", None, "hodlr")
    return jax.shard_map(local, mesh=mesh, in_specs=in_specs, out_specs=out_specs, check_vma=False)
```

```python
import functools

import jax
import jax.numpy as jnp
from jax import lax
from jax.experimental import pallas as pl
from jax.experimental.pallas import tpu as pltpu
from jax.sharding import PartitionSpec as P

VMEM_LIMIT = 24 * 1024 * 1024
FIRST_SHARE = 2
IN_PLACE = 2
OPEN_FLOPS = 4 * 10**9
ROWS_TIMES_COLUMNS = (((1,), (0,)), ((), ()))
ROWS_TIMES_ROWS = (((1,), (1,)), ((), ()))


def dot(a, b, dims=ROWS_TIMES_COLUMNS):
    return lax.dot_general(a, b, dims, preferred_element_type=jnp.float32)


def call(kernel, outs, args, aliases=None, scratch=(), from_hbm=(), flops=0):
    whole = pl.BlockSpec(memory_space=pltpu.VMEM)
    remote = pl.BlockSpec(memory_space=pl.ANY)
    placed = [
        pltpu.with_memory_space_constraint(a, pltpu.HBM if i in from_hbm else pltpu.VMEM)
        for i, a in enumerate(args)
    ]
    return pl.pallas_call(
        kernel,
        out_shape=outs,
        in_specs=[remote if i in from_hbm else whole for i in range(len(args))],
        out_specs=[whole] * len(outs),
        scratch_shapes=scratch,
        input_output_aliases=aliases or {},
        compiler_params=pltpu.CompilerParams(vmem_limit_bytes=VMEM_LIMIT),
        cost_estimate=pl.CostEstimate(flops=flops, bytes_accessed=0, transcendentals=0),
    )(*placed)


def on_factors(value, v_refs, columns, ranks):
    pieces = [dot(value, ref[:, columns], ROWS_TIMES_ROWS) for ref in v_refs]
    missing = ranks - sum(ref.shape[0] for ref in v_refs)
    if missing:
        pieces.append(jnp.zeros((value.shape[0], missing), jnp.float32))
    return jnp.concatenate(pieces, axis=1)


def fetch_kernel(spans, factors, source_ref, v_ref, *refs):
    v_outs, w_outs, sems = refs[:factors], refs[factors:-1], refs[-1]
    copies, level = [], 0
    for out in v_outs:
        copies.append((v_ref.at[pl.ds(level, out.shape[0])], out))
        level += out.shape[0]
    for out, (start, stop) in zip(w_outs, spans):
        copies.append((source_ref.at[:, pl.ds(start, stop - start)], out))
    copies = [pltpu.make_async_copy(a, b, sems.at[i]) for i, (a, b) in enumerate(copies)]
    for copy in copies:
        copy.start()
    for copy in copies:
        copy.wait()


def fetch(spans, shares, source, v):
    _, rank, width = v.shape
    outs = [pltpu.VMEM((n, rank, width), v.dtype) for n in shares]
    outs += [pltpu.VMEM((source.shape[0], stop - start), source.dtype) for start, stop in spans]
    found = call(
        functools.partial(fetch_kernel, spans, len(shares)),
        outs,
        [source, v],
        scratch=[pltpu.SemaphoreType.DMA((len(outs),))],
        from_hbm=(0, 1),
    )
    return [f.reshape(-1, width) for f in found[: len(shares)]], list(found[len(shares) :])


def project_kernel(spans, factors, *refs):
    v_refs, parts, p_ref = refs[:factors], refs[factors:-1], refs[-1]
    total = None
    for ref, (start, stop) in zip(parts, spans):
        term = on_factors(ref[...], v_refs, slice(start, stop), p_ref.shape[1])
        total = term if total is None else total + term
    p_ref[...] = total.astype(p_ref.dtype)


def project(spans, w, far_v, ranks, flops=0):
    outs = [pltpu.VMEM((w[0].shape[0], ranks), jnp.bfloat16)]
    return call(functools.partial(project_kernel, spans, len(far_v)), outs, [*far_v, *w], flops=flops)[0]


def turn_kernel(size, *refs):
    v_refs, out_ref = refs[:-1], refs[-1]
    for c in range(out_ref.shape[0] // size):
        rows = slice(c * size, (c + 1) * size)
        out_ref[rows, :] = jnp.concatenate([ref[:, rows] for ref in v_refs], axis=0).T


def turn(size, v):
    outs = [pltpu.VMEM((v[0].shape[1], sum(x.shape[0] for x in v)), v[0].dtype)]
    return call(functools.partial(turn_kernel, size), outs, v)[0]


def project_turned_kernel(spans, v_ref, *refs):
    parts, p_ref = refs[:-1], refs[-1]
    total = None
    for ref, (start, stop) in zip(parts, spans):
        term = dot(ref[...], v_ref[start:stop, :])
        total = term if total is None else total + term
    p_ref[...] = total.astype(p_ref.dtype)


def project_turned(spans, w, v):
    outs = [pltpu.VMEM((w[0].shape[0], v.shape[1]), jnp.bfloat16)]
    return call(functools.partial(project_turned_kernel, spans), outs, [v, *w])[0]


def leaves_of(span, size):
    return range(span[0] // size, span[1] // size)


def first_kernel(spans, cross, *refs):
    n = len(spans)
    w_refs, (leaf_ref, v_ref), near_out = refs[:n], refs[n : n + 2], refs[n + 2]
    sum_refs, p_refs = refs[n + 3 : 2 * n + 3], refs[2 * n + 3 :]
    size = leaf_ref.shape[1]
    near = p_refs[0].shape[2]
    for i, span in enumerate(spans):
        for j, c in enumerate(leaves_of(span, size)):
            columns = slice(j * size, (j + 1) * size)
            turned = v_ref[cross:, :, c * size : (c + 1) * size].reshape(near, size).T
            group = near_out.shape[2] // near
            near_out[c // group, :, c % group * near : (c % group + 1) * near] = turned
            p_refs[i][j] = dot(w_refs[i][:, columns], turned)
            sum_refs[i][:, columns] = dot(w_refs[i][:, columns], leaf_ref[c])


def first_part(spans, cross, w, leaf, v):
    levels, rank, width = v.shape
    size = leaf.shape[1]
    rows = w[0].shape[0]
    near = (levels - cross) * rank
    group = 2 if all((stop - start) // size % 2 == 0 for start, stop in spans) else 1
    outs = [pltpu.VMEM((width // size // group, size, group * near), v.dtype)]
    outs += [pltpu.VMEM(x.shape, jnp.float32) for x in w]
    outs += [pltpu.VMEM((x.shape[1] // size, rows, near), jnp.float32) for x in w]
    n = len(w)
    found = call(functools.partial(first_kernel, spans, cross), outs, [*w, leaf, v])
    return found[0], list(found[1 : 1 + n]), list(found[1 + n :])


def nearby_kernel(front_ref, v_ref, *refs):
    p_ref = refs[-1]
    term = dot(front_ref[...], v_ref[...], ROWS_TIMES_ROWS)
    before = p_ref.shape[1] - term.shape[1]
    if before:
        term = jnp.concatenate([jnp.zeros((term.shape[0], before), jnp.float32), term], axis=1)
    p_ref[...] = term.astype(p_ref.dtype)


def nearby_part(front, v, ranks, behind):
    outs = [pltpu.VMEM((front.shape[0], ranks), jnp.bfloat16)]
    return call(nearby_kernel, outs, [front, v, *behind])[0]


def near_kernel(span, start, w_ref, front_ref, leaf_ref, v_ref, *refs):
    w_out, sum_out, p_out = refs[-3:]
    size = leaf_ref.shape[1]
    rows = w_ref.shape[0]
    near = p_out.shape[2]
    group = v_ref.shape[2] // near
    members = []
    for j, c in enumerate(leaves_of(span, size)):
        columns = slice(j * size, (j + 1) * size)
        w = w_ref[:, columns] + front_ref[:, start + j * size : start + (j + 1) * size]
        w_out[:, columns] = w
        members.append(w)
        if len(members) == group:
            both = dot(jnp.concatenate(members, axis=0), v_ref[c // group])
            for i in range(group):
                p_out[j - group + 1 + i] = both[i * rows : (i + 1) * rows, i * near : (i + 1) * near]
            members = []
        sum_out[:, columns] = dot(w, leaf_ref[c])


def near_part(span, start, near, w, front, leaf, near_v, behind):
    outs = [
        pltpu.VMEM(w.shape, w.dtype),
        pltpu.VMEM(w.shape, jnp.float32),
        pltpu.VMEM((w.shape[1] // leaf.shape[1], w.shape[0], near), jnp.float32),
    ]
    return call(functools.partial(near_kernel, span, start), outs, [w, front, leaf, near_v, *behind], {0: 0})


def far_kernel(rank, size, spans, chosen, levels_of, *refs):
    refs = list(refs)
    sum_refs = [refs.pop(0) for _ in chosen]
    p_refs = [refs.pop(0) for _ in spans]
    q_ref = refs.pop(0)
    part_refs = [refs.pop(0) for _ in levels_of]
    u_ref = refs.pop(0)
    out_ref, q_out = refs[:2]
    rows, far = q_ref.shape
    near = u_ref.shape[0] - far

    q = q_ref[...]
    lane = lax.broadcasted_iota(jnp.int32, (rows, far), 1) // rank
    for ref, level in zip(part_refs, levels_of):
        q = q + jnp.where(lane == level, ref[...].astype(jnp.float32), 0.0)
    q_out[...] = q

    projected = [ref[j] for ref in p_refs for j in range(ref.shape[0])]
    nleaf = len(projected)
    lane = lax.broadcasted_iota(jnp.int32, (rows, near), 1) // rank
    sums = []
    for level in range(near // rank):
        block = nleaf >> (level + 1)
        sums.append(
            [
                functools.reduce(jnp.add, projected[b * block : (b + 1) * block])
                for b in range(nleaf // block)
            ]
        )
    place = 0
    for i, ref in zip(chosen, sum_refs):
        for j, c in enumerate(leaves_of(spans[i], size)):
            swapped = sums[0][(c // (nleaf >> 1)) ^ 1]
            for level in range(1, near // rank):
                swapped = jnp.where(lane == level, sums[level][(c // (nleaf >> (level + 1))) ^ 1], swapped)
            columns = slice(c * size, (c + 1) * size)
            value = ref[:, j * size : (j + 1) * size]
            value = value + dot(q.astype(jnp.bfloat16), u_ref[:far, columns])
            value = value + dot(swapped.astype(jnp.bfloat16), u_ref[far:, columns])
            out_ref[:, place : place + size] = value.astype(jnp.bfloat16)
            place += size


def far_part(rank, size, spans, chosen, sums, projected, q, parts, levels_of, u, last):
    args = [*[sums[i] for i in chosen], *projected, q, *parts, u]
    width = sum(sums[i].shape[1] for i in chosen)
    space = jax.ShapeDtypeStruct if last else pltpu.VMEM
    outs = [space((q.shape[0], width), jnp.bfloat16), pltpu.VMEM(q.shape, jnp.float32)]
    kernel = functools.partial(far_kernel, rank, size, spans, chosen, tuple(levels_of) if parts else ())
    return call(kernel, outs, args, {len(chosen) + len(projected): 1})


def local(sources, leaves, v_rows, u_rows):
    devices = lax.axis_size("hodlr")
    chain = lax.axis_size("slab")
    cross = devices.bit_length() - 1
    source, right = sources[0], v_rows[0]
    levels, rank, width = right.shape
    nleaf, size = leaves.shape[1:3]
    cut = max(nleaf * FIRST_SHARE // 4, 1) * size
    spans = ((0, cut), (cut, width))
    offsets = list(range(1, devices))
    levels_of = [cross - x.bit_length() for x in offsets]

    def moved(x, moves, offset=0):
        route = [(a * devices + h, b * devices + (h ^ offset)) for a, b in moves for h in range(devices)]
        return lax.ppermute(x, ("slab", "hodlr"), route)

    def exchanged(p, moves):
        return [moved(p, moves, x) for x in offsets]

    shares = [n for n in (cross - 1, 1) if n]
    far_v, w = fetch(spans, shares, source, right)
    shifted = [
        moved(v, [(k, k - 1) for k in range(IN_PLACE + 1 if v is far_v[-1] else 1, chain)]) for v in far_v
    ]
    ranks = cross * rank
    whole = ((0, width),)
    p = project(spans, w, far_v, ranks, OPEN_FLOPS)
    parts = exchanged(p, [(k, k) for k in range(chain)])
    leaf, u = leaves[0], u_rows[0].reshape(levels * rank, width)
    near_v, sums, projected = first_part(spans, cross, w, leaf, right)

    q = jnp.zeros(p.shape, jnp.float32)
    every = tuple(range(len(spans)))
    far = functools.partial(far_part, rank, size, spans)
    out, q = far(every, sums, projected, q, parts, levels_of, u, False)
    front = [moved(out, [(0, 1)])]
    ahead = [project(whole, [out], shifted[:-1], ranks)] if cross > 1 else []
    parts = [moved(ahead[0], [(0, 1)], x) for x in offsets[1:]]
    for k in range(1, chain):
        first = []
        if k <= IN_PLACE:
            first = parts
            if k == IN_PLACE:
                turned = turn(size, shifted)
            nearby = nearby_part(front[0], far_v[-1], ranks, ahead if k == 1 else [turned])
            parts = [moved(nearby, [(k, k)], offsets[0])] + parts
        for i, span in enumerate(spans):
            behind = projected[i - 1 : i] if i else first
            given, start = (front[0], span[0]) if len(front) == 1 else (front[i], 0)
            w[i], sums[i], projected[i] = near_part(span, start, (levels - cross) * rank, w[i], given, leaf, near_v, behind)
        if k == chain - 1:
            out, _ = far(every, sums, projected, q, parts, levels_of, u, True)
            return out[None]
        split = k >= IN_PLACE and k % 2 == 0
        outs, front = [], []
        for chosen in [(i,) for i in every] if split else [every]:
            out, q = far(chosen, sums, projected, q, [] if front else parts, levels_of, u, False)
            outs.append(out)
            front.append(moved(out, [(k, k + 1)]))
        if k < IN_PLACE:
            p = project(whole, outs, shifted[:-1], ranks)
        else:
            p = project_turned(spans if split else whole, outs, turned)
        parts = [moved(p, [(k, k + 1)], x) for x in offsets[1 if k < IN_PLACE else 0 :]]


def solution(mesh):
    in_specs = (
        P("slab", None, "hodlr"),
        P("slab", "hodlr", None, None),
        P("slab", None, None, "hodlr"),
        P("slab", None, None, "hodlr"),
    )
    out_specs = P("slab", None, "hodlr")
    return jax.shard_map(local, mesh=mesh, in_specs=in_specs, out_specs=out_specs, check_vma=False)
```

```python
import functools

import jax
import jax.numpy as jnp
from jax import lax
from jax.experimental import pallas as pl
from jax.experimental.pallas import tpu as pltpu
from jax.sharding import PartitionSpec as P

VMEM_LIMIT = 24 * 1024 * 1024
FIRST_SHARE = 2
IN_PLACE = 2
OPEN_FLOPS = 4 * 10**9
ROWS_TIMES_COLUMNS = (((1,), (0,)), ((), ()))
ROWS_TIMES_ROWS = (((1,), (1,)), ((), ()))


def dot(a, b, dims=ROWS_TIMES_COLUMNS):
    return lax.dot_general(a, b, dims, preferred_element_type=jnp.float32)


def call(kernel, outs, args, aliases=None, scratch=(), from_hbm=(), flops=0):
    whole = pl.BlockSpec(memory_space=pltpu.VMEM)
    remote = pl.BlockSpec(memory_space=pl.ANY)
    placed = [
        pltpu.with_memory_space_constraint(a, pltpu.HBM if i in from_hbm else pltpu.VMEM)
        for i, a in enumerate(args)
    ]
    return pl.pallas_call(
        kernel,
        out_shape=outs,
        in_specs=[remote if i in from_hbm else whole for i in range(len(args))],
        out_specs=[whole] * len(outs),
        scratch_shapes=scratch,
        input_output_aliases=aliases or {},
        compiler_params=pltpu.CompilerParams(vmem_limit_bytes=VMEM_LIMIT),
        cost_estimate=pl.CostEstimate(flops=flops, bytes_accessed=0, transcendentals=0),
    )(*placed)


def on_factors(value, v_refs, columns, ranks):
    pieces = [dot(value, ref[:, columns], ROWS_TIMES_ROWS) for ref in v_refs]
    missing = ranks - sum(ref.shape[0] for ref in v_refs)
    if missing:
        pieces.append(jnp.zeros((value.shape[0], missing), jnp.float32))
    return jnp.concatenate(pieces, axis=1)


def fetch_kernel(spans, factors, source_ref, v_ref, *refs):
    v_outs, w_outs, sems = refs[:factors], refs[factors:-1], refs[-1]
    copies, level = [], 0
    for out in v_outs:
        copies.append((v_ref.at[pl.ds(level, out.shape[0])], out))
        level += out.shape[0]
    for out, (start, stop) in zip(w_outs, spans):
        copies.append((source_ref.at[:, pl.ds(start, stop - start)], out))
    copies = [pltpu.make_async_copy(a, b, sems.at[i]) for i, (a, b) in enumerate(copies)]
    for copy in copies:
        copy.start()
    for copy in copies:
        copy.wait()


def fetch(spans, shares, source, v):
    _, rank, width = v.shape
    outs = [pltpu.VMEM((n, rank, width), v.dtype) for n in shares]
    outs += [pltpu.VMEM((source.shape[0], stop - start), source.dtype) for start, stop in spans]
    found = call(
        functools.partial(fetch_kernel, spans, len(shares)),
        outs,
        [source, v],
        scratch=[pltpu.SemaphoreType.DMA((len(outs),))],
        from_hbm=(0, 1),
    )
    return [f.reshape(-1, width) for f in found[: len(shares)]], list(found[len(shares) :])


def project_kernel(spans, factors, *refs):
    v_refs, parts, p_ref = refs[:factors], refs[factors:-1], refs[-1]
    total = None
    for ref, (start, stop) in zip(parts, spans):
        term = on_factors(ref[...], v_refs, slice(start, stop), p_ref.shape[1])
        total = term if total is None else total + term
    p_ref[...] = total.astype(p_ref.dtype)


def project(spans, w, far_v, ranks, flops=0):
    outs = [pltpu.VMEM((w[0].shape[0], ranks), jnp.bfloat16)]
    return call(functools.partial(project_kernel, spans, len(far_v)), outs, [*far_v, *w], flops=flops)[0]


def turn_kernel(size, *refs):
    v_refs, out_ref = refs[:-1], refs[-1]
    for c in range(out_ref.shape[0] // size):
        rows = slice(c * size, (c + 1) * size)
        out_ref[rows, :] = jnp.concatenate([ref[:, rows] for ref in v_refs], axis=0).T


def turn(size, v):
    outs = [pltpu.VMEM((v[0].shape[1], sum(x.shape[0] for x in v)), v[0].dtype)]
    return call(functools.partial(turn_kernel, size), outs, v)[0]


def project_turned_kernel(spans, v_ref, *refs):
    parts, p_ref = refs[:-1], refs[-1]
    total = None
    for ref, (start, stop) in zip(parts, spans):
        term = dot(ref[...], v_ref[start:stop, :])
        total = term if total is None else total + term
    p_ref[...] = total.astype(p_ref.dtype)


def project_turned(spans, w, v):
    outs = [pltpu.VMEM((w[0].shape[0], v.shape[1]), jnp.bfloat16)]
    return call(functools.partial(project_turned_kernel, spans), outs, [v, *w])[0]


def leaves_of(span, size):
    return range(span[0] // size, span[1] // size)


def first_kernel(spans, cross, *refs):
    n = len(spans)
    w_refs, (leaf_ref, v_ref), near_out = refs[:n], refs[n : n + 2], refs[n + 2]
    sum_refs, p_refs = refs[n + 3 : 2 * n + 3], refs[2 * n + 3 :]
    size = leaf_ref.shape[1]
    near = p_refs[0].shape[2]
    for i, span in enumerate(spans):
        for j, c in enumerate(leaves_of(span, size)):
            columns = slice(j * size, (j + 1) * size)
            turned = v_ref[cross:, :, c * size : (c + 1) * size].reshape(near, size).T
            group = near_out.shape[2] // near
            near_out[c // group, :, c % group * near : (c % group + 1) * near] = turned
            p_refs[i][j] = dot(w_refs[i][:, columns], turned)
            sum_refs[i][:, columns] = dot(w_refs[i][:, columns], leaf_ref[c])


def first_part(spans, cross, w, leaf, v):
    levels, rank, width = v.shape
    size = leaf.shape[1]
    rows = w[0].shape[0]
    near = (levels - cross) * rank
    group = 2 if all((stop - start) // size % 2 == 0 for start, stop in spans) else 1
    outs = [pltpu.VMEM((width // size // group, size, group * near), v.dtype)]
    outs += [pltpu.VMEM(x.shape, jnp.float32) for x in w]
    outs += [pltpu.VMEM((x.shape[1] // size, rows, near), jnp.float32) for x in w]
    n = len(w)
    found = call(functools.partial(first_kernel, spans, cross), outs, [*w, leaf, v])
    return found[0], list(found[1 : 1 + n]), list(found[1 + n :])


def nearby_kernel(rank, levels_of, front_ref, v_ref, *refs):
    part_refs, p_ref = refs[: len(levels_of)], refs[-1]
    term = dot(front_ref[...], v_ref[...], ROWS_TIMES_ROWS)
    rows, ranks = p_ref.shape
    before = ranks - term.shape[1]
    if before:
        term = jnp.concatenate([jnp.zeros((rows, before), jnp.float32), term], axis=1)
    lane = lax.broadcasted_iota(jnp.int32, (rows, ranks), 1) // rank
    for ref, level in zip(part_refs, levels_of):
        term = term + jnp.where(lane == level, ref[...].astype(jnp.float32), 0.0)
    p_ref[...] = term.astype(p_ref.dtype)


def nearby_part(rank, front, v, ranks, parts, levels_of, behind):
    outs = [pltpu.VMEM((front.shape[0], ranks), jnp.bfloat16)]
    return call(functools.partial(nearby_kernel, rank, tuple(levels_of)), outs, [front, v, *parts, *behind])[0]


def near_kernel(span, start, w_ref, front_ref, leaf_ref, v_ref, *refs):
    w_out, sum_out, p_out = refs[-3:]
    size = leaf_ref.shape[1]
    rows = w_ref.shape[0]
    near = p_out.shape[2]
    group = v_ref.shape[2] // near
    members = []
    for j, c in enumerate(leaves_of(span, size)):
        columns = slice(j * size, (j + 1) * size)
        w = w_ref[:, columns] + front_ref[:, start + j * size : start + (j + 1) * size]
        w_out[:, columns] = w
        members.append(w)
        if len(members) == group:
            both = dot(jnp.concatenate(members, axis=0), v_ref[c // group])
            for i in range(group):
                p_out[j - group + 1 + i] = both[i * rows : (i + 1) * rows, i * near : (i + 1) * near]
            members = []
        sum_out[:, columns] = dot(w, leaf_ref[c])


def near_part(span, start, near, w, front, leaf, near_v, behind):
    outs = [
        pltpu.VMEM(w.shape, w.dtype),
        pltpu.VMEM(w.shape, jnp.float32),
        pltpu.VMEM((w.shape[1] // leaf.shape[1], w.shape[0], near), jnp.float32),
    ]
    return call(functools.partial(near_kernel, span, start), outs, [w, front, leaf, near_v, *behind], {0: 0})


def far_kernel(rank, size, spans, chosen, levels_of, *refs):
    refs = list(refs)
    sum_refs = [refs.pop(0) for _ in chosen]
    p_refs = [refs.pop(0) for _ in spans]
    q_ref = refs.pop(0)
    part_refs = [refs.pop(0) for _ in levels_of]
    u_ref = refs.pop(0)
    out_ref, q_out = refs[:2]
    rows, far = q_ref.shape
    near = u_ref.shape[0] - far

    q = q_ref[...]
    lane = lax.broadcasted_iota(jnp.int32, (rows, far), 1) // rank
    for ref, level in zip(part_refs, levels_of):
        part = ref[...].astype(jnp.float32)
        q = q + (part if level is None else jnp.where(lane == level, part, 0.0))
    q_out[...] = q

    projected = [ref[j] for ref in p_refs for j in range(ref.shape[0])]
    nleaf = len(projected)
    lane = lax.broadcasted_iota(jnp.int32, (rows, near), 1) // rank
    sums = []
    for level in range(near // rank):
        block = nleaf >> (level + 1)
        sums.append(
            [
                functools.reduce(jnp.add, projected[b * block : (b + 1) * block])
                for b in range(nleaf // block)
            ]
        )
    place = 0
    for i, ref in zip(chosen, sum_refs):
        for j, c in enumerate(leaves_of(spans[i], size)):
            swapped = sums[0][(c // (nleaf >> 1)) ^ 1]
            for level in range(1, near // rank):
                swapped = jnp.where(lane == level, sums[level][(c // (nleaf >> (level + 1))) ^ 1], swapped)
            columns = slice(c * size, (c + 1) * size)
            value = ref[:, j * size : (j + 1) * size]
            value = value + dot(q.astype(jnp.bfloat16), u_ref[:far, columns])
            value = value + dot(swapped.astype(jnp.bfloat16), u_ref[far:, columns])
            out_ref[:, place : place + size] = value.astype(jnp.bfloat16)
            place += size


def far_part(rank, size, spans, chosen, sums, projected, q, parts, levels_of, u, last):
    args = [*[sums[i] for i in chosen], *projected, q, *parts, u]
    width = sum(sums[i].shape[1] for i in chosen)
    space = jax.ShapeDtypeStruct if last else pltpu.VMEM
    outs = [space((q.shape[0], width), jnp.bfloat16), pltpu.VMEM(q.shape, jnp.float32)]
    kernel = functools.partial(far_kernel, rank, size, spans, chosen, tuple(levels_of) if parts else ())
    return call(kernel, outs, args, {len(chosen) + len(projected): 1})


def local(sources, leaves, v_rows, u_rows):
    devices = lax.axis_size("hodlr")
    chain = lax.axis_size("slab")
    cross = devices.bit_length() - 1
    source, right = sources[0], v_rows[0]
    levels, rank, width = right.shape
    nleaf, size = leaves.shape[1:3]
    cut = max(nleaf * FIRST_SHARE // 4, 1) * size
    spans = ((0, cut), (cut, width))
    offsets = list(range(1, devices))
    levels_of = [cross - x.bit_length() for x in offsets]

    def moved(x, moves, offset=0):
        route = [(a * devices + h, b * devices + (h ^ offset)) for a, b in moves for h in range(devices)]
        return lax.ppermute(x, ("slab", "hodlr"), route)

    def exchanged(p, moves):
        return [moved(p, moves, x) for x in offsets]

    shares = [n for n in (cross - 1, 1) if n]
    far_v, w = fetch(spans, shares, source, right)
    shifted = [
        moved(v, [(k, k - 1) for k in range(IN_PLACE + 1 if v is far_v[-1] else 1, chain)]) for v in far_v
    ]
    ranks = cross * rank
    whole = ((0, width),)
    p = project(spans, w, far_v, ranks, OPEN_FLOPS)
    parts = exchanged(p, [(k, k) for k in range(chain)])
    leaf, u = leaves[0], u_rows[0].reshape(levels * rank, width)
    near_v, sums, projected = first_part(spans, cross, w, leaf, right)

    q = jnp.zeros(p.shape, jnp.float32)
    every = tuple(range(len(spans)))
    far = functools.partial(far_part, rank, size, spans)
    out, q = far(every, sums, projected, q, parts, levels_of, u, False)
    front = [moved(out, [(0, 1)])]
    ahead = [project(whole, [out], shifted[:-1], ranks)] if cross > 1 else []
    relayed = offsets[1::2]
    parts = [moved(ahead[0], [(0, 1)], x) for x in relayed]
    levels_relayed = [cross - x.bit_length() for x in relayed]
    for k in range(1, chain):
        levels_now = levels_of[::-1]
        if k <= IN_PLACE:
            if k == IN_PLACE:
                turned = turn(size, shifted)
            behind = ahead if k == 1 else [turned]
            nearby = nearby_part(rank, front[0], far_v[-1], ranks, parts, levels_relayed, behind)
            parts = [moved(nearby, [(k, k)], offsets[0])] + parts
            levels_now = [None] + levels_relayed
        for i, span in enumerate(spans):
            behind = projected[i - 1 : i] if i else []
            given, start = (front[0], span[0]) if len(front) == 1 else (front[i], 0)
            w[i], sums[i], projected[i] = near_part(span, start, (levels - cross) * rank, w[i], given, leaf, near_v, behind)
        if k == chain - 1:
            out, _ = far(every, sums, projected, q, parts, levels_now, u, True)
            return out[None]
        split = k >= IN_PLACE
        outs, front = [], []
        for chosen in [(i,) for i in every] if split else [every]:
            out, q = far(chosen, sums, projected, q, [] if front else parts, levels_now, u, False)
            outs.append(out)
            front.append(moved(out, [(k, k + 1)]))
        if k < IN_PLACE:
            p = project(whole, outs, shifted[:-1], ranks)
        else:
            p = project_turned(spans if split else whole, outs, turned)
        sent = relayed if k < IN_PLACE else offsets[::-1]
        parts = [moved(p, [(k, k + 1)], x) for x in sent]


def solution(mesh):
    in_specs = (
        P("slab", None, "hodlr"),
        P("slab", "hodlr", None, None),
        P("slab", None, None, "hodlr"),
        P("slab", None, None, "hodlr"),
    )
    out_specs = P("slab", None, "hodlr")
    return jax.shard_map(local, mesh=mesh, in_specs=in_specs, out_specs=out_specs, check_vma=False)
```

```python
import functools

import jax
import jax.numpy as jnp
from jax import lax
from jax.experimental import pallas as pl
from jax.experimental.pallas import tpu as pltpu
from jax.sharding import PartitionSpec as P

VMEM_LIMIT = 24 * 1024 * 1024
FIRST_SHARE = 3
IN_PLACE = 2
OPEN_FLOPS = 4 * 10**9
ROWS_TIMES_COLUMNS = (((1,), (0,)), ((), ()))
ROWS_TIMES_ROWS = (((1,), (1,)), ((), ()))


def dot(a, b, dims=ROWS_TIMES_COLUMNS):
    return lax.dot_general(a, b, dims, preferred_element_type=jnp.float32)


def call(kernel, outs, args, aliases=None, scratch=(), from_hbm=(), flops=0, to_hbm=()):
    whole = pl.BlockSpec(memory_space=pltpu.VMEM)
    remote = pl.BlockSpec(memory_space=pl.ANY)
    placed = [
        pltpu.with_memory_space_constraint(a, pltpu.HBM if i in from_hbm else pltpu.VMEM)
        for i, a in enumerate(args)
    ]
    return pl.pallas_call(
        kernel,
        out_shape=outs,
        in_specs=[remote if i in from_hbm else whole for i in range(len(args))],
        out_specs=[remote if i in to_hbm else whole for i in range(len(outs))],
        scratch_shapes=scratch,
        input_output_aliases=aliases or {},
        compiler_params=pltpu.CompilerParams(vmem_limit_bytes=VMEM_LIMIT),
        cost_estimate=pl.CostEstimate(flops=flops, bytes_accessed=0, transcendentals=0),
    )(*placed)


def on_factors(value, v_refs, columns, ranks):
    pieces = [dot(value, ref[:, columns], ROWS_TIMES_ROWS) for ref in v_refs]
    missing = ranks - sum(ref.shape[0] for ref in v_refs)
    if missing:
        pieces.append(jnp.zeros((value.shape[0], missing), jnp.float32))
    return jnp.concatenate(pieces, axis=1)


def fetch_kernel(spans, factors, source_ref, v_ref, *refs):
    v_outs, w_outs, sems = refs[:factors], refs[factors:-1], refs[-1]
    copies, level = [], 0
    for out in v_outs:
        copies.append((v_ref.at[pl.ds(level, out.shape[0])], out))
        level += out.shape[0]
    for out, (start, stop) in zip(w_outs, spans):
        copies.append((source_ref.at[:, pl.ds(start, stop - start)], out))
    copies = [pltpu.make_async_copy(a, b, sems.at[i]) for i, (a, b) in enumerate(copies)]
    for copy in copies:
        copy.start()
    for copy in copies:
        copy.wait()


def fetch(spans, shares, source, v):
    _, rank, width = v.shape
    outs = [pltpu.VMEM((n, rank, width), v.dtype) for n in shares]
    outs += [pltpu.VMEM((source.shape[0], stop - start), source.dtype) for start, stop in spans]
    found = call(
        functools.partial(fetch_kernel, spans, len(shares)),
        outs,
        [source, v],
        scratch=[pltpu.SemaphoreType.DMA((len(outs),))],
        from_hbm=(0, 1),
    )
    return [f.reshape(-1, width) for f in found[: len(shares)]], list(found[len(shares) :])


def project_kernel(spans, factors, *refs):
    v_refs, parts, p_ref = refs[:factors], refs[factors:-1], refs[-1]
    total = None
    for ref, (start, stop) in zip(parts, spans):
        term = on_factors(ref[...], v_refs, slice(start, stop), p_ref.shape[1])
        total = term if total is None else total + term
    p_ref[...] = total.astype(p_ref.dtype)


def project(spans, w, far_v, ranks, flops=0):
    outs = [pltpu.VMEM((w[0].shape[0], ranks), jnp.bfloat16)]
    return call(functools.partial(project_kernel, spans, len(far_v)), outs, [*far_v, *w], flops=flops)[0]


def turn_kernel(size, *refs):
    v_refs, out_ref = refs[:-1], refs[-1]
    for c in range(out_ref.shape[0] // size):
        rows = slice(c * size, (c + 1) * size)
        out_ref[rows, :] = jnp.concatenate([ref[:, rows] for ref in v_refs], axis=0).T


def turn(size, v):
    outs = [pltpu.VMEM((v[0].shape[1], sum(x.shape[0] for x in v)), v[0].dtype)]
    return call(functools.partial(turn_kernel, size), outs, v)[0]


def project_turned_kernel(spans, v_ref, *refs):
    parts, p_ref = refs[:-1], refs[-1]
    total = None
    for ref, (start, stop) in zip(parts, spans):
        term = dot(ref[...], v_ref[start:stop, :])
        total = term if total is None else total + term
    p_ref[...] = total.astype(p_ref.dtype)


def project_turned(spans, w, v):
    outs = [pltpu.VMEM((w[0].shape[0], v.shape[1]), jnp.bfloat16)]
    return call(functools.partial(project_turned_kernel, spans), outs, [v, *w])[0]


def leaves_of(span, size):
    return range(span[0] // size, span[1] // size)


def first_kernel(spans, cross, *refs):
    n = len(spans)
    w_refs, (leaf_ref, v_ref), near_out = refs[:n], refs[n : n + 2], refs[n + 2]
    sum_refs, p_refs = refs[n + 3 : 2 * n + 3], refs[2 * n + 3 :]
    size = leaf_ref.shape[1]
    near = p_refs[0].shape[2]
    for i, span in enumerate(spans):
        for j, c in enumerate(leaves_of(span, size)):
            columns = slice(j * size, (j + 1) * size)
            turned = v_ref[cross:, :, c * size : (c + 1) * size].reshape(near, size).T
            group = near_out.shape[2] // near
            near_out[c // group, :, c % group * near : (c % group + 1) * near] = turned
            p_refs[i][j] = dot(w_refs[i][:, columns], turned)
            sum_refs[i][:, columns] = dot(w_refs[i][:, columns], leaf_ref[c])


def first_part(spans, cross, w, leaf, v):
    levels, rank, width = v.shape
    size = leaf.shape[1]
    rows = w[0].shape[0]
    near = (levels - cross) * rank
    group = 2 if all((stop - start) // size % 2 == 0 for start, stop in spans) else 1
    outs = [pltpu.VMEM((width // size // group, size, group * near), v.dtype)]
    outs += [pltpu.VMEM(x.shape, jnp.float32) for x in w]
    outs += [pltpu.VMEM((x.shape[1] // size, rows, near), jnp.float32) for x in w]
    n = len(w)
    found = call(functools.partial(first_kernel, spans, cross), outs, [*w, leaf, v])
    return found[0], list(found[1 : 1 + n]), list(found[1 + n :])


def nearby_kernel(rank, levels_of, front_ref, v_ref, *refs):
    part_refs, p_ref = refs[: len(levels_of)], refs[-1]
    term = dot(front_ref[...], v_ref[...], ROWS_TIMES_ROWS)
    rows, ranks = p_ref.shape
    before = ranks - term.shape[1]
    if before:
        term = jnp.concatenate([jnp.zeros((rows, before), jnp.float32), term], axis=1)
    lane = lax.broadcasted_iota(jnp.int32, (rows, ranks), 1) // rank
    for ref, level in zip(part_refs, levels_of):
        term = term + jnp.where(lane == level, ref[...].astype(jnp.float32), 0.0)
    p_ref[...] = term.astype(p_ref.dtype)


def nearby_part(rank, front, v, ranks, parts, levels_of, behind):
    outs = [pltpu.VMEM((front.shape[0], ranks), jnp.bfloat16)]
    return call(functools.partial(nearby_kernel, rank, tuple(levels_of)), outs, [front, v, *parts, *behind])[0]


def near_kernel(span, start, w_ref, front_ref, leaf_ref, v_ref, *refs):
    w_out, sum_out, p_out = refs[-3:]
    size = leaf_ref.shape[1]
    rows = w_ref.shape[0]
    near = p_out.shape[2]
    group = v_ref.shape[2] // near
    members = []
    for j, c in enumerate(leaves_of(span, size)):
        columns = slice(j * size, (j + 1) * size)
        w = w_ref[:, columns] + front_ref[:, start + j * size : start + (j + 1) * size]
        w_out[:, columns] = w
        members.append(w)
        if len(members) == group:
            both = dot(jnp.concatenate(members, axis=0), v_ref[c // group])
            for i in range(group):
                p_out[j - group + 1 + i] = both[i * rows : (i + 1) * rows, i * near : (i + 1) * near]
            members = []
        sum_out[:, columns] = dot(w, leaf_ref[c])


def near_part(span, start, near, w, front, leaf, near_v, behind):
    outs = [
        pltpu.VMEM(w.shape, w.dtype),
        pltpu.VMEM(w.shape, jnp.float32),
        pltpu.VMEM((w.shape[1] // leaf.shape[1], w.shape[0], near), jnp.float32),
    ]
    return call(functools.partial(near_kernel, span, start), outs, [w, front, leaf, near_v, *behind], {0: 0})


def far_kernel(rank, size, spans, chosen, levels_of, *refs):
    refs = list(refs)
    sum_refs = [refs.pop(0) for _ in chosen]
    p_refs = [refs.pop(0) for _ in spans]
    q_ref = refs.pop(0)
    part_refs = [refs.pop(0) for _ in levels_of]
    u_ref = refs.pop(0)
    out_ref, q_out = refs[:2]
    held_ref, sems = refs[2:] if len(refs) > 2 else (out_ref, None)
    copies = []
    rows, far = q_ref.shape
    near = u_ref.shape[0] - far

    q = q_ref[...]
    lane = lax.broadcasted_iota(jnp.int32, (rows, far), 1) // rank
    for ref, level in zip(part_refs, levels_of):
        part = ref[...].astype(jnp.float32)
        q = q + (part if level is None else jnp.where(lane == level, part, 0.0))
    q_out[...] = q

    projected = [ref[j] for ref in p_refs for j in range(ref.shape[0])]
    nleaf = len(projected)
    lane = lax.broadcasted_iota(jnp.int32, (rows, near), 1) // rank
    sums = []
    for level in range(near // rank):
        block = nleaf >> (level + 1)
        sums.append(
            [
                functools.reduce(jnp.add, projected[b * block : (b + 1) * block])
                for b in range(nleaf // block)
            ]
        )
    place = 0
    for i, ref in zip(chosen, sum_refs):
        for j, c in enumerate(leaves_of(spans[i], size)):
            swapped = sums[0][(c // (nleaf >> 1)) ^ 1]
            for level in range(1, near // rank):
                swapped = jnp.where(lane == level, sums[level][(c // (nleaf >> (level + 1))) ^ 1], swapped)
            columns = slice(c * size, (c + 1) * size)
            value = ref[:, j * size : (j + 1) * size]
            value = value + dot(q.astype(jnp.bfloat16), u_ref[:far, columns])
            value = value + dot(swapped.astype(jnp.bfloat16), u_ref[far:, columns])
            held_ref[:, place : place + size] = value.astype(jnp.bfloat16)
            if sems is not None:
                there = pl.ds(place, size)
                copies.append(pltpu.make_async_copy(held_ref.at[:, there], out_ref.at[:, there], sems.at[c]))
                copies[-1].start()
            place += size
    for copy in copies:
        copy.wait()


def far_part(rank, size, spans, chosen, sums, projected, q, parts, levels_of, u, last):
    args = [*[sums[i] for i in chosen], *projected, q, *parts, u]
    width = sum(sums[i].shape[1] for i in chosen)
    space = jax.ShapeDtypeStruct if last else pltpu.VMEM
    outs = [space((q.shape[0], width), jnp.bfloat16), pltpu.VMEM(q.shape, jnp.float32)]
    kernel = functools.partial(far_kernel, rank, size, spans, chosen, tuple(levels_of) if parts else ())
    scratch = [pltpu.VMEM((q.shape[0], width), jnp.bfloat16), pltpu.SemaphoreType.DMA((width // size,))]
    return call(
        kernel,
        outs,
        args,
        {len(chosen) + len(projected): 1},
        scratch=scratch if last else (),
        to_hbm=(0,) if last else (),
    )


def local(sources, leaves, v_rows, u_rows):
    devices = lax.axis_size("hodlr")
    chain = lax.axis_size("slab")
    cross = devices.bit_length() - 1
    source, right = sources[0], v_rows[0]
    levels, rank, width = right.shape
    nleaf, size = leaves.shape[1:3]
    cut = max(nleaf * FIRST_SHARE // 4, 1) * size
    spans = ((0, cut), (cut, width))
    offsets = list(range(1, devices))
    levels_of = [cross - x.bit_length() for x in offsets]

    def moved(x, moves, offset=0):
        route = [(a * devices + h, b * devices + (h ^ offset)) for a, b in moves for h in range(devices)]
        return lax.ppermute(x, ("slab", "hodlr"), route)

    def exchanged(p, moves):
        return [moved(p, moves, x) for x in offsets]

    shares = [n for n in (cross - 1, 1) if n]
    far_v, w = fetch(spans, shares, source, right)
    shifted = [
        moved(v, [(k, k - 1) for k in range(IN_PLACE + 1 if v is far_v[-1] else 1, chain)]) for v in far_v
    ]
    ranks = cross * rank
    whole = ((0, width),)
    p = project(spans, w, far_v, ranks, OPEN_FLOPS)
    parts = exchanged(p, [(k, k) for k in range(chain)])
    leaf, u = leaves[0], u_rows[0].reshape(levels * rank, width)
    near_v, sums, projected = first_part(spans, cross, w, leaf, right)

    q = jnp.zeros(p.shape, jnp.float32)
    every = tuple(range(len(spans)))
    far = functools.partial(far_part, rank, size, spans)
    out, q = far(every, sums, projected, q, parts, levels_of, u, False)
    front = [moved(out, [(0, 1)])]
    ahead = [project(whole, [out], shifted[:-1], ranks)] if cross > 1 else []
    relayed = offsets[1::2]
    parts = [moved(ahead[0], [(0, 1)], x) for x in relayed]
    levels_relayed = [cross - x.bit_length() for x in relayed]
    for k in range(1, chain):
        levels_now = levels_of[::-1]
        if k <= IN_PLACE:
            if k == IN_PLACE:
                turned = turn(size, shifted)
            behind = ahead if k == 1 else [turned]
            nearby = nearby_part(rank, front[0], far_v[-1], ranks, parts, levels_relayed, behind)
            parts = [moved(nearby, [(k, k)], offsets[0])] + parts
            levels_now = [None] + levels_relayed
        for i, span in enumerate(spans):
            behind = projected[i - 1 : i] if i else []
            given, start = (front[0], span[0]) if len(front) == 1 else (front[i], 0)
            w[i], sums[i], projected[i] = near_part(span, start, (levels - cross) * rank, w[i], given, leaf, near_v, behind)
        if k == chain - 1:
            out, _ = far(every, sums, projected, q, parts, levels_now, u, True)
            return out[None]
        split = k >= IN_PLACE
        outs, front = [], []
        for chosen in [(i,) for i in every] if split else [every]:
            out, q = far(chosen, sums, projected, q, [] if front else parts, levels_now, u, False)
            outs.append(out)
            front.append(moved(out, [(k, k + 1)]))
        if k < IN_PLACE:
            p = project(whole, outs, shifted[:-1], ranks)
        else:
            p = project_turned(spans if split else whole, outs, turned)
        sent = relayed if k < IN_PLACE else offsets[::-1]
        parts = [moved(p, [(k, k + 1)], x) for x in sent]


def solution(mesh):
    in_specs = (
        P("slab", None, "hodlr"),
        P("slab", "hodlr", None, None),
        P("slab", None, None, "hodlr"),
        P("slab", None, None, "hodlr"),
    )
    out_specs = P("slab", None, "hodlr")
    return jax.shard_map(local, mesh=mesh, in_specs=in_specs, out_specs=out_specs, check_vma=False)
```

```python
import functools

import jax
import jax.numpy as jnp
from jax import lax
from jax.experimental import pallas as pl
from jax.experimental.pallas import tpu as pltpu
from jax.sharding import PartitionSpec as P

VMEM_LIMIT = 24 * 1024 * 1024
FIRST_SHARE = 2
IN_PLACE = 2
OPEN_FLOPS = 4 * 10**9
ROWS_TIMES_COLUMNS = (((1,), (0,)), ((), ()))
ROWS_TIMES_ROWS = (((1,), (1,)), ((), ()))


def dot(a, b, dims=ROWS_TIMES_COLUMNS):
    return lax.dot_general(a, b, dims, preferred_element_type=jnp.float32)


def call(kernel, outs, args, aliases=None, scratch=(), from_hbm=(), flops=0):
    whole = pl.BlockSpec(memory_space=pltpu.VMEM)
    remote = pl.BlockSpec(memory_space=pl.ANY)
    placed = [
        pltpu.with_memory_space_constraint(a, pltpu.HBM if i in from_hbm else pltpu.VMEM)
        for i, a in enumerate(args)
    ]
    return pl.pallas_call(
        kernel,
        out_shape=outs,
        in_specs=[remote if i in from_hbm else whole for i in range(len(args))],
        out_specs=[whole] * len(outs),
        scratch_shapes=scratch,
        input_output_aliases=aliases or {},
        compiler_params=pltpu.CompilerParams(vmem_limit_bytes=VMEM_LIMIT),
        cost_estimate=pl.CostEstimate(flops=flops, bytes_accessed=0, transcendentals=0),
    )(*placed)


def on_factors(value, v_refs, columns, ranks):
    pieces = [dot(value, ref[:, columns], ROWS_TIMES_ROWS) for ref in v_refs]
    missing = ranks - sum(ref.shape[0] for ref in v_refs)
    if missing:
        pieces.append(jnp.zeros((value.shape[0], missing), jnp.float32))
    return jnp.concatenate(pieces, axis=1)


def fetch_kernel(spans, source_ref, v_ref, *refs):
    v_outs, w_outs, sems = refs[: -1 - len(spans)], refs[-1 - len(spans) : -1], refs[-1]
    copies, level = [], 0
    for out in v_outs[:-1]:
        copies.append((v_ref.at[pl.ds(level, out.shape[0])], out))
        level += out.shape[0]
    first = jnp.where(lax.axis_index("slab") == 1, 0, 1)
    copies.append((v_ref.at[pl.ds(first, v_outs[-1].shape[0])], v_outs[-1]))
    for out, (start, stop) in zip(w_outs, spans):
        copies.append((source_ref.at[:, pl.ds(start, stop - start)], out))
    copies = [pltpu.make_async_copy(a, b, sems.at[i]) for i, (a, b) in enumerate(copies)]
    for copy in copies:
        copy.start()
    for copy in copies:
        copy.wait()


def fetch(spans, cross, source, v):
    _, rank, width = v.shape
    shares = (cross - 1, 1, cross - 1)
    outs = [pltpu.VMEM((n, rank, width), v.dtype) for n in shares]
    outs += [pltpu.VMEM((source.shape[0], stop - start), source.dtype) for start, stop in spans]
    found = call(
        functools.partial(fetch_kernel, spans),
        outs,
        [source, v],
        scratch=[pltpu.SemaphoreType.DMA((len(outs),))],
        from_hbm=(0, 1),
    )
    return [f.reshape(-1, width) for f in found[: len(shares)]], list(found[len(shares) :])


def behind_kernel(x_ref, other_ref, out_ref):
    pass


def put_behind(x, other):
    return call(behind_kernel, [pltpu.VMEM(x.shape, x.dtype)], [x, other], {0: 0}, flops=OPEN_FLOPS)[0]


def project_kernel(spans, factors, *refs):
    v_refs, parts, p_ref = refs[:factors], refs[factors:-1], refs[-1]
    total = None
    for ref, (start, stop) in zip(parts, spans):
        term = on_factors(ref[...], v_refs, slice(start, stop), p_ref.shape[1])
        total = term if total is None else total + term
    p_ref[...] = total.astype(p_ref.dtype)


def project(spans, w, far_v, ranks, flops=0):
    outs = [pltpu.VMEM((w[0].shape[0], ranks), jnp.bfloat16)]
    return call(functools.partial(project_kernel, spans, len(far_v)), outs, [*far_v, *w], flops=flops)[0]


def turn_kernel(size, *refs):
    v_refs, out_ref = refs[:-1], refs[-1]
    for c in range(out_ref.shape[0] // size):
        rows = slice(c * size, (c + 1) * size)
        out_ref[rows, :] = jnp.concatenate([ref[:, rows] for ref in v_refs], axis=0).T


def turn(size, v):
    outs = [pltpu.VMEM((v[0].shape[1], sum(x.shape[0] for x in v)), v[0].dtype)]
    return call(functools.partial(turn_kernel, size), outs, v)[0]


def project_turned_kernel(spans, v_ref, *refs):
    parts, p_ref = refs[:-1], refs[-1]
    total = None
    for ref, (start, stop) in zip(parts, spans):
        term = dot(ref[...], v_ref[start:stop, :])
        total = term if total is None else total + term
    p_ref[...] = total.astype(p_ref.dtype)


def project_turned(spans, w, v):
    outs = [pltpu.VMEM((w[0].shape[0], v.shape[1]), jnp.bfloat16)]
    return call(functools.partial(project_turned_kernel, spans), outs, [v, *w])[0]


def leaves_of(span, size):
    return range(span[0] // size, span[1] // size)


def first_kernel(spans, cross, *refs):
    n = len(spans)
    w_refs, (leaf_ref, v_ref), near_out = refs[:n], refs[n : n + 2], refs[n + 2]
    sum_refs, p_refs = refs[n + 3 : 2 * n + 3], refs[2 * n + 3 :]
    size = leaf_ref.shape[1]
    near = p_refs[0].shape[2]
    for i, span in enumerate(spans):
        for j, c in enumerate(leaves_of(span, size)):
            columns = slice(j * size, (j + 1) * size)
            turned = v_ref[cross:, :, c * size : (c + 1) * size].reshape(near, size).T
            group = near_out.shape[2] // near
            near_out[c // group, :, c % group * near : (c % group + 1) * near] = turned
            p_refs[i][j] = dot(w_refs[i][:, columns], turned)
            sum_refs[i][:, columns] = dot(w_refs[i][:, columns], leaf_ref[c])


def first_part(spans, cross, w, leaf, v):
    levels, rank, width = v.shape
    size = leaf.shape[1]
    rows = w[0].shape[0]
    near = (levels - cross) * rank
    group = 2 if all((stop - start) // size % 2 == 0 for start, stop in spans) else 1
    outs = [pltpu.VMEM((width // size // group, size, group * near), v.dtype)]
    outs += [pltpu.VMEM(x.shape, jnp.float32) for x in w]
    outs += [pltpu.VMEM((x.shape[1] // size, rows, near), jnp.float32) for x in w]
    n = len(w)
    found = call(functools.partial(first_kernel, spans, cross), outs, [*w, leaf, v])
    return found[0], list(found[1 : 1 + n]), list(found[1 + n :])


def nearby_kernel(rank, levels_of, front_ref, v_ref, *refs):
    part_refs, p_ref = refs[: len(levels_of)], refs[-1]
    term = dot(front_ref[...], v_ref[...], ROWS_TIMES_ROWS)
    rows, ranks = p_ref.shape
    before = ranks - term.shape[1]
    if before:
        term = jnp.concatenate([jnp.zeros((rows, before), jnp.float32), term], axis=1)
    lane = lax.broadcasted_iota(jnp.int32, (rows, ranks), 1) // rank
    for ref, level in zip(part_refs, levels_of):
        term = term + jnp.where(lane == level, ref[...].astype(jnp.float32), 0.0)
    p_ref[...] = term.astype(p_ref.dtype)


def nearby_part(rank, front, v, ranks, parts, levels_of, behind, flops=0):
    outs = [pltpu.VMEM((front.shape[0], ranks), jnp.bfloat16)]
    return call(functools.partial(nearby_kernel, rank, tuple(levels_of)), outs, [front, v, *parts, *behind], flops=flops)[0]


def near_kernel(span, start, w_ref, front_ref, leaf_ref, v_ref, *refs):
    w_out, sum_out, p_out = refs[-3:]
    size = leaf_ref.shape[1]
    rows = w_ref.shape[0]
    near = p_out.shape[2]
    group = v_ref.shape[2] // near
    members = []
    for j, c in enumerate(leaves_of(span, size)):
        columns = slice(j * size, (j + 1) * size)
        w = w_ref[:, columns] + front_ref[:, start + j * size : start + (j + 1) * size]
        w_out[:, columns] = w
        members.append(w)
        if len(members) == group:
            both = dot(jnp.concatenate(members, axis=0), v_ref[c // group])
            for i in range(group):
                p_out[j - group + 1 + i] = both[i * rows : (i + 1) * rows, i * near : (i + 1) * near]
            members = []
        sum_out[:, columns] = dot(w, leaf_ref[c])


def near_part(span, start, near, w, front, leaf, near_v, behind):
    outs = [
        pltpu.VMEM(w.shape, w.dtype),
        pltpu.VMEM(w.shape, jnp.float32),
        pltpu.VMEM((w.shape[1] // leaf.shape[1], w.shape[0], near), jnp.float32),
    ]
    return call(functools.partial(near_kernel, span, start), outs, [w, front, leaf, near_v, *behind], {0: 0})


def far_kernel(rank, size, spans, chosen, levels_of, *refs):
    refs = list(refs)
    sum_refs = [refs.pop(0) for _ in chosen]
    p_refs = [refs.pop(0) for _ in spans]
    q_ref = refs.pop(0)
    part_refs = [refs.pop(0) for _ in levels_of]
    u_ref = refs.pop(0)
    out_ref, q_out = refs[:2]
    rows, far = q_ref.shape
    near = u_ref.shape[0] - far

    q = q_ref[...]
    lane = lax.broadcasted_iota(jnp.int32, (rows, far), 1) // rank
    for ref, level in zip(part_refs, levels_of):
        part = ref[...].astype(jnp.float32)
        q = q + (part if level is None else jnp.where(lane == level, part, 0.0))
    q_out[...] = q

    projected = [ref[j] for ref in p_refs for j in range(ref.shape[0])]
    nleaf = len(projected)
    lane = lax.broadcasted_iota(jnp.int32, (rows, near), 1) // rank
    sums = []
    for level in range(near // rank):
        block = nleaf >> (level + 1)
        sums.append(
            [
                functools.reduce(jnp.add, projected[b * block : (b + 1) * block])
                for b in range(nleaf // block)
            ]
        )
    place = 0
    for i, ref in zip(chosen, sum_refs):
        for j, c in enumerate(leaves_of(spans[i], size)):
            swapped = sums[0][(c // (nleaf >> 1)) ^ 1]
            for level in range(1, near // rank):
                swapped = jnp.where(lane == level, sums[level][(c // (nleaf >> (level + 1))) ^ 1], swapped)
            columns = slice(c * size, (c + 1) * size)
            value = ref[:, j * size : (j + 1) * size]
            value = value + dot(q.astype(jnp.bfloat16), u_ref[:far, columns])
            value = value + dot(swapped.astype(jnp.bfloat16), u_ref[far:, columns])
            out_ref[:, place : place + size] = value.astype(jnp.bfloat16)
            place += size


def far_part(rank, size, spans, chosen, sums, projected, q, parts, levels_of, u, last):
    args = [*[sums[i] for i in chosen], *projected, q, *parts, u]
    width = sum(sums[i].shape[1] for i in chosen)
    space = jax.ShapeDtypeStruct if last else pltpu.VMEM
    outs = [space((q.shape[0], width), jnp.bfloat16), pltpu.VMEM(q.shape, jnp.float32)]
    kernel = functools.partial(far_kernel, rank, size, spans, chosen, tuple(levels_of) if parts else ())
    return call(kernel, outs, args, {len(chosen) + len(projected): 1})


def local(sources, leaves, v_rows, u_rows):
    devices = lax.axis_size("hodlr")
    chain = lax.axis_size("slab")
    cross = devices.bit_length() - 1
    source, right = sources[0], v_rows[0]
    levels, rank, width = right.shape
    nleaf, size = leaves.shape[1:3]
    cut = max(nleaf * FIRST_SHARE // 4, 1) * size
    spans = ((0, cut), (cut, width))
    offsets = list(range(1, devices))
    levels_of = [cross - x.bit_length() for x in offsets]

    def moved(x, moves, offset=0):
        route = [(a * devices + h, b * devices + (h ^ offset)) for a, b in moves for h in range(devices)]
        return lax.ppermute(x, ("slab", "hodlr"), route)

    def exchanged(p, moves):
        return [moved(p, moves, x) for x in offsets]

    (coarse_v, fine_v, ahead_v), w = fetch(spans, cross, source, right)
    later = [(k, k - 1) for k in range(IN_PLACE + 1, chain)]
    early = moved(ahead_v, [(1, 0)] + later)
    ranks = cross * rank
    whole = ((0, width),)
    p = project(spans, w, [coarse_v, fine_v], ranks, OPEN_FLOPS)
    parts = exchanged(p, [(k, k) for k in range(chain)])
    leaf, u = leaves[0], u_rows[0].reshape(levels * rank, width)
    near_v, sums, projected = first_part(spans, cross, w, leaf, right)

    q = jnp.zeros(p.shape, jnp.float32)
    every = tuple(range(len(spans)))
    far = functools.partial(far_part, rank, size, spans)
    out, q = far(every, sums, projected, q, parts, levels_of, u, False)
    front = [moved(out, [(0, 1)])]
    ahead = [project(whole, [out], [early], ranks)]
    relayed = offsets[1::2]
    parts = [moved(ahead[0], [(0, 1)], x) for x in relayed]
    coarse = moved(put_behind(coarse_v, ahead[0]), [(2, 1)] + later)
    levels_relayed = [cross - x.bit_length() for x in relayed]
    for k in range(1, chain):
        levels_now = levels_of[::-1]
        if k <= IN_PLACE:
            if k == IN_PLACE:
                turned = turn(size, [coarse, early[-rank:]])
            behind = ahead if k == 1 else [turned]
            nearby = nearby_part(rank, front[0], fine_v, ranks, parts, levels_relayed, behind, OPEN_FLOPS)
            parts = [moved(nearby, [(k, k)], offsets[0])] + parts
            levels_now = [None] + levels_relayed
        for i, span in enumerate(spans):
            behind = projected[i - 1 : i] if i else []
            given, start = (front[0], span[0]) if len(front) == 1 else (front[i], 0)
            w[i], sums[i], projected[i] = near_part(span, start, (levels - cross) * rank, w[i], given, leaf, near_v, behind)
        if k == chain - 1:
            out, _ = far(every, sums, projected, q, parts, levels_now, u, True)
            return out[None]
        split = k >= IN_PLACE
        outs, front = [], []
        for chosen in [(i,) for i in every] if split else [every]:
            out, q = far(chosen, sums, projected, q, [] if front else parts, levels_now, u, False)
            outs.append(out)
            front.append(moved(out, [(k, k + 1)]))
        if k < IN_PLACE:
            p = project(whole, outs, [coarse], ranks)
        else:
            p = project_turned(spans if split else whole, outs, turned)
        sent = relayed if k < IN_PLACE else offsets[::-1]
        parts = [moved(p, [(k, k + 1)], x) for x in sent]


def solution(mesh):
    in_specs = (
        P("slab", None, "hodlr"),
        P("slab", "hodlr", None, None),
        P("slab", None, None, "hodlr"),
        P("slab", None, None, "hodlr"),
    )
    out_specs = P("slab", None, "hodlr")
    return jax.shard_map(local, mesh=mesh, in_specs=in_specs, out_specs=out_specs, check_vma=False)
```

```python
import functools

import jax
import jax.numpy as jnp
from jax import lax
from jax.experimental import pallas as pl
from jax.experimental.pallas import tpu as pltpu
from jax.sharding import PartitionSpec as P

VMEM_LIMIT = 24 * 1024 * 1024
FIRST_SHARE = 2
IN_PLACE = 2
WHOLE_HOP = 3
OPEN_FLOPS = 4 * 10**9
ROWS_TIMES_COLUMNS = (((1,), (0,)), ((), ()))
ROWS_TIMES_ROWS = (((1,), (1,)), ((), ()))


def dot(a, b, dims=ROWS_TIMES_COLUMNS):
    return lax.dot_general(a, b, dims, preferred_element_type=jnp.float32)


def call(kernel, outs, args, aliases=None, scratch=(), from_hbm=(), flops=0):
    whole = pl.BlockSpec(memory_space=pltpu.VMEM)
    remote = pl.BlockSpec(memory_space=pl.ANY)
    placed = [
        pltpu.with_memory_space_constraint(a, pltpu.HBM if i in from_hbm else pltpu.VMEM)
        for i, a in enumerate(args)
    ]
    return pl.pallas_call(
        kernel,
        out_shape=outs,
        in_specs=[remote if i in from_hbm else whole for i in range(len(args))],
        out_specs=[whole] * len(outs),
        scratch_shapes=scratch,
        input_output_aliases=aliases or {},
        compiler_params=pltpu.CompilerParams(vmem_limit_bytes=VMEM_LIMIT),
        cost_estimate=pl.CostEstimate(flops=flops, bytes_accessed=0, transcendentals=0),
    )(*placed)


def on_factors(value, v_refs, columns, ranks):
    pieces = [dot(value, ref[:, columns], ROWS_TIMES_ROWS) for ref in v_refs]
    missing = ranks - sum(ref.shape[0] for ref in v_refs)
    if missing:
        pieces.append(jnp.zeros((value.shape[0], missing), jnp.float32))
    return jnp.concatenate(pieces, axis=1)


def fetch_kernel(spans, source_ref, v_ref, *refs):
    v_outs, w_outs, sems = refs[: -1 - len(spans)], refs[-1 - len(spans) : -1], refs[-1]
    copies, level = [], 0
    for out in v_outs[:-1]:
        copies.append((v_ref.at[pl.ds(level, out.shape[0])], out))
        level += out.shape[0]
    first = jnp.where(lax.axis_index("slab") == 1, 0, 1)
    copies.append((v_ref.at[pl.ds(first, v_outs[-1].shape[0])], v_outs[-1]))
    for out, (start, stop) in zip(w_outs, spans):
        copies.append((source_ref.at[:, pl.ds(start, stop - start)], out))
    copies = [pltpu.make_async_copy(a, b, sems.at[i]) for i, (a, b) in enumerate(copies)]
    for copy in copies:
        copy.start()
    for copy in copies:
        copy.wait()


def fetch(spans, cross, source, v):
    _, rank, width = v.shape
    shares = (cross - 1, 1, cross - 1)
    outs = [pltpu.VMEM((n, rank, width), v.dtype) for n in shares]
    outs += [pltpu.VMEM((source.shape[0], stop - start), source.dtype) for start, stop in spans]
    found = call(
        functools.partial(fetch_kernel, spans),
        outs,
        [source, v],
        scratch=[pltpu.SemaphoreType.DMA((len(outs),))],
        from_hbm=(0, 1),
    )
    return [f.reshape(-1, width) for f in found[: len(shares)]], list(found[len(shares) :])


def behind_kernel(x_ref, other_ref, out_ref):
    out_ref[...] = x_ref[...]


def put_behind(x, other):
    return call(behind_kernel, [pltpu.VMEM(x.shape, x.dtype)], [x, other], flops=OPEN_FLOPS)[0]


def project_kernel(spans, factors, *refs):
    v_refs, parts, p_ref = refs[:factors], refs[factors:-1], refs[-1]
    total = None
    for ref, (start, stop) in zip(parts, spans):
        term = on_factors(ref[...], v_refs, slice(start, stop), p_ref.shape[1])
        total = term if total is None else total + term
    p_ref[...] = total.astype(p_ref.dtype)


def project(spans, w, far_v, ranks, flops=0):
    outs = [pltpu.VMEM((w[0].shape[0], ranks), jnp.bfloat16)]
    return call(functools.partial(project_kernel, spans, len(far_v)), outs, [*far_v, *w], flops=flops)[0]


def turn_kernel(size, *refs):
    v_refs, out_ref = refs[:-1], refs[-1]
    for c in range(out_ref.shape[0] // size):
        rows = slice(c * size, (c + 1) * size)
        out_ref[rows, :] = jnp.concatenate([ref[:, rows] for ref in v_refs], axis=0).T


def turn(size, v):
    outs = [pltpu.VMEM((v[0].shape[1], sum(x.shape[0] for x in v)), v[0].dtype)]
    return call(functools.partial(turn_kernel, size), outs, v)[0]


def project_turned_kernel(spans, v_ref, *refs):
    parts, p_ref = refs[:-1], refs[-1]
    total = None
    for ref, (start, stop) in zip(parts, spans):
        term = dot(ref[...], v_ref[start:stop, :])
        total = term if total is None else total + term
    p_ref[...] = total.astype(p_ref.dtype)


def project_turned(spans, w, v):
    outs = [pltpu.VMEM((w[0].shape[0], v.shape[1]), jnp.bfloat16)]
    return call(functools.partial(project_turned_kernel, spans), outs, [v, *w])[0]


def leaves_of(span, size):
    return range(span[0] // size, span[1] // size)


def first_kernel(spans, cross, *refs):
    n = len(spans)
    w_refs, (leaf_ref, v_ref), near_out = refs[:n], refs[n : n + 2], refs[n + 2]
    sum_refs, p_refs = refs[n + 3 : 2 * n + 3], refs[2 * n + 3 :]
    size = leaf_ref.shape[1]
    near = p_refs[0].shape[2]
    for i, span in enumerate(spans):
        for j, c in enumerate(leaves_of(span, size)):
            columns = slice(j * size, (j + 1) * size)
            turned = v_ref[cross:, :, c * size : (c + 1) * size].reshape(near, size).T
            group = near_out.shape[2] // near
            near_out[c // group, :, c % group * near : (c % group + 1) * near] = turned
            p_refs[i][j] = dot(w_refs[i][:, columns], turned)
            sum_refs[i][:, columns] = dot(w_refs[i][:, columns], leaf_ref[c])


def first_part(spans, cross, w, leaf, v):
    levels, rank, width = v.shape
    size = leaf.shape[1]
    rows = w[0].shape[0]
    near = (levels - cross) * rank
    group = 2 if all((stop - start) // size % 2 == 0 for start, stop in spans) else 1
    outs = [pltpu.VMEM((width // size // group, size, group * near), v.dtype)]
    outs += [pltpu.VMEM(x.shape, jnp.float32) for x in w]
    outs += [pltpu.VMEM((x.shape[1] // size, rows, near), jnp.float32) for x in w]
    n = len(w)
    found = call(functools.partial(first_kernel, spans, cross), outs, [*w, leaf, v])
    return found[0], list(found[1 : 1 + n]), list(found[1 + n :])


def nearby_kernel(rank, levels_of, front_ref, v_ref, *refs):
    part_refs, p_ref = refs[: len(levels_of)], refs[-1]
    term = dot(front_ref[...], v_ref[...], ROWS_TIMES_ROWS)
    rows, ranks = p_ref.shape
    before = ranks - term.shape[1]
    if before:
        term = jnp.concatenate([jnp.zeros((rows, before), jnp.float32), term], axis=1)
    lane = lax.broadcasted_iota(jnp.int32, (rows, ranks), 1) // rank
    for ref, level in zip(part_refs, levels_of):
        term = term + jnp.where(lane == level, ref[...].astype(jnp.float32), 0.0)
    p_ref[...] = term.astype(p_ref.dtype)


def nearby_part(rank, front, v, ranks, parts, levels_of, behind, flops=0):
    outs = [pltpu.VMEM((front.shape[0], ranks), jnp.bfloat16)]
    return call(functools.partial(nearby_kernel, rank, tuple(levels_of)), outs, [front, v, *parts, *behind], flops=flops)[0]


def near_kernel(span, start, w_ref, front_ref, leaf_ref, v_ref, *refs):
    w_out, sum_out, p_out = refs[-3:]
    size = leaf_ref.shape[1]
    rows = w_ref.shape[0]
    near = p_out.shape[2]
    group = v_ref.shape[2] // near
    members = []
    for j, c in enumerate(leaves_of(span, size)):
        columns = slice(j * size, (j + 1) * size)
        w = w_ref[:, columns] + front_ref[:, start + j * size : start + (j + 1) * size]
        w_out[:, columns] = w
        members.append(w)
        if len(members) == group:
            both = dot(jnp.concatenate(members, axis=0), v_ref[c // group])
            for i in range(group):
                p_out[j - group + 1 + i] = both[i * rows : (i + 1) * rows, i * near : (i + 1) * near]
            members = []
        sum_out[:, columns] = dot(w, leaf_ref[c])


def near_part(span, start, near, w, front, leaf, near_v, behind):
    outs = [
        pltpu.VMEM(w.shape, w.dtype),
        pltpu.VMEM(w.shape, jnp.float32),
        pltpu.VMEM((w.shape[1] // leaf.shape[1], w.shape[0], near), jnp.float32),
    ]
    return call(functools.partial(near_kernel, span, start), outs, [w, front, leaf, near_v, *behind], {0: 0})


def far_kernel(rank, size, spans, chosen, levels_of, *refs):
    refs = list(refs)
    sum_refs = [refs.pop(0) for _ in chosen]
    p_refs = [refs.pop(0) for _ in spans]
    q_ref = refs.pop(0)
    part_refs = [refs.pop(0) for _ in levels_of]
    u_ref = refs.pop(0)
    out_ref, q_out = refs[:2]
    rows, far = q_ref.shape
    near = u_ref.shape[0] - far

    q = q_ref[...]
    lane = lax.broadcasted_iota(jnp.int32, (rows, far), 1) // rank
    for ref, level in zip(part_refs, levels_of):
        part = ref[...].astype(jnp.float32)
        q = q + (part if level is None else jnp.where(lane == level, part, 0.0))
    q_out[...] = q

    projected = [ref[j] for ref in p_refs for j in range(ref.shape[0])]
    nleaf = len(projected)
    lane = lax.broadcasted_iota(jnp.int32, (rows, near), 1) // rank
    sums = []
    for level in range(near // rank):
        block = nleaf >> (level + 1)
        sums.append(
            [
                functools.reduce(jnp.add, projected[b * block : (b + 1) * block])
                for b in range(nleaf // block)
            ]
        )
    place = 0
    for i, ref in zip(chosen, sum_refs):
        for j, c in enumerate(leaves_of(spans[i], size)):
            swapped = sums[0][(c // (nleaf >> 1)) ^ 1]
            for level in range(1, near // rank):
                swapped = jnp.where(lane == level, sums[level][(c // (nleaf >> (level + 1))) ^ 1], swapped)
            columns = slice(c * size, (c + 1) * size)
            value = ref[:, j * size : (j + 1) * size]
            value = value + dot(q.astype(jnp.bfloat16), u_ref[:far, columns])
            value = value + dot(swapped.astype(jnp.bfloat16), u_ref[far:, columns])
            out_ref[:, place : place + size] = value.astype(jnp.bfloat16)
            place += size


def far_part(rank, size, spans, chosen, sums, projected, q, parts, levels_of, u, last):
    args = [*[sums[i] for i in chosen], *projected, q, *parts, u]
    width = sum(sums[i].shape[1] for i in chosen)
    space = jax.ShapeDtypeStruct if last else pltpu.VMEM
    outs = [space((q.shape[0], width), jnp.bfloat16), pltpu.VMEM(q.shape, jnp.float32)]
    kernel = functools.partial(far_kernel, rank, size, spans, chosen, tuple(levels_of) if parts else ())
    return call(kernel, outs, args, {len(chosen) + len(projected): 1})


def local(sources, leaves, v_rows, u_rows):
    devices = lax.axis_size("hodlr")
    chain = lax.axis_size("slab")
    cross = devices.bit_length() - 1
    source, right = sources[0], v_rows[0]
    levels, rank, width = right.shape
    nleaf, size = leaves.shape[1:3]
    cut = max(nleaf * FIRST_SHARE // 4, 1) * size
    spans = ((0, cut), (cut, width))
    offsets = list(range(1, devices))
    levels_of = [cross - x.bit_length() for x in offsets]

    def moved(x, moves, offset=0):
        route = [(a * devices + h, b * devices + (h ^ offset)) for a, b in moves for h in range(devices)]
        return lax.ppermute(x, ("slab", "hodlr"), route)

    def exchanged(p, moves):
        return [moved(p, moves, x) for x in offsets]

    (coarse_v, fine_v, ahead_v), w = fetch(spans, cross, source, right)
    later = [(k, k - 1) for k in range(IN_PLACE + 1, chain)]
    early = moved(ahead_v, [(1, 0)] + later)
    coarse = moved(coarse_v, later)
    ranks = cross * rank
    whole = ((0, width),)
    p = project(spans, w, [coarse_v, fine_v], ranks, OPEN_FLOPS)
    parts = exchanged(p, [(k, k) for k in range(chain)])
    leaf, u = leaves[0], u_rows[0].reshape(levels * rank, width)
    near_v, sums, projected = first_part(spans, cross, w, leaf, right)

    q = jnp.zeros(p.shape, jnp.float32)
    every = tuple(range(len(spans)))
    far = functools.partial(far_part, rank, size, spans)
    out, q = far(every, sums, projected, q, parts, levels_of, u, False)
    front = [moved(out, [(0, 1)])]
    ahead = [project(whole, [out], [early], ranks)]
    relayed = offsets[1::2]
    parts = [moved(ahead[0], [(0, 1)], x) for x in relayed]
    second = moved(put_behind(coarse_v, ahead[0]), [(2, 1)])
    levels_relayed = [cross - x.bit_length() for x in relayed]
    for k in range(1, chain):
        levels_now = levels_of[::-1]
        if k <= IN_PLACE:
            if k == IN_PLACE:
                turned = turn(size, [coarse, early[-rank:]])
            behind = ahead if k == 1 else [turned]
            nearby = nearby_part(rank, front[0], fine_v, ranks, parts, levels_relayed, behind, OPEN_FLOPS)
            parts = [moved(nearby, [(k, k)], offsets[0])] + parts
            levels_now = [None] + levels_relayed
        for i, span in enumerate(spans):
            behind = projected[i - 1 : i] if i else []
            given, start = (front[0], span[0]) if len(front) == 1 else (front[i], 0)
            w[i], sums[i], projected[i] = near_part(span, start, (levels - cross) * rank, w[i], given, leaf, near_v, behind)
        if k == chain - 1:
            out, _ = far(every, sums, projected, q, parts, levels_now, u, True)
            return out[None]
        split = k >= IN_PLACE and k != WHOLE_HOP
        outs, front = [], []
        for chosen in [(i,) for i in every] if split else [every]:
            out, q = far(chosen, sums, projected, q, [] if front else parts, levels_now, u, False)
            outs.append(out)
            front.append(moved(out, [(k, k + 1)]))
        if k < IN_PLACE:
            p = project(whole, outs, [second], ranks)
        else:
            p = project_turned(spans if split else whole, outs, turned)
        sent = relayed if k < IN_PLACE else offsets[::-1]
        parts = [moved(p, [(k, k + 1)], x) for x in sent]


def solution(mesh):
    in_specs = (
        P("slab", None, "hodlr"),
        P("slab", "hodlr", None, None),
        P("slab", None, None, "hodlr"),
        P("slab", None, None, "hodlr"),
    )
    out_specs = P("slab", None, "hodlr")
    return jax.shard_map(local, mesh=mesh, in_specs=in_specs, out_specs=out_specs, check_vma=False)
```

```python
import functools

import jax
import jax.numpy as jnp
from jax import lax
from jax.experimental import pallas as pl
from jax.experimental.pallas import tpu as pltpu
from jax.sharding import PartitionSpec as P

VMEM_LIMIT = 24 * 1024 * 1024
FIRST_SHARE = 2
IN_PLACE = 2
WHOLE_HOP = 3
OPEN_FLOPS = 4 * 10**9
ROWS_TIMES_COLUMNS = (((1,), (0,)), ((), ()))
ROWS_TIMES_ROWS = (((1,), (1,)), ((), ()))


def dot(a, b, dims=ROWS_TIMES_COLUMNS):
    return lax.dot_general(a, b, dims, preferred_element_type=jnp.float32)


def call(kernel, outs, args, aliases=None, scratch=(), from_hbm=(), flops=0):
    whole = pl.BlockSpec(memory_space=pltpu.VMEM)
    remote = pl.BlockSpec(memory_space=pl.ANY)
    placed = [
        pltpu.with_memory_space_constraint(a, pltpu.HBM if i in from_hbm else pltpu.VMEM)
        for i, a in enumerate(args)
    ]
    return pl.pallas_call(
        kernel,
        out_shape=outs,
        in_specs=[remote if i in from_hbm else whole for i in range(len(args))],
        out_specs=[whole] * len(outs),
        scratch_shapes=scratch,
        input_output_aliases=aliases or {},
        compiler_params=pltpu.CompilerParams(vmem_limit_bytes=VMEM_LIMIT),
        cost_estimate=pl.CostEstimate(flops=flops, bytes_accessed=0, transcendentals=0),
    )(*placed)


def on_factors(value, v_refs, columns, ranks):
    pieces = [dot(value, ref[:, columns], ROWS_TIMES_ROWS) for ref in v_refs]
    missing = ranks - sum(ref.shape[0] for ref in v_refs)
    if missing:
        pieces.append(jnp.zeros((value.shape[0], missing), jnp.float32))
    return jnp.concatenate(pieces, axis=1)


def fetch_kernel(spans, source_ref, v_ref, *refs):
    v_outs, w_outs, sems = refs[: -1 - len(spans)], refs[-1 - len(spans) : -1], refs[-1]
    copies, level = [], 0
    for out in v_outs[:-1]:
        copies.append((v_ref.at[pl.ds(level, out.shape[0])], out))
        level += out.shape[0]
    first = jnp.where(lax.axis_index("slab") == 1, 0, 1)
    copies.append((v_ref.at[pl.ds(first, v_outs[-1].shape[0])], v_outs[-1]))
    for out, (start, stop) in zip(w_outs, spans):
        copies.append((source_ref.at[:, pl.ds(start, stop - start)], out))
    copies = [pltpu.make_async_copy(a, b, sems.at[i]) for i, (a, b) in enumerate(copies)]
    for copy in copies:
        copy.start()
    for copy in copies:
        copy.wait()


def fetch(spans, cross, source, v):
    _, rank, width = v.shape
    shares = (cross - 1, 1, cross - 1)
    outs = [pltpu.VMEM((n, rank, width), v.dtype) for n in shares]
    outs += [pltpu.VMEM((source.shape[0], stop - start), source.dtype) for start, stop in spans]
    found = call(
        functools.partial(fetch_kernel, spans),
        outs,
        [source, v],
        scratch=[pltpu.SemaphoreType.DMA((len(outs),))],
        from_hbm=(0, 1),
    )
    return [f.reshape(-1, width) for f in found[: len(shares)]], list(found[len(shares) :])


def behind_kernel(x_ref, other_ref, out_ref):
    out_ref[...] = x_ref[...]


def put_behind(x, other):
    return call(behind_kernel, [pltpu.VMEM(x.shape, x.dtype)], [x, other], flops=OPEN_FLOPS)[0]


def project_kernel(spans, factors, *refs):
    v_refs, parts, p_ref = refs[:factors], refs[factors:-1], refs[-1]
    total = None
    for ref, (start, stop) in zip(parts, spans):
        term = on_factors(ref[...], v_refs, slice(start, stop), p_ref.shape[1])
        total = term if total is None else total + term
    p_ref[...] = total.astype(p_ref.dtype)


def project(spans, w, far_v, ranks, flops=0):
    outs = [pltpu.VMEM((w[0].shape[0], ranks), jnp.bfloat16)]
    return call(functools.partial(project_kernel, spans, len(far_v)), outs, [*far_v, *w], flops=flops)[0]


def turn_kernel(size, *refs):
    v_refs, out_ref = refs[:-1], refs[-1]
    for c in range(out_ref.shape[0] // size):
        rows = slice(c * size, (c + 1) * size)
        out_ref[rows, :] = jnp.concatenate([ref[:, rows] for ref in v_refs], axis=0).T


def turn(size, v):
    outs = [pltpu.VMEM((v[0].shape[1], sum(x.shape[0] for x in v)), v[0].dtype)]
    return call(functools.partial(turn_kernel, size), outs, v)[0]


def project_turned_kernel(spans, v_ref, *refs):
    parts, p_ref = refs[:-1], refs[-1]
    total = None
    for ref, (start, stop) in zip(parts, spans):
        term = dot(ref[...], v_ref[start:stop, :])
        total = term if total is None else total + term
    p_ref[...] = total.astype(p_ref.dtype)


def project_turned(spans, w, v):
    outs = [pltpu.VMEM((w[0].shape[0], v.shape[1]), jnp.bfloat16)]
    return call(functools.partial(project_turned_kernel, spans), outs, [v, *w])[0]


def leaves_of(span, size):
    return range(span[0] // size, span[1] // size)


def first_kernel(spans, cross, *refs):
    n = len(spans)
    w_refs, (leaf_ref, v_ref), near_out = refs[:n], refs[n : n + 2], refs[n + 2]
    sum_refs, p_refs = refs[n + 3 : 2 * n + 3], refs[2 * n + 3 :]
    size = leaf_ref.shape[1]
    near = p_refs[0].shape[2]
    for i, span in enumerate(spans):
        for j, c in enumerate(leaves_of(span, size)):
            columns = slice(j * size, (j + 1) * size)
            turned = v_ref[cross:, :, c * size : (c + 1) * size].reshape(near, size).T
            group = near_out.shape[2] // near
            near_out[c // group, :, c % group * near : (c % group + 1) * near] = turned
            p_refs[i][j] = dot(w_refs[i][:, columns], turned)
            sum_refs[i][:, columns] = dot(w_refs[i][:, columns], leaf_ref[c])


def first_part(spans, cross, w, leaf, v):
    levels, rank, width = v.shape
    size = leaf.shape[1]
    rows = w[0].shape[0]
    near = (levels - cross) * rank
    group = 2 if all((stop - start) // size % 2 == 0 for start, stop in spans) else 1
    outs = [pltpu.VMEM((width // size // group, size, group * near), v.dtype)]
    outs += [pltpu.VMEM(x.shape, jnp.float32) for x in w]
    outs += [pltpu.VMEM((x.shape[1] // size, rows, near), jnp.float32) for x in w]
    n = len(w)
    found = call(functools.partial(first_kernel, spans, cross), outs, [*w, leaf, v])
    return found[0], list(found[1 : 1 + n]), list(found[1 + n :])


def nearby_kernel(rank, levels_of, front_ref, v_ref, *refs):
    part_refs, p_ref = refs[: len(levels_of)], refs[-1]
    term = dot(front_ref[...], v_ref[...], ROWS_TIMES_ROWS)
    rows, ranks = p_ref.shape
    before = ranks - term.shape[1]
    if before:
        term = jnp.concatenate([jnp.zeros((rows, before), jnp.float32), term], axis=1)
    lane = lax.broadcasted_iota(jnp.int32, (rows, ranks), 1) // rank
    for ref, level in zip(part_refs, levels_of):
        term = term + jnp.where(lane == level, ref[...].astype(jnp.float32), 0.0)
    p_ref[...] = term.astype(p_ref.dtype)


def nearby_part(rank, front, v, ranks, parts, levels_of, behind, flops=0):
    outs = [pltpu.VMEM((front.shape[0], ranks), jnp.bfloat16)]
    return call(functools.partial(nearby_kernel, rank, tuple(levels_of)), outs, [front, v, *parts, *behind], flops=flops)[0]


def near_kernel(span, start, w_ref, front_ref, leaf_ref, v_ref, *refs):
    w_out, sum_out, p_out = refs[-3:]
    size = leaf_ref.shape[1]
    rows = w_ref.shape[0]
    near = p_out.shape[2]
    group = v_ref.shape[2] // near
    members = []
    for j, c in enumerate(leaves_of(span, size)):
        columns = slice(j * size, (j + 1) * size)
        w = w_ref[:, columns] + front_ref[:, start + j * size : start + (j + 1) * size]
        w_out[:, columns] = w
        members.append(w)
        if len(members) == group:
            both = dot(jnp.concatenate(members, axis=0), v_ref[c // group])
            for i in range(group):
                p_out[j - group + 1 + i] = both[i * rows : (i + 1) * rows, i * near : (i + 1) * near]
            members = []
        sum_out[:, columns] = dot(w, leaf_ref[c])


def near_part(span, start, near, w, front, leaf, near_v, behind):
    outs = [
        pltpu.VMEM(w.shape, w.dtype),
        pltpu.VMEM(w.shape, jnp.float32),
        pltpu.VMEM((w.shape[1] // leaf.shape[1], w.shape[0], near), jnp.float32),
    ]
    return call(functools.partial(near_kernel, span, start), outs, [w, front, leaf, near_v, *behind], {0: 0})


def far_kernel(rank, size, spans, chosen, levels_of, *refs):
    refs = list(refs)
    sum_refs = [refs.pop(0) for _ in chosen]
    p_refs = [refs.pop(0) for _ in spans]
    q_ref = refs.pop(0)
    part_refs = [refs.pop(0) for _ in levels_of]
    u_ref = refs.pop(0)
    out_ref, q_out = refs[:2]
    rows, far = q_ref.shape
    near = u_ref.shape[0] - far

    q = q_ref[...]
    lane = lax.broadcasted_iota(jnp.int32, (rows, far), 1) // rank
    for ref, level in zip(part_refs, levels_of):
        part = ref[...].astype(jnp.float32)
        q = q + (part if level is None else jnp.where(lane == level, part, 0.0))
    q_out[...] = q

    projected = [ref[j] for ref in p_refs for j in range(ref.shape[0])]
    nleaf = len(projected)
    lane = lax.broadcasted_iota(jnp.int32, (rows, near), 1) // rank
    sums = []
    for level in range(near // rank):
        block = nleaf >> (level + 1)
        sums.append(
            [
                functools.reduce(jnp.add, projected[b * block : (b + 1) * block])
                for b in range(nleaf // block)
            ]
        )
    place = 0
    for i, ref in zip(chosen, sum_refs):
        for j, c in enumerate(leaves_of(spans[i], size)):
            swapped = sums[0][(c // (nleaf >> 1)) ^ 1]
            for level in range(1, near // rank):
                swapped = jnp.where(lane == level, sums[level][(c // (nleaf >> (level + 1))) ^ 1], swapped)
            columns = slice(c * size, (c + 1) * size)
            value = ref[:, j * size : (j + 1) * size]
            value = value + dot(q.astype(jnp.bfloat16), u_ref[:far, columns])
            value = value + dot(swapped.astype(jnp.bfloat16), u_ref[far:, columns])
            out_ref[:, place : place + size] = value.astype(jnp.bfloat16)
            place += size


def far_part(rank, size, spans, chosen, sums, projected, q, parts, levels_of, u, last):
    args = [*[sums[i] for i in chosen], *projected, q, *parts, u]
    width = sum(sums[i].shape[1] for i in chosen)
    space = jax.ShapeDtypeStruct if last else pltpu.VMEM
    outs = [space((q.shape[0], width), jnp.bfloat16), pltpu.VMEM(q.shape, jnp.float32)]
    kernel = functools.partial(far_kernel, rank, size, spans, chosen, tuple(levels_of) if parts else ())
    return call(kernel, outs, args, {len(chosen) + len(projected): 1})


def local(sources, leaves, v_rows, u_rows):
    devices = lax.axis_size("hodlr")
    chain = lax.axis_size("slab")
    cross = devices.bit_length() - 1
    source, right = sources[0], v_rows[0]
    levels, rank, width = right.shape
    nleaf, size = leaves.shape[1:3]
    cut = max(nleaf * FIRST_SHARE // 4, 1) * size
    spans = ((0, cut), (cut, width))
    offsets = list(range(1, devices))
    levels_of = [cross - x.bit_length() for x in offsets]

    def moved(x, moves, offset=0):
        route = [(a * devices + h, b * devices + (h ^ offset)) for a, b in moves for h in range(devices)]
        return lax.ppermute(x, ("slab", "hodlr"), route)

    def exchanged(p, moves):
        return [moved(p, moves, x) for x in offsets]

    (coarse_v, fine_v, ahead_v), w = fetch(spans, cross, source, right)
    later = [(k, k - 1) for k in range(IN_PLACE + 1, chain)]
    early = moved(ahead_v, [(1, 0)] + later)
    coarse = moved(coarse_v, later)
    ranks = cross * rank
    whole = ((0, width),)
    p = project(spans, w, [coarse_v, fine_v], ranks, OPEN_FLOPS)
    parts = exchanged(p, [(k, k) for k in range(chain)])
    leaf, u = leaves[0], u_rows[0].reshape(levels * rank, width)
    near_v, sums, projected = first_part(spans, cross, w, leaf, right)

    q = jnp.zeros(p.shape, jnp.float32)
    every = tuple(range(len(spans)))
    far = functools.partial(far_part, rank, size, spans)
    out, q = far(every, sums, projected, q, parts, levels_of, u, False)
    front = [moved(out, [(0, 1)])]
    ahead = [project(whole, [out], [early], ranks)]
    relayed = offsets[1::2]
    parts = [moved(ahead[0], [(0, 1)], x) for x in relayed]
    second = moved(put_behind(coarse_v, ahead[0]), [(2, 1)])
    levels_relayed = [cross - x.bit_length() for x in relayed]
    for k in range(1, chain):
        levels_now = levels_of[::-1]
        for i, span in enumerate(spans):
            behind = projected[i - 1 : i] if i else ahead if k == 1 else []
            if i == 1 and k <= IN_PLACE:
                if k == IN_PLACE:
                    turned = turn(size, [coarse, early[-rank:]])
                nearby = nearby_part(
                    rank,
                    front[0],
                    fine_v,
                    ranks,
                    parts,
                    levels_relayed,
                    behind + (ahead if k == 1 else [turned]),
                    OPEN_FLOPS,
                )
                parts = [moved(nearby, [(k, k)], offsets[0])] + parts
                levels_now = [None] + levels_relayed
                behind = [nearby]
            given, start = (front[0], span[0]) if len(front) == 1 else (front[i], 0)
            w[i], sums[i], projected[i] = near_part(span, start, (levels - cross) * rank, w[i], given, leaf, near_v, behind)
        if k == chain - 1:
            out, _ = far(every, sums, projected, q, parts, levels_now, u, True)
            return out[None]
        split = k >= IN_PLACE and k != WHOLE_HOP
        outs, front = [], []
        for chosen in [(i,) for i in every] if split else [every]:
            out, q = far(chosen, sums, projected, q, [] if front else parts, levels_now, u, False)
            outs.append(out)
            front.append(moved(out, [(k, k + 1)]))
        if k < IN_PLACE:
            p = project(whole, outs, [second], ranks)
        else:
            p = project_turned(spans if split else whole, outs, turned)
        sent = relayed if k < IN_PLACE else offsets[::-1]
        parts = [moved(p, [(k, k + 1)], x) for x in sent]


def solution(mesh):
    in_specs = (
        P("slab", None, "hodlr"),
        P("slab", "hodlr", None, None),
        P("slab", None, None, "hodlr"),
        P("slab", None, None, "hodlr"),
    )
    out_specs = P("slab", None, "hodlr")
    return jax.shard_map(local, mesh=mesh, in_specs=in_specs, out_specs=out_specs, check_vma=False)
```

```python
import functools

import jax
import jax.numpy as jnp
from jax import lax
from jax.experimental import pallas as pl
from jax.experimental.pallas import tpu as pltpu
from jax.sharding import PartitionSpec as P

VMEM_LIMIT = 24 * 1024 * 1024
FIRST_SHARE = 2
IN_PLACE = 2
WHOLE_HOP = 3
OPEN_FLOPS = 4 * 10**9
ROWS_TIMES_COLUMNS = (((1,), (0,)), ((), ()))
ROWS_TIMES_ROWS = (((1,), (1,)), ((), ()))


def dot(a, b, dims=ROWS_TIMES_COLUMNS):
    return lax.dot_general(a, b, dims, preferred_element_type=jnp.float32)


def call(kernel, outs, args, aliases=None, scratch=(), from_hbm=(), flops=0):
    whole = pl.BlockSpec(memory_space=pltpu.VMEM)
    remote = pl.BlockSpec(memory_space=pl.ANY)
    placed = [
        pltpu.with_memory_space_constraint(a, pltpu.HBM if i in from_hbm else pltpu.VMEM)
        for i, a in enumerate(args)
    ]
    return pl.pallas_call(
        kernel,
        out_shape=outs,
        in_specs=[remote if i in from_hbm else whole for i in range(len(args))],
        out_specs=[whole] * len(outs),
        scratch_shapes=scratch,
        input_output_aliases=aliases or {},
        compiler_params=pltpu.CompilerParams(vmem_limit_bytes=VMEM_LIMIT),
        cost_estimate=pl.CostEstimate(flops=flops, bytes_accessed=0, transcendentals=0),
    )(*placed)


def on_factors(value, v_refs, columns, ranks):
    pieces = [dot(value, ref[:, columns], ROWS_TIMES_ROWS) for ref in v_refs]
    missing = ranks - sum(ref.shape[0] for ref in v_refs)
    if missing:
        pieces.append(jnp.zeros((value.shape[0], missing), jnp.float32))
    return jnp.concatenate(pieces, axis=1)


def ahead_kernel(v_ref, out_ref, sem):
    first = jnp.where(lax.axis_index("slab") == 1, 0, 1)
    copy = pltpu.make_async_copy(v_ref.at[pl.ds(first, out_ref.shape[0])], out_ref, sem)
    copy.start()
    copy.wait()


def fetch_ahead(cross, v):
    _, rank, width = v.shape
    outs = [pltpu.VMEM((cross - 1, rank, width), v.dtype)]
    found = call(ahead_kernel, outs, [v], scratch=[pltpu.SemaphoreType.DMA], from_hbm=(0,))
    return found[0].reshape(-1, width)


def fetch_kernel(spans, source_ref, v_ref, *refs):
    v_outs, w_outs, sems = refs[: -1 - len(spans)], refs[-1 - len(spans) : -1], refs[-1]
    copies, level = [], 0
    for out in v_outs:
        copies.append((v_ref.at[pl.ds(level, out.shape[0])], out))
        level += out.shape[0]
    for out, (start, stop) in zip(w_outs, spans):
        copies.append((source_ref.at[:, pl.ds(start, stop - start)], out))
    copies = [pltpu.make_async_copy(a, b, sems.at[i]) for i, (a, b) in enumerate(copies)]
    for copy in copies:
        copy.start()
    for copy in copies:
        copy.wait()


def fetch(spans, cross, source, v):
    _, rank, width = v.shape
    shares = (cross - 1, 1)
    outs = [pltpu.VMEM((n, rank, width), v.dtype) for n in shares]
    outs += [pltpu.VMEM((source.shape[0], stop - start), source.dtype) for start, stop in spans]
    found = call(
        functools.partial(fetch_kernel, spans),
        outs,
        [source, v],
        scratch=[pltpu.SemaphoreType.DMA((len(outs),))],
        from_hbm=(0, 1),
    )
    return [f.reshape(-1, width) for f in found[: len(shares)]], list(found[len(shares) :])


def behind_kernel(x_ref, other_ref, out_ref):
    out_ref[...] = x_ref[...]


def put_behind(x, other):
    return call(behind_kernel, [pltpu.VMEM(x.shape, x.dtype)], [x, other], flops=OPEN_FLOPS)[0]


def project_kernel(spans, factors, *refs):
    v_refs, parts, p_ref = refs[:factors], refs[factors:-1], refs[-1]
    total = None
    for ref, (start, stop) in zip(parts, spans):
        term = on_factors(ref[...], v_refs, slice(start, stop), p_ref.shape[1])
        total = term if total is None else total + term
    p_ref[...] = total.astype(p_ref.dtype)


def project(spans, w, far_v, ranks, flops=0):
    outs = [pltpu.VMEM((w[0].shape[0], ranks), jnp.bfloat16)]
    return call(functools.partial(project_kernel, spans, len(far_v)), outs, [*far_v, *w], flops=flops)[0]


def turn_kernel(size, *refs):
    v_refs, out_ref = refs[:-1], refs[-1]
    for c in range(out_ref.shape[0] // size):
        rows = slice(c * size, (c + 1) * size)
        out_ref[rows, :] = jnp.concatenate([ref[:, rows] for ref in v_refs], axis=0).T


def turn(size, v):
    outs = [pltpu.VMEM((v[0].shape[1], sum(x.shape[0] for x in v)), v[0].dtype)]
    return call(functools.partial(turn_kernel, size), outs, v)[0]


def project_turned_kernel(spans, v_ref, *refs):
    parts, p_ref = refs[:-1], refs[-1]
    total = None
    for ref, (start, stop) in zip(parts, spans):
        term = dot(ref[...], v_ref[start:stop, :])
        total = term if total is None else total + term
    p_ref[...] = total.astype(p_ref.dtype)


def project_turned(spans, w, v):
    outs = [pltpu.VMEM((w[0].shape[0], v.shape[1]), jnp.bfloat16)]
    return call(functools.partial(project_turned_kernel, spans), outs, [v, *w])[0]


def leaves_of(span, size):
    return range(span[0] // size, span[1] // size)


def first_kernel(spans, cross, *refs):
    n = len(spans)
    w_refs, (leaf_ref, v_ref), near_out = refs[:n], refs[n : n + 2], refs[n + 2]
    sum_refs, p_refs = refs[n + 3 : 2 * n + 3], refs[2 * n + 3 :]
    size = leaf_ref.shape[1]
    near = p_refs[0].shape[2]
    for i, span in enumerate(spans):
        for j, c in enumerate(leaves_of(span, size)):
            columns = slice(j * size, (j + 1) * size)
            turned = v_ref[cross:, :, c * size : (c + 1) * size].reshape(near, size).T
            group = near_out.shape[2] // near
            near_out[c // group, :, c % group * near : (c % group + 1) * near] = turned
            p_refs[i][j] = dot(w_refs[i][:, columns], turned)
            sum_refs[i][:, columns] = dot(w_refs[i][:, columns], leaf_ref[c])


def first_part(spans, cross, w, leaf, v):
    levels, rank, width = v.shape
    size = leaf.shape[1]
    rows = w[0].shape[0]
    near = (levels - cross) * rank
    group = 2 if all((stop - start) // size % 2 == 0 for start, stop in spans) else 1
    outs = [pltpu.VMEM((width // size // group, size, group * near), v.dtype)]
    outs += [pltpu.VMEM(x.shape, jnp.float32) for x in w]
    outs += [pltpu.VMEM((x.shape[1] // size, rows, near), jnp.float32) for x in w]
    n = len(w)
    found = call(functools.partial(first_kernel, spans, cross), outs, [*w, leaf, v])
    return found[0], list(found[1 : 1 + n]), list(found[1 + n :])


def nearby_kernel(rank, levels_of, front_ref, v_ref, *refs):
    part_refs, p_ref = refs[: len(levels_of)], refs[-1]
    term = dot(front_ref[...], v_ref[...], ROWS_TIMES_ROWS)
    rows, ranks = p_ref.shape
    before = ranks - term.shape[1]
    if before:
        term = jnp.concatenate([jnp.zeros((rows, before), jnp.float32), term], axis=1)
    lane = lax.broadcasted_iota(jnp.int32, (rows, ranks), 1) // rank
    for ref, level in zip(part_refs, levels_of):
        term = term + jnp.where(lane == level, ref[...].astype(jnp.float32), 0.0)
    p_ref[...] = term.astype(p_ref.dtype)


def nearby_part(rank, front, v, ranks, parts, levels_of, behind, flops=0):
    outs = [pltpu.VMEM((front.shape[0], ranks), jnp.bfloat16)]
    return call(functools.partial(nearby_kernel, rank, tuple(levels_of)), outs, [front, v, *parts, *behind], flops=flops)[0]


def near_kernel(span, start, w_ref, front_ref, leaf_ref, v_ref, *refs):
    w_out, sum_out, p_out = refs[-3:]
    size = leaf_ref.shape[1]
    rows = w_ref.shape[0]
    near = p_out.shape[2]
    group = v_ref.shape[2] // near
    members = []
    for j, c in enumerate(leaves_of(span, size)):
        columns = slice(j * size, (j + 1) * size)
        w = w_ref[:, columns] + front_ref[:, start + j * size : start + (j + 1) * size]
        w_out[:, columns] = w
        members.append(w)
        if len(members) == group:
            both = dot(jnp.concatenate(members, axis=0), v_ref[c // group])
            for i in range(group):
                p_out[j - group + 1 + i] = both[i * rows : (i + 1) * rows, i * near : (i + 1) * near]
            members = []
        sum_out[:, columns] = dot(w, leaf_ref[c])


def near_part(span, start, near, w, front, leaf, near_v, behind):
    outs = [
        pltpu.VMEM(w.shape, w.dtype),
        pltpu.VMEM(w.shape, jnp.float32),
        pltpu.VMEM((w.shape[1] // leaf.shape[1], w.shape[0], near), jnp.float32),
    ]
    return call(functools.partial(near_kernel, span, start), outs, [w, front, leaf, near_v, *behind], {0: 0})


def far_kernel(rank, size, spans, chosen, levels_of, *refs):
    refs = list(refs)
    sum_refs = [refs.pop(0) for _ in chosen]
    p_refs = [refs.pop(0) for _ in spans]
    q_ref = refs.pop(0)
    part_refs = [refs.pop(0) for _ in levels_of]
    u_ref = refs.pop(0)
    out_ref, q_out = refs[:2]
    rows, far = q_ref.shape
    near = u_ref.shape[0] - far

    q = q_ref[...]
    lane = lax.broadcasted_iota(jnp.int32, (rows, far), 1) // rank
    for ref, level in zip(part_refs, levels_of):
        part = ref[...].astype(jnp.float32)
        q = q + (part if level is None else jnp.where(lane == level, part, 0.0))
    q_out[...] = q

    projected = [ref[j] for ref in p_refs for j in range(ref.shape[0])]
    nleaf = len(projected)
    lane = lax.broadcasted_iota(jnp.int32, (rows, near), 1) // rank
    sums = []
    for level in range(near // rank):
        block = nleaf >> (level + 1)
        sums.append(
            [
                functools.reduce(jnp.add, projected[b * block : (b + 1) * block])
                for b in range(nleaf // block)
            ]
        )
    place = 0
    for i, ref in zip(chosen, sum_refs):
        for j, c in enumerate(leaves_of(spans[i], size)):
            swapped = sums[0][(c // (nleaf >> 1)) ^ 1]
            for level in range(1, near // rank):
                swapped = jnp.where(lane == level, sums[level][(c // (nleaf >> (level + 1))) ^ 1], swapped)
            columns = slice(c * size, (c + 1) * size)
            value = ref[:, j * size : (j + 1) * size]
            value = value + dot(q.astype(jnp.bfloat16), u_ref[:far, columns])
            value = value + dot(swapped.astype(jnp.bfloat16), u_ref[far:, columns])
            out_ref[:, place : place + size] = value.astype(jnp.bfloat16)
            place += size


def far_part(rank, size, spans, chosen, sums, projected, q, parts, levels_of, u, last):
    args = [*[sums[i] for i in chosen], *projected, q, *parts, u]
    width = sum(sums[i].shape[1] for i in chosen)
    space = jax.ShapeDtypeStruct if last else pltpu.VMEM
    outs = [space((q.shape[0], width), jnp.bfloat16), pltpu.VMEM(q.shape, jnp.float32)]
    kernel = functools.partial(far_kernel, rank, size, spans, chosen, tuple(levels_of) if parts else ())
    return call(kernel, outs, args, {len(chosen) + len(projected): 1})


def local(sources, leaves, v_rows, u_rows):
    devices = lax.axis_size("hodlr")
    chain = lax.axis_size("slab")
    cross = devices.bit_length() - 1
    source, right = sources[0], v_rows[0]
    levels, rank, width = right.shape
    nleaf, size = leaves.shape[1:3]
    cut = max(nleaf * FIRST_SHARE // 4, 1) * size
    spans = ((0, cut), (cut, width))
    offsets = list(range(1, devices))
    levels_of = [cross - x.bit_length() for x in offsets]

    def moved(x, moves, offset=0):
        route = [(a * devices + h, b * devices + (h ^ offset)) for a, b in moves for h in range(devices)]
        return lax.ppermute(x, ("slab", "hodlr"), route)

    def exchanged(p, moves):
        return [moved(p, moves, x) for x in offsets]

    later = [(k, k - 1) for k in range(IN_PLACE + 1, chain)]
    early = moved(fetch_ahead(cross, right), [(1, 0)] + later)
    (coarse_v, fine_v), w = fetch(spans, cross, source, right)
    coarse = moved(coarse_v, later)
    ranks = cross * rank
    whole = ((0, width),)
    p = project(spans, w, [coarse_v, fine_v], ranks, OPEN_FLOPS)
    parts = exchanged(p, [(k, k) for k in range(chain)])
    leaf, u = leaves[0], u_rows[0].reshape(levels * rank, width)
    near_v, sums, projected = first_part(spans, cross, w, leaf, right)

    q = jnp.zeros(p.shape, jnp.float32)
    every = tuple(range(len(spans)))
    far = functools.partial(far_part, rank, size, spans)
    out, q = far(every, sums, projected, q, parts, levels_of, u, False)
    front = [moved(out, [(0, 1)])]
    ahead = [project(whole, [out], [early], ranks)]
    relayed = offsets[1::2]
    parts = [moved(ahead[0], [(0, 1)], x) for x in relayed]
    second = moved(put_behind(coarse_v, ahead[0]), [(2, 1)])
    levels_relayed = [cross - x.bit_length() for x in relayed]
    for k in range(1, chain):
        levels_now = levels_of[::-1]
        for i, span in enumerate(spans):
            behind = projected[i - 1 : i] if i else ahead if k == 1 else []
            if i == 1 and k <= IN_PLACE:
                if k == IN_PLACE:
                    turned = turn(size, [coarse, early[-rank:]])
                nearby = nearby_part(
                    rank,
                    front[0],
                    fine_v,
                    ranks,
                    parts,
                    levels_relayed,
                    behind + (ahead if k == 1 else [turned]),
                    OPEN_FLOPS,
                )
                parts = [moved(nearby, [(k, k)], offsets[0])] + parts
                levels_now = [None] + levels_relayed
                behind = [nearby]
            given, start = (front[0], span[0]) if len(front) == 1 else (front[i], 0)
            w[i], sums[i], projected[i] = near_part(span, start, (levels - cross) * rank, w[i], given, leaf, near_v, behind)
        if k == chain - 1:
            out, _ = far(every, sums, projected, q, parts, levels_now, u, True)
            return out[None]
        split = k >= IN_PLACE and k != WHOLE_HOP
        outs, front = [], []
        for chosen in [(i,) for i in every] if split else [every]:
            out, q = far(chosen, sums, projected, q, [] if front else parts, levels_now, u, False)
            outs.append(out)
            front.append(moved(out, [(k, k + 1)]))
        if k < IN_PLACE:
            p = project(whole, outs, [second], ranks)
        else:
            p = project_turned(spans if split else whole, outs, turned)
        sent = relayed if k < IN_PLACE else offsets[::-1]
        parts = [moved(p, [(k, k + 1)], x) for x in sent]


def solution(mesh):
    in_specs = (
        P("slab", None, "hodlr"),
        P("slab", "hodlr", None, None),
        P("slab", None, None, "hodlr"),
        P("slab", None, None, "hodlr"),
    )
    out_specs = P("slab", None, "hodlr")
    return jax.shard_map(local, mesh=mesh, in_specs=in_specs, out_specs=out_specs, check_vma=False)
```

```python
import functools

import jax
import jax.numpy as jnp
from jax import lax
from jax.experimental import pallas as pl
from jax.experimental.pallas import tpu as pltpu
from jax.sharding import PartitionSpec as P

VMEM_LIMIT = 24 * 1024 * 1024
FIRST_SHARE = 2
IN_PLACE = 2
WHOLE_HOP = 3
OPEN_FLOPS = 4 * 10**9
ROWS_TIMES_COLUMNS = (((1,), (0,)), ((), ()))
ROWS_TIMES_ROWS = (((1,), (1,)), ((), ()))


def dot(a, b, dims=ROWS_TIMES_COLUMNS):
    return lax.dot_general(a, b, dims, preferred_element_type=jnp.float32)


def call(kernel, outs, args, aliases=None, scratch=(), from_hbm=(), flops=0):
    whole = pl.BlockSpec(memory_space=pltpu.VMEM)
    remote = pl.BlockSpec(memory_space=pl.ANY)
    placed = [
        pltpu.with_memory_space_constraint(a, pltpu.HBM if i in from_hbm else pltpu.VMEM)
        for i, a in enumerate(args)
    ]
    return pl.pallas_call(
        kernel,
        out_shape=outs,
        in_specs=[remote if i in from_hbm else whole for i in range(len(args))],
        out_specs=[whole] * len(outs),
        scratch_shapes=scratch,
        input_output_aliases=aliases or {},
        compiler_params=pltpu.CompilerParams(vmem_limit_bytes=VMEM_LIMIT),
        cost_estimate=pl.CostEstimate(flops=flops, bytes_accessed=0, transcendentals=0),
    )(*placed)


def on_factors(value, v_refs, columns, ranks):
    pieces = [dot(value, ref[:, columns], ROWS_TIMES_ROWS) for ref in v_refs]
    missing = ranks - sum(ref.shape[0] for ref in v_refs)
    if missing:
        pieces.append(jnp.zeros((value.shape[0], missing), jnp.float32))
    return jnp.concatenate(pieces, axis=1)


def ahead_kernel(v_ref, out_ref, sem):
    first = jnp.where(lax.axis_index("slab") == 1, 0, 1)
    copy = pltpu.make_async_copy(v_ref.at[pl.ds(first, out_ref.shape[0])], out_ref, sem)
    copy.start()
    copy.wait()


def fetch_ahead(cross, v):
    _, rank, width = v.shape
    outs = [pltpu.VMEM((cross - 1, rank, width), v.dtype)]
    found = call(ahead_kernel, outs, [v], scratch=[pltpu.SemaphoreType.DMA], from_hbm=(0,))
    return found[0].reshape(-1, width)


def fetch_kernel(spans, source_ref, v_ref, *refs):
    v_outs, w_outs, sems = refs[: -1 - len(spans)], refs[-1 - len(spans) : -1], refs[-1]
    copies, level = [], 0
    for out in v_outs:
        copies.append((v_ref.at[pl.ds(level, out.shape[0])], out))
        level += out.shape[0]
    for out, (start, stop) in zip(w_outs, spans):
        copies.append((source_ref.at[:, pl.ds(start, stop - start)], out))
    copies = [pltpu.make_async_copy(a, b, sems.at[i]) for i, (a, b) in enumerate(copies)]
    for copy in copies:
        copy.start()
    for copy in copies:
        copy.wait()


def fetch(spans, cross, source, v):
    _, rank, width = v.shape
    shares = (cross - 1, 1)
    outs = [pltpu.VMEM((n, rank, width), v.dtype) for n in shares]
    outs += [pltpu.VMEM((source.shape[0], stop - start), source.dtype) for start, stop in spans]
    found = call(
        functools.partial(fetch_kernel, spans),
        outs,
        [source, v],
        scratch=[pltpu.SemaphoreType.DMA((len(outs),))],
        from_hbm=(0, 1),
    )
    return [f.reshape(-1, width) for f in found[: len(shares)]], list(found[len(shares) :])


def behind_kernel(x_ref, other_ref, out_ref):
    out_ref[...] = x_ref[...]


def put_behind(x, other):
    return call(behind_kernel, [pltpu.VMEM(x.shape, x.dtype)], [x, other], flops=OPEN_FLOPS)[0]


def project_kernel(spans, factors, *refs):
    v_refs, parts, p_ref = refs[:factors], refs[factors:-1], refs[-1]
    total = None
    for ref, (start, stop) in zip(parts, spans):
        term = on_factors(ref[...], v_refs, slice(start, stop), p_ref.shape[1])
        total = term if total is None else total + term
    p_ref[...] = total.astype(p_ref.dtype)


def project(spans, w, far_v, ranks, flops=0):
    outs = [pltpu.VMEM((w[0].shape[0], ranks), jnp.bfloat16)]
    return call(functools.partial(project_kernel, spans, len(far_v)), outs, [*far_v, *w], flops=flops)[0]


def turn_kernel(size, *refs):
    v_refs, out_ref = refs[:-1], refs[-1]
    for c in range(out_ref.shape[0] // size):
        rows = slice(c * size, (c + 1) * size)
        out_ref[rows, :] = jnp.concatenate([ref[:, rows] for ref in v_refs], axis=0).T


def turn(size, v):
    outs = [pltpu.VMEM((v[0].shape[1], sum(x.shape[0] for x in v)), v[0].dtype)]
    return call(functools.partial(turn_kernel, size), outs, v)[0]


def project_turned_kernel(spans, v_ref, *refs):
    parts, p_ref = refs[:-1], refs[-1]
    total = None
    for ref, (start, stop) in zip(parts, spans):
        term = dot(ref[...], v_ref[start:stop, :])
        total = term if total is None else total + term
    p_ref[...] = total.astype(p_ref.dtype)


def project_turned(spans, w, v):
    outs = [pltpu.VMEM((w[0].shape[0], v.shape[1]), jnp.bfloat16)]
    return call(functools.partial(project_turned_kernel, spans), outs, [v, *w])[0]


def leaves_of(span, size):
    return range(span[0] // size, span[1] // size)


def first_kernel(spans, cross, *refs):
    n = len(spans)
    w_refs, (leaf_ref, v_ref), near_out = refs[:n], refs[n : n + 2], refs[n + 2]
    sum_refs, p_refs = refs[n + 3 : 2 * n + 3], refs[2 * n + 3 :]
    size = leaf_ref.shape[1]
    near = p_refs[0].shape[2]
    for i, span in enumerate(spans):
        for j, c in enumerate(leaves_of(span, size)):
            columns = slice(j * size, (j + 1) * size)
            turned = v_ref[cross:, :, c * size : (c + 1) * size].reshape(near, size).T
            group = near_out.shape[2] // near
            near_out[c // group, :, c % group * near : (c % group + 1) * near] = turned
            p_refs[i][j] = dot(w_refs[i][:, columns], turned)
            sum_refs[i][:, columns] = dot(w_refs[i][:, columns], leaf_ref[c])


def first_part(spans, cross, w, leaf, v):
    levels, rank, width = v.shape
    size = leaf.shape[1]
    rows = w[0].shape[0]
    near = (levels - cross) * rank
    group = 2 if all((stop - start) // size % 2 == 0 for start, stop in spans) else 1
    outs = [pltpu.VMEM((width // size // group, size, group * near), v.dtype)]
    outs += [pltpu.VMEM(x.shape, jnp.float32) for x in w]
    outs += [pltpu.VMEM((x.shape[1] // size, rows, near), jnp.float32) for x in w]
    n = len(w)
    found = call(functools.partial(first_kernel, spans, cross), outs, [*w, leaf, v])
    return found[0], list(found[1 : 1 + n]), list(found[1 + n :])


def nearby_kernel(rank, levels_of, front_ref, v_ref, *refs):
    part_refs, p_ref = refs[: len(levels_of)], refs[-1]
    term = dot(front_ref[...], v_ref[...], ROWS_TIMES_ROWS)
    rows, ranks = p_ref.shape
    before = ranks - term.shape[1]
    if before:
        term = jnp.concatenate([jnp.zeros((rows, before), jnp.float32), term], axis=1)
    lane = lax.broadcasted_iota(jnp.int32, (rows, ranks), 1) // rank
    for ref, level in zip(part_refs, levels_of):
        term = term + jnp.where(lane == level, ref[...].astype(jnp.float32), 0.0)
    p_ref[...] = term.astype(p_ref.dtype)


def nearby_part(rank, front, v, ranks, parts, levels_of, behind, flops=0):
    outs = [pltpu.VMEM((front.shape[0], ranks), jnp.bfloat16)]
    return call(functools.partial(nearby_kernel, rank, tuple(levels_of)), outs, [front, v, *parts, *behind], flops=flops)[0]


def near_kernel(span, start, w_ref, front_ref, leaf_ref, v_ref, *refs):
    w_out, sum_out, p_out = refs[-3:]
    size = leaf_ref.shape[1]
    rows = w_ref.shape[0]
    near = p_out.shape[2]
    group = v_ref.shape[2] // near
    members = []
    for j, c in enumerate(leaves_of(span, size)):
        columns = slice(j * size, (j + 1) * size)
        w = w_ref[:, columns] + front_ref[:, start + j * size : start + (j + 1) * size]
        w_out[:, columns] = w
        members.append(w)
        if len(members) == group:
            both = dot(jnp.concatenate(members, axis=0), v_ref[c // group])
            for i in range(group):
                p_out[j - group + 1 + i] = both[i * rows : (i + 1) * rows, i * near : (i + 1) * near]
            members = []
        sum_out[:, columns] = dot(w, leaf_ref[c])


def near_part(span, start, near, w, front, leaf, near_v, behind):
    outs = [
        pltpu.VMEM(w.shape, w.dtype),
        pltpu.VMEM(w.shape, jnp.float32),
        pltpu.VMEM((w.shape[1] // leaf.shape[1], w.shape[0], near), jnp.float32),
    ]
    return call(functools.partial(near_kernel, span, start), outs, [w, front, leaf, near_v, *behind], {0: 0})


def far_kernel(rank, size, spans, chosen, levels_of, *refs):
    refs = list(refs)
    sum_refs = [refs.pop(0) for _ in chosen]
    p_refs = [refs.pop(0) for _ in spans]
    q_ref = refs.pop(0)
    part_refs = [refs.pop(0) for _ in levels_of]
    u_ref = refs.pop(0)
    out_ref, q_out = refs[:2]
    rows, far = q_ref.shape
    near = u_ref.shape[0] - far

    q = q_ref[...]
    lane = lax.broadcasted_iota(jnp.int32, (rows, far), 1) // rank
    for ref, level in zip(part_refs, levels_of):
        part = ref[...].astype(jnp.float32)
        q = q + (part if level is None else jnp.where(lane == level, part, 0.0))
    q_out[...] = q

    projected = [ref[j] for ref in p_refs for j in range(ref.shape[0])]
    nleaf = len(projected)
    lane = lax.broadcasted_iota(jnp.int32, (rows, near), 1) // rank
    sums = []
    for level in range(near // rank):
        block = nleaf >> (level + 1)
        sums.append(
            [
                functools.reduce(jnp.add, projected[b * block : (b + 1) * block])
                for b in range(nleaf // block)
            ]
        )
    place = 0
    for i, ref in zip(chosen, sum_refs):
        for j, c in enumerate(leaves_of(spans[i], size)):
            swapped = sums[0][(c // (nleaf >> 1)) ^ 1]
            for level in range(1, near // rank):
                swapped = jnp.where(lane == level, sums[level][(c // (nleaf >> (level + 1))) ^ 1], swapped)
            columns = slice(c * size, (c + 1) * size)
            value = ref[:, j * size : (j + 1) * size]
            value = value + dot(q.astype(jnp.bfloat16), u_ref[:far, columns])
            value = value + dot(swapped.astype(jnp.bfloat16), u_ref[far:, columns])
            out_ref[:, place : place + size] = value.astype(jnp.bfloat16)
            place += size


def far_part(rank, size, spans, chosen, sums, projected, q, parts, levels_of, u, last):
    args = [*[sums[i] for i in chosen], *projected, q, *parts, u]
    width = sum(sums[i].shape[1] for i in chosen)
    space = jax.ShapeDtypeStruct if last else pltpu.VMEM
    outs = [space((q.shape[0], width), jnp.bfloat16), pltpu.VMEM(q.shape, jnp.float32)]
    kernel = functools.partial(far_kernel, rank, size, spans, chosen, tuple(levels_of) if parts else ())
    return call(kernel, outs, args, {len(chosen) + len(projected): 1})


def local(sources, leaves, v_rows, u_rows):
    devices = lax.axis_size("hodlr")
    chain = lax.axis_size("slab")
    cross = devices.bit_length() - 1
    source, right = sources[0], v_rows[0]
    levels, rank, width = right.shape
    nleaf, size = leaves.shape[1:3]
    cut = max(nleaf * FIRST_SHARE // 4, 1) * size
    spans = ((0, cut), (cut, width))
    offsets = list(range(1, devices))
    levels_of = [cross - x.bit_length() for x in offsets]

    def moved(x, moves, offset=0):
        route = [(a * devices + h, b * devices + (h ^ offset)) for a, b in moves for h in range(devices)]
        return lax.ppermute(x, ("slab", "hodlr"), route)

    def exchanged(p, moves):
        return [moved(p, moves, x) for x in offsets]

    later = [(k, k - 1) for k in range(IN_PLACE + 1, chain)]
    early = moved(fetch_ahead(cross, right), [(1, 0)] + later)
    (coarse_v, fine_v), w = fetch(spans, cross, source, right)
    coarse = moved(coarse_v, later)
    ranks = cross * rank
    whole = ((0, width),)
    p = project(spans, w, [coarse_v, fine_v], ranks, OPEN_FLOPS)
    parts = exchanged(p, [(k, k) for k in range(chain)])
    leaf, u = leaves[0], u_rows[0].reshape(levels * rank, width)
    near_v, sums, projected = first_part(spans, cross, w, leaf, right)

    q = jnp.zeros(p.shape, jnp.float32)
    every = tuple(range(len(spans)))
    far = functools.partial(far_part, rank, size, spans)
    out, q = far(every, sums, projected, q, parts, levels_of, u, False)
    front = [moved(out, [(0, 1)])]
    ahead = [project(whole, [out], [early], ranks)]
    relayed = offsets[1::2]
    parts = [moved(ahead[0], [(0, 1)], x) for x in relayed]
    second = moved(put_behind(coarse_v, front[0]), [(2, 1)])
    levels_relayed = [cross - x.bit_length() for x in relayed]
    for k in range(1, chain):
        levels_now = levels_of[::-1]
        for i, span in enumerate(spans):
            behind = projected[i - 1 : i] if i else ahead if k == 1 else []
            if i == 1 and k <= IN_PLACE:
                if k == IN_PLACE:
                    turned = turn(size, [coarse, early[-rank:]])
                nearby = nearby_part(
                    rank,
                    front[0],
                    fine_v,
                    ranks,
                    parts,
                    levels_relayed,
                    behind + (ahead if k == 1 else [turned]),
                    OPEN_FLOPS,
                )
                parts = [moved(nearby, [(k, k)], offsets[0])] + parts
                levels_now = [None] + levels_relayed
                behind = [nearby]
            given, start = (front[0], span[0]) if len(front) == 1 else (front[i], 0)
            w[i], sums[i], projected[i] = near_part(span, start, (levels - cross) * rank, w[i], given, leaf, near_v, behind)
        if k == chain - 1:
            out, _ = far(every, sums, projected, q, parts, levels_now, u, True)
            return out[None]
        split = k >= IN_PLACE and k != WHOLE_HOP
        outs, front = [], []
        for chosen in [(i,) for i in every] if split else [every]:
            out, q = far(chosen, sums, projected, q, [] if front else parts, levels_now, u, False)
            outs.append(out)
            front.append(moved(out, [(k, k + 1)]))
        if k < IN_PLACE:
            p = project(whole, outs, [second], ranks)
        else:
            p = project_turned(spans if split else whole, outs, turned)
        sent = relayed if k < IN_PLACE else offsets[::-1]
        parts = [moved(p, [(k, k + 1)], x) for x in sent]


def solution(mesh):
    in_specs = (
        P("slab", None, "hodlr"),
        P("slab", "hodlr", None, None),
        P("slab", None, None, "hodlr"),
        P("slab", None, None, "hodlr"),
    )
    out_specs = P("slab", None, "hodlr")
    return jax.shard_map(local, mesh=mesh, in_specs=in_specs, out_specs=out_specs, check_vma=False)
```

```python
import functools

import jax
import jax.numpy as jnp
from jax import lax
from jax.experimental import pallas as pl
from jax.experimental.pallas import tpu as pltpu
from jax.sharding import PartitionSpec as P

VMEM_LIMIT = 24 * 1024 * 1024
FIRST_SHARE = 2
IN_PLACE = 2
WHOLE_HOP = 3
OPEN_FLOPS = 4 * 10**9
ROWS_TIMES_COLUMNS = (((1,), (0,)), ((), ()))
ROWS_TIMES_ROWS = (((1,), (1,)), ((), ()))


def dot(a, b, dims=ROWS_TIMES_COLUMNS):
    return lax.dot_general(a, b, dims, preferred_element_type=jnp.float32)


def call(kernel, outs, args, aliases=None, scratch=(), from_hbm=(), flops=0):
    whole = pl.BlockSpec(memory_space=pltpu.VMEM)
    remote = pl.BlockSpec(memory_space=pl.ANY)
    placed = [
        pltpu.with_memory_space_constraint(a, pltpu.HBM if i in from_hbm else pltpu.VMEM)
        for i, a in enumerate(args)
    ]
    return pl.pallas_call(
        kernel,
        out_shape=outs,
        in_specs=[remote if i in from_hbm else whole for i in range(len(args))],
        out_specs=[whole] * len(outs),
        scratch_shapes=scratch,
        input_output_aliases=aliases or {},
        compiler_params=pltpu.CompilerParams(vmem_limit_bytes=VMEM_LIMIT),
        cost_estimate=pl.CostEstimate(flops=flops, bytes_accessed=0, transcendentals=0),
    )(*placed)


def on_factors(value, v_refs, columns, ranks):
    pieces = [dot(value, ref[:, columns], ROWS_TIMES_ROWS) for ref in v_refs]
    missing = ranks - sum(ref.shape[0] for ref in v_refs)
    if missing:
        pieces.append(jnp.zeros((value.shape[0], missing), jnp.float32))
    return jnp.concatenate(pieces, axis=1)


def fetch_kernel(spans, source_ref, v_ref, *refs):
    v_outs, w_outs, sems = refs[: -1 - len(spans)], refs[-1 - len(spans) : -1], refs[-1]
    copies, level = [], 0
    for out in v_outs[:-1]:
        copies.append((v_ref.at[pl.ds(level, out.shape[0])], out))
        level += out.shape[0]
    first = jnp.where(lax.axis_index("slab") == 1, 0, 1)
    copies.append((v_ref.at[pl.ds(first, v_outs[-1].shape[0])], v_outs[-1]))
    for out, (start, stop) in zip(w_outs, spans):
        copies.append((source_ref.at[:, pl.ds(start, stop - start)], out))
    copies = [pltpu.make_async_copy(a, b, sems.at[i]) for i, (a, b) in enumerate(copies)]
    for copy in copies:
        copy.start()
    for copy in copies:
        copy.wait()


def fetch(spans, cross, source, v):
    _, rank, width = v.shape
    shares = (cross - 1, 1, cross - 1)
    outs = [pltpu.VMEM((n, rank, width), v.dtype) for n in shares]
    outs += [pltpu.VMEM((source.shape[0], stop - start), source.dtype) for start, stop in spans]
    found = call(
        functools.partial(fetch_kernel, spans),
        outs,
        [source, v],
        scratch=[pltpu.SemaphoreType.DMA((len(outs),))],
        from_hbm=(0, 1),
    )
    return [f.reshape(-1, width) for f in found[: len(shares)]], list(found[len(shares) :])


def turn_near_kernel(cross, near, x_ref, v_ref, other_ref, x_out, near_out):
    size = near_out.shape[1]
    group = near_out.shape[2] // near
    for c in range(near_out.shape[0] * group):
        turned = v_ref[cross:, :, c * size : (c + 1) * size].reshape(near, size).T
        near_out[c // group, :, c % group * near : (c % group + 1) * near] = turned
    x_out[...] = x_ref[...]


def turn_near(spans, cross, size, x, v, other):
    levels, rank, width = v.shape
    near = (levels - cross) * rank
    group = 2 if all((stop - start) // size % 2 == 0 for start, stop in spans) else 1
    outs = [pltpu.VMEM(x.shape, x.dtype), pltpu.VMEM((width // size // group, size, group * near), v.dtype)]
    return call(functools.partial(turn_near_kernel, cross, near), outs, [x, v, other], flops=OPEN_FLOPS)


def project_kernel(spans, factors, *refs):
    v_refs, parts, p_ref = refs[:factors], refs[factors:-1], refs[-1]
    total = None
    for ref, (start, stop) in zip(parts, spans):
        term = on_factors(ref[...], v_refs, slice(start, stop), p_ref.shape[1])
        total = term if total is None else total + term
    p_ref[...] = total.astype(p_ref.dtype)


def project(spans, w, far_v, ranks, flops=0):
    outs = [pltpu.VMEM((w[0].shape[0], ranks), jnp.bfloat16)]
    return call(functools.partial(project_kernel, spans, len(far_v)), outs, [*far_v, *w], flops=flops)[0]


def turn_kernel(size, *refs):
    v_refs, out_ref = refs[:-1], refs[-1]
    for c in range(out_ref.shape[0] // size):
        rows = slice(c * size, (c + 1) * size)
        out_ref[rows, :] = jnp.concatenate([ref[:, rows] for ref in v_refs], axis=0).T


def turn(size, v):
    outs = [pltpu.VMEM((v[0].shape[1], sum(x.shape[0] for x in v)), v[0].dtype)]
    return call(functools.partial(turn_kernel, size), outs, v)[0]


def project_turned_kernel(spans, v_ref, *refs):
    parts, p_ref = refs[:-1], refs[-1]
    total = None
    for ref, (start, stop) in zip(parts, spans):
        term = dot(ref[...], v_ref[start:stop, :])
        total = term if total is None else total + term
    p_ref[...] = total.astype(p_ref.dtype)


def project_turned(spans, w, v):
    outs = [pltpu.VMEM((w[0].shape[0], v.shape[1]), jnp.bfloat16)]
    return call(functools.partial(project_turned_kernel, spans), outs, [v, *w])[0]


def leaves_of(span, size):
    return range(span[0] // size, span[1] // size)


def first_kernel(spans, cross, *refs):
    n = len(spans)
    w_refs, (leaf_ref, v_ref) = refs[:n], refs[n : n + 2]
    sum_refs, p_refs = refs[n + 2 : 2 * n + 2], refs[2 * n + 2 :]
    size = leaf_ref.shape[1]
    near = p_refs[0].shape[2]
    for i, span in enumerate(spans):
        for j, c in enumerate(leaves_of(span, size)):
            columns = slice(j * size, (j + 1) * size)
            rows = v_ref[cross:, :, c * size : (c + 1) * size].reshape(near, size)
            p_refs[i][j] = dot(w_refs[i][:, columns], rows, ROWS_TIMES_ROWS)
            sum_refs[i][:, columns] = dot(w_refs[i][:, columns], leaf_ref[c])


def first_part(spans, cross, w, leaf, v):
    levels, rank, width = v.shape
    size = leaf.shape[1]
    rows = w[0].shape[0]
    near = (levels - cross) * rank
    outs = [pltpu.VMEM(x.shape, jnp.float32) for x in w]
    outs += [pltpu.VMEM((x.shape[1] // size, rows, near), jnp.float32) for x in w]
    n = len(w)
    found = call(functools.partial(first_kernel, spans, cross), outs, [*w, leaf, v])
    return list(found[:n]), list(found[n:])


def nearby_kernel(rank, levels_of, front_ref, v_ref, *refs):
    part_refs, p_ref = refs[: len(levels_of)], refs[-1]
    term = dot(front_ref[...], v_ref[...], ROWS_TIMES_ROWS)
    rows, ranks = p_ref.shape
    before = ranks - term.shape[1]
    if before:
        term = jnp.concatenate([jnp.zeros((rows, before), jnp.float32), term], axis=1)
    lane = lax.broadcasted_iota(jnp.int32, (rows, ranks), 1) // rank
    for ref, level in zip(part_refs, levels_of):
        term = term + jnp.where(lane == level, ref[...].astype(jnp.float32), 0.0)
    p_ref[...] = term.astype(p_ref.dtype)


def nearby_part(rank, front, v, ranks, parts, levels_of, behind, flops=0):
    outs = [pltpu.VMEM((front.shape[0], ranks), jnp.bfloat16)]
    return call(functools.partial(nearby_kernel, rank, tuple(levels_of)), outs, [front, v, *parts, *behind], flops=flops)[0]


def near_kernel(span, start, w_ref, front_ref, leaf_ref, v_ref, *refs):
    w_out, sum_out, p_out = refs[-3:]
    size = leaf_ref.shape[1]
    rows = w_ref.shape[0]
    near = p_out.shape[2]
    group = v_ref.shape[2] // near
    members = []
    for j, c in enumerate(leaves_of(span, size)):
        columns = slice(j * size, (j + 1) * size)
        w = w_ref[:, columns] + front_ref[:, start + j * size : start + (j + 1) * size]
        w_out[:, columns] = w
        members.append(w)
        if len(members) == group:
            both = dot(jnp.concatenate(members, axis=0), v_ref[c // group])
            for i in range(group):
                p_out[j - group + 1 + i] = both[i * rows : (i + 1) * rows, i * near : (i + 1) * near]
            members = []
        sum_out[:, columns] = dot(w, leaf_ref[c])


def near_part(span, start, near, w, front, leaf, near_v, behind):
    outs = [
        pltpu.VMEM(w.shape, w.dtype),
        pltpu.VMEM(w.shape, jnp.float32),
        pltpu.VMEM((w.shape[1] // leaf.shape[1], w.shape[0], near), jnp.float32),
    ]
    return call(functools.partial(near_kernel, span, start), outs, [w, front, leaf, near_v, *behind], {0: 0})


def far_kernel(rank, size, spans, chosen, levels_of, *refs):
    refs = list(refs)
    sum_refs = [refs.pop(0) for _ in chosen]
    p_refs = [refs.pop(0) for _ in spans]
    q_ref = refs.pop(0)
    part_refs = [refs.pop(0) for _ in levels_of]
    u_ref = refs.pop(0)
    out_ref, q_out = refs[:2]
    rows, far = q_ref.shape
    near = u_ref.shape[0] - far

    q = q_ref[...]
    lane = lax.broadcasted_iota(jnp.int32, (rows, far), 1) // rank
    for ref, level in zip(part_refs, levels_of):
        part = ref[...].astype(jnp.float32)
        q = q + (part if level is None else jnp.where(lane == level, part, 0.0))
    q_out[...] = q

    projected = [ref[j] for ref in p_refs for j in range(ref.shape[0])]
    nleaf = len(projected)
    lane = lax.broadcasted_iota(jnp.int32, (rows, near), 1) // rank
    sums = []
    for level in range(near // rank):
        block = nleaf >> (level + 1)
        sums.append(
            [
                functools.reduce(jnp.add, projected[b * block : (b + 1) * block])
                for b in range(nleaf // block)
            ]
        )
    place = 0
    for i, ref in zip(chosen, sum_refs):
        for j, c in enumerate(leaves_of(spans[i], size)):
            swapped = sums[0][(c // (nleaf >> 1)) ^ 1]
            for level in range(1, near // rank):
                swapped = jnp.where(lane == level, sums[level][(c // (nleaf >> (level + 1))) ^ 1], swapped)
            columns = slice(c * size, (c + 1) * size)
            value = ref[:, j * size : (j + 1) * size]
            value = value + dot(q.astype(jnp.bfloat16), u_ref[:far, columns])
            value = value + dot(swapped.astype(jnp.bfloat16), u_ref[far:, columns])
            out_ref[:, place : place + size] = value.astype(jnp.bfloat16)
            place += size


def far_part(rank, size, spans, chosen, sums, projected, q, parts, levels_of, u, last):
    args = [*[sums[i] for i in chosen], *projected, q, *parts, u]
    width = sum(sums[i].shape[1] for i in chosen)
    space = jax.ShapeDtypeStruct if last else pltpu.VMEM
    outs = [space((q.shape[0], width), jnp.bfloat16), pltpu.VMEM(q.shape, jnp.float32)]
    kernel = functools.partial(far_kernel, rank, size, spans, chosen, tuple(levels_of) if parts else ())
    return call(kernel, outs, args, {len(chosen) + len(projected): 1})


def local(sources, leaves, v_rows, u_rows):
    devices = lax.axis_size("hodlr")
    chain = lax.axis_size("slab")
    cross = devices.bit_length() - 1
    source, right = sources[0], v_rows[0]
    levels, rank, width = right.shape
    nleaf, size = leaves.shape[1:3]
    cut = max(nleaf * FIRST_SHARE // 4, 1) * size
    spans = ((0, cut), (cut, width))
    offsets = list(range(1, devices))
    levels_of = [cross - x.bit_length() for x in offsets]

    def moved(x, moves, offset=0):
        route = [(a * devices + h, b * devices + (h ^ offset)) for a, b in moves for h in range(devices)]
        return lax.ppermute(x, ("slab", "hodlr"), route)

    def exchanged(p, moves):
        return [moved(p, moves, x) for x in offsets]

    (coarse_v, fine_v, ahead_v), w = fetch(spans, cross, source, right)
    later = [(k, k - 1) for k in range(IN_PLACE + 1, chain)]
    early = moved(ahead_v, [(1, 0)] + later)
    coarse = moved(coarse_v, later)
    ranks = cross * rank
    whole = ((0, width),)
    p = project(spans, w, [coarse_v, fine_v], ranks, OPEN_FLOPS)
    parts = exchanged(p, [(k, k) for k in range(chain)])
    leaf, u = leaves[0], u_rows[0].reshape(levels * rank, width)
    sums, projected = first_part(spans, cross, w, leaf, right)

    q = jnp.zeros(p.shape, jnp.float32)
    every = tuple(range(len(spans)))
    far = functools.partial(far_part, rank, size, spans)
    out, q = far(every, sums, projected, q, parts, levels_of, u, False)
    front = [moved(out, [(0, 1)])]
    ahead = [project(whole, [out], [early], ranks)]
    relayed = offsets[1::2]
    parts = [moved(ahead[0], [(0, 1)], x) for x in relayed]
    late, near_v = turn_near(spans, cross, size, coarse_v, right, ahead[0])
    second = moved(late, [(2, 1)])
    levels_relayed = [cross - x.bit_length() for x in relayed]
    for k in range(1, chain):
        levels_now = levels_of[::-1]
        for i, span in enumerate(spans):
            behind = projected[i - 1 : i] if i else ahead if k == 1 else []
            if i == 1 and k <= IN_PLACE:
                if k == IN_PLACE:
                    turned = turn(size, [coarse, early[-rank:]])
                nearby = nearby_part(
                    rank,
                    front[0],
                    fine_v,
                    ranks,
                    parts,
                    levels_relayed,
                    behind + (ahead if k == 1 else [turned]),
                    OPEN_FLOPS,
                )
                parts = [moved(nearby, [(k, k)], offsets[0])] + parts
                levels_now = [None] + levels_relayed
                behind = [nearby]
            given, start = (front[0], span[0]) if len(front) == 1 else (front[i], 0)
            w[i], sums[i], projected[i] = near_part(span, start, (levels - cross) * rank, w[i], given, leaf, near_v, behind)
        if k == chain - 1:
            out, _ = far(every, sums, projected, q, parts, levels_now, u, True)
            return out[None]
        split = k >= IN_PLACE and k != WHOLE_HOP
        outs, front = [], []
        for chosen in [(i,) for i in every] if split else [every]:
            out, q = far(chosen, sums, projected, q, [] if front else parts, levels_now, u, False)
            outs.append(out)
            front.append(moved(out, [(k, k + 1)]))
        if k < IN_PLACE:
            p = project(whole, outs, [second], ranks)
        else:
            p = project_turned(spans if split else whole, outs, turned)
        sent = relayed if k < IN_PLACE else offsets[::-1]
        parts = [moved(p, [(k, k + 1)], x) for x in sent]


def solution(mesh):
    in_specs = (
        P("slab", None, "hodlr"),
        P("slab", "hodlr", None, None),
        P("slab", None, None, "hodlr"),
        P("slab", None, None, "hodlr"),
    )
    out_specs = P("slab", None, "hodlr")
    return jax.shard_map(local, mesh=mesh, in_specs=in_specs, out_specs=out_specs, check_vma=False)
```

```python
import functools

import jax
import jax.numpy as jnp
from jax import lax
from jax.experimental import pallas as pl
from jax.experimental.pallas import tpu as pltpu
from jax.sharding import PartitionSpec as P

VMEM_LIMIT = 24 * 1024 * 1024
FIRST_SHARE = 2
IN_PLACE = 2
WHOLE_HOP = 3
OPEN_FLOPS = 4 * 10**9
ROWS_TIMES_COLUMNS = (((1,), (0,)), ((), ()))
ROWS_TIMES_ROWS = (((1,), (1,)), ((), ()))


def dot(a, b, dims=ROWS_TIMES_COLUMNS):
    return lax.dot_general(a, b, dims, preferred_element_type=jnp.float32)


def call(kernel, outs, args, aliases=None, scratch=(), from_hbm=(), flops=0):
    whole = pl.BlockSpec(memory_space=pltpu.VMEM)
    remote = pl.BlockSpec(memory_space=pl.ANY)
    placed = [
        pltpu.with_memory_space_constraint(a, pltpu.HBM if i in from_hbm else pltpu.VMEM)
        for i, a in enumerate(args)
    ]
    return pl.pallas_call(
        kernel,
        out_shape=outs,
        in_specs=[remote if i in from_hbm else whole for i in range(len(args))],
        out_specs=[whole] * len(outs),
        scratch_shapes=scratch,
        input_output_aliases=aliases or {},
        compiler_params=pltpu.CompilerParams(vmem_limit_bytes=VMEM_LIMIT),
        cost_estimate=pl.CostEstimate(flops=flops, bytes_accessed=0, transcendentals=0),
    )(*placed)


def on_factors(value, v_refs, columns, ranks):
    pieces = [dot(value, ref[:, columns], ROWS_TIMES_ROWS) for ref in v_refs]
    missing = ranks - sum(ref.shape[0] for ref in v_refs)
    if missing:
        pieces.append(jnp.zeros((value.shape[0], missing), jnp.float32))
    return jnp.concatenate(pieces, axis=1)


def fetch_kernel(spans, source_ref, v_ref, *refs):
    v_outs, w_outs, sems = refs[: -1 - len(spans)], refs[-1 - len(spans) : -1], refs[-1]
    copies, level = [], 0
    for out in v_outs[:-1]:
        copies.append((v_ref.at[pl.ds(level, out.shape[0])], out))
        level += out.shape[0]
    first = jnp.where(lax.axis_index("slab") == 1, 0, 1)
    copies.append((v_ref.at[pl.ds(first, v_outs[-1].shape[0])], v_outs[-1]))
    for out, (start, stop) in zip(w_outs, spans):
        copies.append((source_ref.at[:, pl.ds(start, stop - start)], out))
    copies = [pltpu.make_async_copy(a, b, sems.at[i]) for i, (a, b) in enumerate(copies)]
    for copy in copies:
        copy.start()
    for copy in copies:
        copy.wait()


def fetch(spans, cross, source, v):
    _, rank, width = v.shape
    shares = (cross - 1, 1, cross - 1)
    outs = [pltpu.VMEM((n, rank, width), v.dtype) for n in shares]
    outs += [pltpu.VMEM((source.shape[0], stop - start), source.dtype) for start, stop in spans]
    found = call(
        functools.partial(fetch_kernel, spans),
        outs,
        [source, v],
        scratch=[pltpu.SemaphoreType.DMA((len(outs),))],
        from_hbm=(0, 1),
    )
    return [f.reshape(-1, width) for f in found[: len(shares)]], list(found[len(shares) :])


def turn_near_kernel(cross, near, x_ref, v_ref, other_ref, x_out, near_out):
    size = near_out.shape[1]
    group = near_out.shape[2] // near
    for c in range(near_out.shape[0] * group):
        turned = v_ref[cross:, :, c * size : (c + 1) * size].reshape(near, size).T
        near_out[c // group, :, c % group * near : (c % group + 1) * near] = turned
    x_out[...] = x_ref[...]


def turn_near(spans, cross, size, x, v, other):
    levels, rank, width = v.shape
    near = (levels - cross) * rank
    group = 2 if all((stop - start) // size % 2 == 0 for start, stop in spans) else 1
    outs = [pltpu.VMEM(x.shape, x.dtype), pltpu.VMEM((width // size // group, size, group * near), v.dtype)]
    return call(functools.partial(turn_near_kernel, cross, near), outs, [x, v, other], flops=OPEN_FLOPS)


def project_kernel(spans, factors, *refs):
    v_refs, parts, p_ref = refs[:factors], refs[factors:-1], refs[-1]
    total = None
    for ref, (start, stop) in zip(parts, spans):
        term = on_factors(ref[...], v_refs, slice(start, stop), p_ref.shape[1])
        total = term if total is None else total + term
    p_ref[...] = total.astype(p_ref.dtype)


def project(spans, w, far_v, ranks, flops=0):
    outs = [pltpu.VMEM((w[0].shape[0], ranks), jnp.bfloat16)]
    return call(functools.partial(project_kernel, spans, len(far_v)), outs, [*far_v, *w], flops=flops)[0]


def turn_kernel(size, *refs):
    v_refs, out_ref = refs[:-1], refs[-1]
    for c in range(out_ref.shape[0] // size):
        rows = slice(c * size, (c + 1) * size)
        out_ref[rows, :] = jnp.concatenate([ref[:, rows] for ref in v_refs], axis=0).T


def turn(size, v):
    outs = [pltpu.VMEM((v[0].shape[1], sum(x.shape[0] for x in v)), v[0].dtype)]
    return call(functools.partial(turn_kernel, size), outs, v)[0]


def project_turned_kernel(spans, v_ref, *refs):
    parts, p_ref = refs[:-1], refs[-1]
    total = None
    for ref, (start, stop) in zip(parts, spans):
        term = dot(ref[...], v_ref[start:stop, :])
        total = term if total is None else total + term
    p_ref[...] = total.astype(p_ref.dtype)


def project_turned(spans, w, v):
    outs = [pltpu.VMEM((w[0].shape[0], v.shape[1]), jnp.bfloat16)]
    return call(functools.partial(project_turned_kernel, spans), outs, [v, *w])[0]


def leaves_of(span, size):
    return range(span[0] // size, span[1] // size)


def first_kernel(spans, cross, *refs):
    n = len(spans)
    w_refs, (leaf_ref, v_ref) = refs[:n], refs[n : n + 2]
    sum_refs, p_refs = refs[n + 2 : 2 * n + 2], refs[2 * n + 2 :]
    size = leaf_ref.shape[1]
    near = p_refs[0].shape[2]
    for i, span in enumerate(spans):
        for j, c in enumerate(leaves_of(span, size)):
            columns = slice(j * size, (j + 1) * size)
            rows = v_ref[cross:, :, c * size : (c + 1) * size].reshape(near, size)
            p_refs[i][j] = dot(w_refs[i][:, columns], rows, ROWS_TIMES_ROWS)
            sum_refs[i][:, columns] = dot(w_refs[i][:, columns], leaf_ref[c])


def first_part(spans, cross, w, leaf, v):
    levels, rank, width = v.shape
    size = leaf.shape[1]
    rows = w[0].shape[0]
    near = (levels - cross) * rank
    outs = [pltpu.VMEM(x.shape, jnp.float32) for x in w]
    outs += [pltpu.VMEM((x.shape[1] // size, rows, near), jnp.float32) for x in w]
    n = len(w)
    found = call(functools.partial(first_kernel, spans, cross), outs, [*w, leaf, v])
    return list(found[:n]), list(found[n:])


def nearby_kernel(rank, levels_of, front_ref, v_ref, *refs):
    part_refs, p_ref = refs[: len(levels_of)], refs[-1]
    term = dot(front_ref[...], v_ref[...], ROWS_TIMES_ROWS)
    rows, ranks = p_ref.shape
    before = ranks - term.shape[1]
    if before:
        term = jnp.concatenate([jnp.zeros((rows, before), jnp.float32), term], axis=1)
    lane = lax.broadcasted_iota(jnp.int32, (rows, ranks), 1) // rank
    for ref, level in zip(part_refs, levels_of):
        term = term + jnp.where(lane == level, ref[...].astype(jnp.float32), 0.0)
    p_ref[...] = term.astype(p_ref.dtype)


def nearby_part(rank, front, v, ranks, parts, levels_of, behind, flops=0):
    outs = [pltpu.VMEM((front.shape[0], ranks), jnp.bfloat16)]
    return call(functools.partial(nearby_kernel, rank, tuple(levels_of)), outs, [front, v, *parts, *behind], flops=flops)[0]


def near_kernel(span, start, w_ref, front_ref, leaf_ref, v_ref, *refs):
    w_out, sum_out, p_out = refs[-3:]
    size = leaf_ref.shape[1]
    rows = w_ref.shape[0]
    near = p_out.shape[2]
    group = v_ref.shape[2] // near
    members = []
    for j, c in enumerate(leaves_of(span, size)):
        columns = slice(j * size, (j + 1) * size)
        w = w_ref[:, columns] + front_ref[:, start + j * size : start + (j + 1) * size]
        w_out[:, columns] = w
        members.append(w)
        if len(members) == group:
            both = dot(jnp.concatenate(members, axis=0), v_ref[c // group])
            for i in range(group):
                p_out[j - group + 1 + i] = both[i * rows : (i + 1) * rows, i * near : (i + 1) * near]
            members = []
        sum_out[:, columns] = dot(w, leaf_ref[c])


def near_part(span, start, near, w, front, leaf, near_v, behind):
    outs = [
        pltpu.VMEM(w.shape, w.dtype),
        pltpu.VMEM(w.shape, jnp.float32),
        pltpu.VMEM((w.shape[1] // leaf.shape[1], w.shape[0], near), jnp.float32),
    ]
    return call(functools.partial(near_kernel, span, start), outs, [w, front, leaf, near_v, *behind], {0: 0})


def far_kernel(rank, size, spans, chosen, levels_of, *refs):
    refs = list(refs)
    sum_refs = [refs.pop(0) for _ in chosen]
    p_refs = [refs.pop(0) for _ in spans]
    q_ref = refs.pop(0)
    part_refs = [refs.pop(0) for _ in levels_of]
    u_ref = refs.pop(0)
    out_ref, q_out = refs[:2]
    rows, far = q_ref.shape
    near = u_ref.shape[0] - far

    q = q_ref[...]
    lane = lax.broadcasted_iota(jnp.int32, (rows, far), 1) // rank
    for ref, level in zip(part_refs, levels_of):
        part = ref[...].astype(jnp.float32)
        q = q + (part if level is None else jnp.where(lane == level, part, 0.0))
    q_out[...] = q

    projected = [ref[j] for ref in p_refs for j in range(ref.shape[0])]
    nleaf = len(projected)
    lane = lax.broadcasted_iota(jnp.int32, (rows, near), 1) // rank
    sums = []
    for level in range(near // rank):
        block = nleaf >> (level + 1)
        sums.append(
            [
                functools.reduce(jnp.add, projected[b * block : (b + 1) * block])
                for b in range(nleaf // block)
            ]
        )
    place = 0
    for i, ref in zip(chosen, sum_refs):
        for j, c in enumerate(leaves_of(spans[i], size)):
            swapped = sums[0][(c // (nleaf >> 1)) ^ 1]
            for level in range(1, near // rank):
                swapped = jnp.where(lane == level, sums[level][(c // (nleaf >> (level + 1))) ^ 1], swapped)
            columns = slice(c * size, (c + 1) * size)
            value = ref[:, j * size : (j + 1) * size]
            value = value + dot(q.astype(jnp.bfloat16), u_ref[:far, columns])
            value = value + dot(swapped.astype(jnp.bfloat16), u_ref[far:, columns])
            out_ref[:, place : place + size] = value.astype(jnp.bfloat16)
            place += size


def far_part(rank, size, spans, chosen, sums, projected, q, parts, levels_of, u, last):
    args = [*[sums[i] for i in chosen], *projected, q, *parts, u]
    width = sum(sums[i].shape[1] for i in chosen)
    space = jax.ShapeDtypeStruct if last else pltpu.VMEM
    outs = [space((q.shape[0], width), jnp.bfloat16), pltpu.VMEM(q.shape, jnp.float32)]
    kernel = functools.partial(far_kernel, rank, size, spans, chosen, tuple(levels_of) if parts else ())
    return call(kernel, outs, args, {len(chosen) + len(projected): 1})


def local(sources, leaves, v_rows, u_rows):
    devices = lax.axis_size("hodlr")
    chain = lax.axis_size("slab")
    cross = devices.bit_length() - 1
    source, right = sources[0], v_rows[0]
    levels, rank, width = right.shape
    nleaf, size = leaves.shape[1:3]
    cut = max(nleaf * FIRST_SHARE // 4, 1) * size
    spans = ((0, cut), (cut, width))
    offsets = list(range(1, devices))
    levels_of = [cross - x.bit_length() for x in offsets]
    other_core_first = sorted(offsets, key=lambda x: (x % 2 == 0, -x))

    def moved(x, moves, offset=0):
        route = [(a * devices + h, b * devices + (h ^ offset)) for a, b in moves for h in range(devices)]
        return lax.ppermute(x, ("slab", "hodlr"), route)

    def exchanged(p, moves):
        return [moved(p, moves, x) for x in offsets]

    (coarse_v, fine_v, ahead_v), w = fetch(spans, cross, source, right)
    later = [(k, k - 1) for k in range(IN_PLACE + 1, chain)]
    early = moved(ahead_v, [(1, 0)] + later)
    coarse = moved(coarse_v, later)
    ranks = cross * rank
    whole = ((0, width),)
    p = project(spans, w, [coarse_v, fine_v], ranks, OPEN_FLOPS)
    parts = exchanged(p, [(k, k) for k in range(chain)])
    leaf, u = leaves[0], u_rows[0].reshape(levels * rank, width)
    sums, projected = first_part(spans, cross, w, leaf, right)

    q = jnp.zeros(p.shape, jnp.float32)
    every = tuple(range(len(spans)))
    far = functools.partial(far_part, rank, size, spans)
    out, q = far(every, sums, projected, q, parts, levels_of, u, False)
    front = [moved(out, [(0, 1)])]
    ahead = [project(whole, [out], [early], ranks)]
    relayed = offsets[1::2]
    parts = [moved(ahead[0], [(0, 1)], x) for x in relayed]
    late, near_v = turn_near(spans, cross, size, coarse_v, right, ahead[0])
    second = moved(late, [(2, 1)])
    levels_relayed = [cross - x.bit_length() for x in relayed]
    for k in range(1, chain):
        levels_now = [cross - x.bit_length() for x in other_core_first]
        for i, span in enumerate(spans):
            behind = projected[i - 1 : i] if i else ahead if k == 1 else []
            if i == 1 and k <= IN_PLACE:
                if k == IN_PLACE:
                    turned = turn(size, [coarse, early[-rank:]])
                nearby = nearby_part(
                    rank,
                    front[0],
                    fine_v,
                    ranks,
                    parts,
                    levels_relayed,
                    behind + (ahead if k == 1 else [turned]),
                    OPEN_FLOPS,
                )
                parts = [moved(nearby, [(k, k)], offsets[0])] + parts
                levels_now = [None] + levels_relayed
                behind = [nearby]
            given, start = (front[0], span[0]) if len(front) == 1 else (front[i], 0)
            w[i], sums[i], projected[i] = near_part(span, start, (levels - cross) * rank, w[i], given, leaf, near_v, behind)
        if k == chain - 1:
            out, _ = far(every, sums, projected, q, parts, levels_now, u, True)
            return out[None]
        split = k >= IN_PLACE and k != WHOLE_HOP
        outs, front = [], []
        for chosen in [(i,) for i in every] if split else [every]:
            out, q = far(chosen, sums, projected, q, [] if front else parts, levels_now, u, False)
            outs.append(out)
            front.append(moved(out, [(k, k + 1)]))
        if k < IN_PLACE:
            p = project(whole, outs, [second], ranks)
        else:
            p = project_turned(spans if split else whole, outs, turned)
        sent = relayed if k < IN_PLACE else other_core_first
        parts = [moved(p, [(k, k + 1)], x) for x in sent]


def solution(mesh):
    in_specs = (
        P("slab", None, "hodlr"),
        P("slab", "hodlr", None, None),
        P("slab", None, None, "hodlr"),
        P("slab", None, None, "hodlr"),
    )
    out_specs = P("slab", None, "hodlr")
    return jax.shard_map(local, mesh=mesh, in_specs=in_specs, out_specs=out_specs, check_vma=False)
```

```python
import functools

import jax
import jax.numpy as jnp
from jax import lax
from jax.experimental import pallas as pl
from jax.experimental.pallas import tpu as pltpu
from jax.sharding import PartitionSpec as P

VMEM_LIMIT = 24 * 1024 * 1024
FIRST_SHARE = 2
IN_PLACE = 2
OPEN_FLOPS = 4 * 10**9
ROWS_TIMES_COLUMNS = (((1,), (0,)), ((), ()))
ROWS_TIMES_ROWS = (((1,), (1,)), ((), ()))


def dot(a, b, dims=ROWS_TIMES_COLUMNS):
    return lax.dot_general(a, b, dims, preferred_element_type=jnp.float32)


def call(kernel, outs, args, aliases=None, scratch=(), from_hbm=(), flops=0):
    whole = pl.BlockSpec(memory_space=pltpu.VMEM)
    remote = pl.BlockSpec(memory_space=pl.ANY)
    placed = [
        pltpu.with_memory_space_constraint(a, pltpu.HBM if i in from_hbm else pltpu.VMEM)
        for i, a in enumerate(args)
    ]
    return pl.pallas_call(
        kernel,
        out_shape=outs,
        in_specs=[remote if i in from_hbm else whole for i in range(len(args))],
        out_specs=[whole] * len(outs),
        scratch_shapes=scratch,
        input_output_aliases=aliases or {},
        compiler_params=pltpu.CompilerParams(vmem_limit_bytes=VMEM_LIMIT),
        cost_estimate=pl.CostEstimate(flops=flops, bytes_accessed=0, transcendentals=0),
    )(*placed)


def on_factors(value, v_refs, columns, ranks):
    pieces = [dot(value, ref[:, columns], ROWS_TIMES_ROWS) for ref in v_refs]
    missing = ranks - sum(ref.shape[0] for ref in v_refs)
    if missing:
        pieces.append(jnp.zeros((value.shape[0], missing), jnp.float32))
    return jnp.concatenate(pieces, axis=1)


def fetch_kernel(spans, source_ref, v_ref, *refs):
    v_outs, w_outs, sems = refs[: -1 - len(spans)], refs[-1 - len(spans) : -1], refs[-1]
    copies, level = [], 0
    for out in v_outs[:-1]:
        copies.append((v_ref.at[pl.ds(level, out.shape[0])], out))
        level += out.shape[0]
    first = jnp.where(lax.axis_index("slab") == 1, 0, 1)
    copies.append((v_ref.at[pl.ds(first, v_outs[-1].shape[0])], v_outs[-1]))
    for out, (start, stop) in zip(w_outs, spans):
        copies.append((source_ref.at[:, pl.ds(start, stop - start)], out))
    copies = [pltpu.make_async_copy(a, b, sems.at[i]) for i, (a, b) in enumerate(copies)]
    for copy in copies:
        copy.start()
    for copy in copies:
        copy.wait()


def fetch(spans, cross, source, v):
    _, rank, width = v.shape
    shares = (cross - 1, 1, cross - 1)
    outs = [pltpu.VMEM((n, rank, width), v.dtype) for n in shares]
    outs += [pltpu.VMEM((source.shape[0], stop - start), source.dtype) for start, stop in spans]
    found = call(
        functools.partial(fetch_kernel, spans),
        outs,
        [source, v],
        scratch=[pltpu.SemaphoreType.DMA((len(outs),))],
        from_hbm=(0, 1),
    )
    return [f.reshape(-1, width) for f in found[: len(shares)]], list(found[len(shares) :])


def behind_kernel(x_ref, other_ref, out_ref):
    out_ref[...] = x_ref[...]


def put_behind(x, other):
    return call(behind_kernel, [pltpu.VMEM(x.shape, x.dtype)], [x, other], flops=OPEN_FLOPS)[0]


def project_kernel(spans, factors, *refs):
    v_refs, parts, p_ref = refs[:factors], refs[factors:-1], refs[-1]
    total = None
    for ref, (start, stop) in zip(parts, spans):
        term = on_factors(ref[...], v_refs, slice(start, stop), p_ref.shape[1])
        total = term if total is None else total + term
    p_ref[...] = total.astype(p_ref.dtype)


def project(spans, w, far_v, ranks, flops=0):
    outs = [pltpu.VMEM((w[0].shape[0], ranks), jnp.bfloat16)]
    return call(functools.partial(project_kernel, spans, len(far_v)), outs, [*far_v, *w], flops=flops)[0]


def turn_kernel(size, *refs):
    v_refs, out_ref = refs[:-1], refs[-1]
    for c in range(out_ref.shape[0] // size):
        rows = slice(c * size, (c + 1) * size)
        out_ref[rows, :] = jnp.concatenate([ref[:, rows] for ref in v_refs], axis=0).T


def turn(size, v):
    outs = [pltpu.VMEM((v[0].shape[1], sum(x.shape[0] for x in v)), v[0].dtype)]
    return call(functools.partial(turn_kernel, size), outs, v)[0]


def project_turned_kernel(spans, v_ref, *refs):
    parts, p_ref = refs[:-1], refs[-1]
    total = None
    for ref, (start, stop) in zip(parts, spans):
        term = dot(ref[...], v_ref[start:stop, :])
        total = term if total is None else total + term
    p_ref[...] = total.astype(p_ref.dtype)


def project_turned(spans, w, v):
    outs = [pltpu.VMEM((w[0].shape[0], v.shape[1]), jnp.bfloat16)]
    return call(functools.partial(project_turned_kernel, spans), outs, [v, *w])[0]


def leaves_of(span, size):
    return range(span[0] // size, span[1] // size)


def first_kernel(spans, cross, *refs):
    n = len(spans)
    w_refs, (leaf_ref, v_ref), near_out = refs[:n], refs[n : n + 2], refs[n + 2]
    sum_refs, p_refs = refs[n + 3 : 2 * n + 3], refs[2 * n + 3 :]
    size = leaf_ref.shape[1]
    near = p_refs[0].shape[2]
    for i, span in enumerate(spans):
        for j, c in enumerate(leaves_of(span, size)):
            columns = slice(j * size, (j + 1) * size)
            turned = v_ref[cross:, :, c * size : (c + 1) * size].reshape(near, size).T
            group = near_out.shape[2] // near
            near_out[c // group, :, c % group * near : (c % group + 1) * near] = turned
            p_refs[i][j] = dot(w_refs[i][:, columns], turned)
            sum_refs[i][:, columns] = dot(w_refs[i][:, columns], leaf_ref[c])


def first_part(spans, cross, w, leaf, v):
    levels, rank, width = v.shape
    size = leaf.shape[1]
    rows = w[0].shape[0]
    near = (levels - cross) * rank
    group = 2 if all((stop - start) // size % 2 == 0 for start, stop in spans) else 1
    outs = [pltpu.VMEM((width // size // group, size, group * near), v.dtype)]
    outs += [pltpu.VMEM(x.shape, jnp.float32) for x in w]
    outs += [pltpu.VMEM((x.shape[1] // size, rows, near), jnp.float32) for x in w]
    n = len(w)
    found = call(functools.partial(first_kernel, spans, cross), outs, [*w, leaf, v])
    return found[0], list(found[1 : 1 + n]), list(found[1 + n :])


def nearby_kernel(rank, levels_of, front_ref, v_ref, *refs):
    part_refs, p_ref = refs[: len(levels_of)], refs[-1]
    term = dot(front_ref[...], v_ref[...], ROWS_TIMES_ROWS)
    rows, ranks = p_ref.shape
    before = ranks - term.shape[1]
    if before:
        term = jnp.concatenate([jnp.zeros((rows, before), jnp.float32), term], axis=1)
    lane = lax.broadcasted_iota(jnp.int32, (rows, ranks), 1) // rank
    for ref, level in zip(part_refs, levels_of):
        term = term + jnp.where(lane == level, ref[...].astype(jnp.float32), 0.0)
    p_ref[...] = term.astype(p_ref.dtype)


def nearby_part(rank, front, v, ranks, parts, levels_of, behind, flops=0):
    outs = [pltpu.VMEM((front.shape[0], ranks), jnp.bfloat16)]
    return call(functools.partial(nearby_kernel, rank, tuple(levels_of)), outs, [front, v, *parts, *behind], flops=flops)[0]


def near_kernel(span, start, w_ref, front_ref, leaf_ref, v_ref, *refs):
    w_out, sum_out, p_out = refs[-3:]
    size = leaf_ref.shape[1]
    rows = w_ref.shape[0]
    near = p_out.shape[2]
    group = v_ref.shape[2] // near
    members = []
    for j, c in enumerate(leaves_of(span, size)):
        columns = slice(j * size, (j + 1) * size)
        w = w_ref[:, columns] + front_ref[:, start + j * size : start + (j + 1) * size]
        w_out[:, columns] = w
        members.append(w)
        if len(members) == group:
            both = dot(jnp.concatenate(members, axis=0), v_ref[c // group])
            for i in range(group):
                p_out[j - group + 1 + i] = both[i * rows : (i + 1) * rows, i * near : (i + 1) * near]
            members = []
        sum_out[:, columns] = dot(w, leaf_ref[c])


def near_part(span, start, near, w, front, leaf, near_v, behind):
    outs = [
        pltpu.VMEM(w.shape, w.dtype),
        pltpu.VMEM(w.shape, jnp.float32),
        pltpu.VMEM((w.shape[1] // leaf.shape[1], w.shape[0], near), jnp.float32),
    ]
    return call(functools.partial(near_kernel, span, start), outs, [w, front, leaf, near_v, *behind], {0: 0})


def far_kernel(rank, size, spans, chosen, levels_of, *refs):
    refs = list(refs)
    sum_refs = [refs.pop(0) for _ in chosen]
    p_refs = [refs.pop(0) for _ in spans]
    q_ref = refs.pop(0)
    part_refs = [refs.pop(0) for _ in levels_of]
    u_ref = refs.pop(0)
    out_ref, q_out = refs[:2]
    rows, far = q_ref.shape
    near = u_ref.shape[0] - far

    q = q_ref[...]
    lane = lax.broadcasted_iota(jnp.int32, (rows, far), 1) // rank
    for ref, level in zip(part_refs, levels_of):
        part = ref[...].astype(jnp.float32)
        q = q + (part if level is None else jnp.where(lane == level, part, 0.0))
    q_out[...] = q

    projected = [ref[j] for ref in p_refs for j in range(ref.shape[0])]
    nleaf = len(projected)
    lane = lax.broadcasted_iota(jnp.int32, (rows, near), 1) // rank
    sums = []
    for level in range(near // rank):
        block = nleaf >> (level + 1)
        sums.append(
            [
                functools.reduce(jnp.add, projected[b * block : (b + 1) * block])
                for b in range(nleaf // block)
            ]
        )
    place = 0
    for i, ref in zip(chosen, sum_refs):
        for j, c in enumerate(leaves_of(spans[i], size)):
            swapped = sums[0][(c // (nleaf >> 1)) ^ 1]
            for level in range(1, near // rank):
                swapped = jnp.where(lane == level, sums[level][(c // (nleaf >> (level + 1))) ^ 1], swapped)
            columns = slice(c * size, (c + 1) * size)
            value = ref[:, j * size : (j + 1) * size]
            value = value + dot(q.astype(jnp.bfloat16), u_ref[:far, columns])
            value = value + dot(swapped.astype(jnp.bfloat16), u_ref[far:, columns])
            out_ref[:, place : place + size] = value.astype(jnp.bfloat16)
            place += size


def far_part(rank, size, spans, chosen, sums, projected, q, parts, levels_of, u, last):
    args = [*[sums[i] for i in chosen], *projected, q, *parts, u]
    width = sum(sums[i].shape[1] for i in chosen)
    space = jax.ShapeDtypeStruct if last else pltpu.VMEM
    outs = [space((q.shape[0], width), jnp.bfloat16), pltpu.VMEM(q.shape, jnp.float32)]
    kernel = functools.partial(far_kernel, rank, size, spans, chosen, tuple(levels_of) if parts else ())
    return call(kernel, outs, args, {len(chosen) + len(projected): 1})


def local(sources, leaves, v_rows, u_rows):
    devices = lax.axis_size("hodlr")
    chain = lax.axis_size("slab")
    cross = devices.bit_length() - 1
    source, right = sources[0], v_rows[0]
    levels, rank, width = right.shape
    nleaf, size = leaves.shape[1:3]
    cut = max(nleaf * FIRST_SHARE // 4, 1) * size
    spans = ((0, cut), (cut, width))
    offsets = list(range(1, devices))
    levels_of = [cross - x.bit_length() for x in offsets]

    def moved(x, moves, offset=0):
        route = [(a * devices + h, b * devices + (h ^ offset)) for a, b in moves for h in range(devices)]
        return lax.ppermute(x, ("slab", "hodlr"), route)

    def exchanged(p, moves):
        return [moved(p, moves, x) for x in offsets]

    (coarse_v, fine_v, ahead_v), w = fetch(spans, cross, source, right)
    later = [(k, k - 1) for k in range(IN_PLACE + 1, chain)]
    early = moved(ahead_v, [(1, 0)] + later)
    coarse = moved(coarse_v, later)
    ranks = cross * rank
    whole = ((0, width),)
    p = project(spans, w, [coarse_v, fine_v], ranks, OPEN_FLOPS)
    parts = exchanged(p, [(k, k) for k in range(chain)])
    leaf, u = leaves[0], u_rows[0].reshape(levels * rank, width)
    near_v, sums, projected = first_part(spans, cross, w, leaf, right)

    q = jnp.zeros(p.shape, jnp.float32)
    every = tuple(range(len(spans)))
    far = functools.partial(far_part, rank, size, spans)
    out, q = far(every, sums, projected, q, parts, levels_of, u, False)
    front = [moved(out, [(0, 1)])]
    ahead = [project(whole, [out], [early], ranks)]
    relayed = offsets[1::2]
    parts = [moved(ahead[0], [(0, 1)], x) for x in offsets[1:]]
    second = moved(put_behind(coarse_v, ahead[0]), [(2, 1)])
    levels_relayed = [cross - x.bit_length() for x in relayed]
    for k in range(1, chain):
        levels_now = levels_of[::-1]
        for i, span in enumerate(spans):
            behind = projected[i - 1 : i] if i else ahead if k == 1 else []
            if i == 1 and k <= IN_PLACE:
                if k == IN_PLACE:
                    turned = turn(size, [coarse, early[-rank:]])
                nearby = nearby_part(
                    rank,
                    front[0],
                    fine_v,
                    ranks,
                    parts if k == IN_PLACE else [],
                    levels_relayed if k == IN_PLACE else [],
                    behind + (ahead if k == 1 else [turned]),
                    OPEN_FLOPS,
                )
                parts = [moved(nearby, [(k, k)], offsets[0])] + parts
                levels_now = [None] + levels_relayed if k == IN_PLACE else levels_of
                behind = [nearby] + (parts[1:] if k == 1 else [])
            given, start = (front[0], span[0]) if len(front) == 1 else (front[i], 0)
            w[i], sums[i], projected[i] = near_part(span, start, (levels - cross) * rank, w[i], given, leaf, near_v, behind)
        if k == chain - 1:
            out, _ = far(every, sums, projected, q, parts, levels_now, u, True)
            return out[None]
        split = k >= IN_PLACE and k % 2 == 0
        outs, front = [], []
        for chosen in [(i,) for i in every] if split else [every]:
            out, q = far(chosen, sums, projected, q, [] if front else parts, levels_now, u, False)
            outs.append(out)
            front.append(moved(out, [(k, k + 1)]))
        if k < IN_PLACE:
            p = project(whole, outs, [second], ranks)
        else:
            p = project_turned(spans if split else whole, outs, turned)
        sent = relayed if k < IN_PLACE else offsets[::-1]
        parts = [moved(p, [(k, k + 1)], x) for x in sent]


def solution(mesh):
    in_specs = (
        P("slab", None, "hodlr"),
        P("slab", "hodlr", None, None),
        P("slab", None, None, "hodlr"),
        P("slab", None, None, "hodlr"),
    )
    out_specs = P("slab", None, "hodlr")
    return jax.shard_map(local, mesh=mesh, in_specs=in_specs, out_specs=out_specs, check_vma=False)
```

```python
import functools

import jax
import jax.numpy as jnp
from jax import lax
from jax.experimental import pallas as pl
from jax.experimental.pallas import tpu as pltpu
from jax.sharding import PartitionSpec as P

VMEM_LIMIT = 24 * 1024 * 1024
FIRST_SHARE = 2
IN_PLACE = 2
WHOLE_HOP = 3
OPEN_FLOPS = 4 * 10**9
ROWS_TIMES_COLUMNS = (((1,), (0,)), ((), ()))
ROWS_TIMES_ROWS = (((1,), (1,)), ((), ()))


def dot(a, b, dims=ROWS_TIMES_COLUMNS):
    return lax.dot_general(a, b, dims, preferred_element_type=jnp.float32)


def call(kernel, outs, args, aliases=None, scratch=(), from_hbm=(), flops=0):
    whole = pl.BlockSpec(memory_space=pltpu.VMEM)
    remote = pl.BlockSpec(memory_space=pl.ANY)
    placed = [
        pltpu.with_memory_space_constraint(a, pltpu.HBM if i in from_hbm else pltpu.VMEM)
        for i, a in enumerate(args)
    ]
    return pl.pallas_call(
        kernel,
        out_shape=outs,
        in_specs=[remote if i in from_hbm else whole for i in range(len(args))],
        out_specs=[whole] * len(outs),
        scratch_shapes=scratch,
        input_output_aliases=aliases or {},
        compiler_params=pltpu.CompilerParams(vmem_limit_bytes=VMEM_LIMIT),
        cost_estimate=pl.CostEstimate(flops=flops, bytes_accessed=0, transcendentals=0),
    )(*placed)


def on_factors(value, v_refs, columns, ranks):
    pieces = [dot(value, ref[:, columns], ROWS_TIMES_ROWS) for ref in v_refs]
    missing = ranks - sum(ref.shape[0] for ref in v_refs)
    if missing:
        pieces.append(jnp.zeros((value.shape[0], missing), jnp.float32))
    return jnp.concatenate(pieces, axis=1)


def fetch_kernel(spans, source_ref, v_ref, *refs):
    v_outs, w_outs, sems = refs[: -1 - len(spans)], refs[-1 - len(spans) : -1], refs[-1]
    copies, level = [], 0
    for out in v_outs[:-1]:
        copies.append((v_ref.at[pl.ds(level, out.shape[0])], out))
        level += out.shape[0]
    first = jnp.where(lax.axis_index("slab") == 1, 0, 1)
    copies.append((v_ref.at[pl.ds(first, v_outs[-1].shape[0])], v_outs[-1]))
    for out, (start, stop) in zip(w_outs, spans):
        copies.append((source_ref.at[:, pl.ds(start, stop - start)], out))
    copies = [pltpu.make_async_copy(a, b, sems.at[i]) for i, (a, b) in enumerate(copies)]
    for copy in copies:
        copy.start()
    for copy in copies:
        copy.wait()


def fetch(spans, cross, source, v):
    _, rank, width = v.shape
    shares = (cross - 1, 1, cross - 1)
    outs = [pltpu.VMEM((n, rank, width), v.dtype) for n in shares]
    outs += [pltpu.VMEM((source.shape[0], stop - start), source.dtype) for start, stop in spans]
    found = call(
        functools.partial(fetch_kernel, spans),
        outs,
        [source, v],
        scratch=[pltpu.SemaphoreType.DMA((len(outs),))],
        from_hbm=(0, 1),
    )
    return [f.reshape(-1, width) for f in found[: len(shares)]], list(found[len(shares) :])


def behind_kernel(x_ref, other_ref, out_ref):
    out_ref[...] = x_ref[...]


def put_behind(x, other):
    return call(behind_kernel, [pltpu.VMEM(x.shape, x.dtype)], [x, other], flops=OPEN_FLOPS)[0]


def project_kernel(spans, factors, *refs):
    v_refs, parts, p_ref = refs[:factors], refs[factors:-1], refs[-1]
    total = None
    for ref, (start, stop) in zip(parts, spans):
        term = on_factors(ref[...], v_refs, slice(start, stop), p_ref.shape[1])
        total = term if total is None else total + term
    p_ref[...] = total.astype(p_ref.dtype)


def project(spans, w, far_v, ranks, flops=0):
    outs = [pltpu.VMEM((w[0].shape[0], ranks), jnp.bfloat16)]
    return call(functools.partial(project_kernel, spans, len(far_v)), outs, [*far_v, *w], flops=flops)[0]


def turn_kernel(size, *refs):
    v_refs, out_ref = refs[:-1], refs[-1]
    for c in range(out_ref.shape[0] // size):
        rows = slice(c * size, (c + 1) * size)
        out_ref[rows, :] = jnp.concatenate([ref[:, rows] for ref in v_refs], axis=0).T


def turn(size, v):
    outs = [pltpu.VMEM((v[0].shape[1], sum(x.shape[0] for x in v)), v[0].dtype)]
    return call(functools.partial(turn_kernel, size), outs, v)[0]


def project_turned_kernel(spans, v_ref, *refs):
    parts, p_ref = refs[:-1], refs[-1]
    total = None
    for ref, (start, stop) in zip(parts, spans):
        term = dot(ref[...], v_ref[start:stop, :])
        total = term if total is None else total + term
    p_ref[...] = total.astype(p_ref.dtype)


def project_turned(spans, w, v):
    outs = [pltpu.VMEM((w[0].shape[0], v.shape[1]), jnp.bfloat16)]
    return call(functools.partial(project_turned_kernel, spans), outs, [v, *w])[0]


def leaves_of(span, size):
    return range(span[0] // size, span[1] // size)


def first_kernel(spans, cross, *refs):
    n = len(spans)
    w_refs, (leaf_ref, v_ref), near_out = refs[:n], refs[n : n + 2], refs[n + 2]
    sum_refs, p_refs = refs[n + 3 : 2 * n + 3], refs[2 * n + 3 :]
    size = leaf_ref.shape[1]
    near = p_refs[0].shape[2]
    for i, span in enumerate(spans):
        for j, c in enumerate(leaves_of(span, size)):
            columns = slice(j * size, (j + 1) * size)
            turned = v_ref[cross:, :, c * size : (c + 1) * size].reshape(near, size).T
            group = near_out.shape[2] // near
            near_out[c // group, :, c % group * near : (c % group + 1) * near] = turned
            p_refs[i][j] = dot(w_refs[i][:, columns], turned)
            sum_refs[i][:, columns] = dot(w_refs[i][:, columns], leaf_ref[c])


def first_part(spans, cross, w, leaf, v):
    levels, rank, width = v.shape
    size = leaf.shape[1]
    rows = w[0].shape[0]
    near = (levels - cross) * rank
    group = 2 if all((stop - start) // size % 2 == 0 for start, stop in spans) else 1
    outs = [pltpu.VMEM((width // size // group, size, group * near), v.dtype)]
    outs += [pltpu.VMEM(x.shape, jnp.float32) for x in w]
    outs += [pltpu.VMEM((x.shape[1] // size, rows, near), jnp.float32) for x in w]
    n = len(w)
    found = call(functools.partial(first_kernel, spans, cross), outs, [*w, leaf, v])
    return found[0], list(found[1 : 1 + n]), list(found[1 + n :])


def nearby_kernel(rank, levels_of, front_ref, v_ref, *refs):
    part_refs, p_ref = refs[: len(levels_of)], refs[-1]
    term = dot(front_ref[...], v_ref[...], ROWS_TIMES_ROWS)
    rows, ranks = p_ref.shape
    before = ranks - term.shape[1]
    if before:
        term = jnp.concatenate([jnp.zeros((rows, before), jnp.float32), term], axis=1)
    lane = lax.broadcasted_iota(jnp.int32, (rows, ranks), 1) // rank
    for ref, level in zip(part_refs, levels_of):
        term = term + jnp.where(lane == level, ref[...].astype(jnp.float32), 0.0)
    p_ref[...] = term.astype(p_ref.dtype)


def nearby_part(rank, front, v, ranks, parts, levels_of, behind, flops=0):
    outs = [pltpu.VMEM((front.shape[0], ranks), jnp.bfloat16)]
    return call(functools.partial(nearby_kernel, rank, tuple(levels_of)), outs, [front, v, *parts, *behind], flops=flops)[0]


def near_kernel(span, start, w_ref, front_ref, leaf_ref, v_ref, *refs):
    w_out, sum_out, p_out = refs[-3:]
    size = leaf_ref.shape[1]
    rows = w_ref.shape[0]
    near = p_out.shape[2]
    group = v_ref.shape[2] // near
    members = []
    for j, c in enumerate(leaves_of(span, size)):
        columns = slice(j * size, (j + 1) * size)
        w = w_ref[:, columns] + front_ref[:, start + j * size : start + (j + 1) * size]
        w_out[:, columns] = w
        members.append(w)
        if len(members) == group:
            both = dot(jnp.concatenate(members, axis=0), v_ref[c // group])
            for i in range(group):
                p_out[j - group + 1 + i] = both[i * rows : (i + 1) * rows, i * near : (i + 1) * near]
            members = []
        sum_out[:, columns] = dot(w, leaf_ref[c])


def near_part(span, start, near, w, front, leaf, near_v, behind):
    outs = [
        pltpu.VMEM(w.shape, w.dtype),
        pltpu.VMEM(w.shape, jnp.float32),
        pltpu.VMEM((w.shape[1] // leaf.shape[1], w.shape[0], near), jnp.float32),
    ]
    return call(functools.partial(near_kernel, span, start), outs, [w, front, leaf, near_v, *behind], {0: 0})


def far_kernel(rank, size, spans, chosen, levels_of, sends, *refs):
    refs = list(refs)
    p_out = refs.pop() if sends else None
    sum_refs = [refs.pop(0) for _ in chosen]
    p_refs = [refs.pop(0) for _ in spans]
    q_ref = refs.pop(0)
    part_refs = [refs.pop(0) for _ in levels_of]
    u_ref = refs.pop(0)
    next_ref, earlier_ref = (refs.pop(0), refs.pop(0)) if sends else (None, None)
    out_ref, q_out = refs[:2]
    rows, far = q_ref.shape
    near = u_ref.shape[0] - far

    q = q_ref[...]
    lane = lax.broadcasted_iota(jnp.int32, (rows, far), 1) // rank
    for ref, level in zip(part_refs, levels_of):
        part = ref[...].astype(jnp.float32)
        q = q + (part if level is None else jnp.where(lane == level, part, 0.0))
    q_out[...] = q

    projected = [ref[j] for ref in p_refs for j in range(ref.shape[0])]
    nleaf = len(projected)
    lane = lax.broadcasted_iota(jnp.int32, (rows, near), 1) // rank
    sums = []
    for level in range(near // rank):
        block = nleaf >> (level + 1)
        sums.append(
            [
                functools.reduce(jnp.add, projected[b * block : (b + 1) * block])
                for b in range(nleaf // block)
            ]
        )
    place = 0
    for i, ref in zip(chosen, sum_refs):
        for j, c in enumerate(leaves_of(spans[i], size)):
            swapped = sums[0][(c // (nleaf >> 1)) ^ 1]
            for level in range(1, near // rank):
                swapped = jnp.where(lane == level, sums[level][(c // (nleaf >> (level + 1))) ^ 1], swapped)
            columns = slice(c * size, (c + 1) * size)
            value = ref[:, j * size : (j + 1) * size]
            value = value + dot(q.astype(jnp.bfloat16), u_ref[:far, columns])
            value = value + dot(swapped.astype(jnp.bfloat16), u_ref[far:, columns])
            out_ref[:, place : place + size] = value.astype(jnp.bfloat16)
            place += size
    if sends:
        before = earlier_ref.shape[1]
        total = dot(earlier_ref[...], next_ref[:before, :]) + dot(out_ref[...], next_ref[before:, :])
        p_out[...] = total.astype(p_out.dtype)


def far_part(rank, size, spans, chosen, sums, projected, q, parts, levels_of, u, last, sends=()):
    args = [*[sums[i] for i in chosen], *projected, q, *parts, u, *sends]
    width = sum(sums[i].shape[1] for i in chosen)
    space = jax.ShapeDtypeStruct if last else pltpu.VMEM
    outs = [space((q.shape[0], width), jnp.bfloat16), pltpu.VMEM(q.shape, jnp.float32)]
    outs += [pltpu.VMEM((q.shape[0], sends[0].shape[1]), jnp.bfloat16)] if sends else []
    kernel = functools.partial(far_kernel, rank, size, spans, chosen, tuple(levels_of) if parts else (), len(sends) > 0)
    return call(kernel, outs, args, {len(chosen) + len(projected): 1})


def local(sources, leaves, v_rows, u_rows):
    devices = lax.axis_size("hodlr")
    chain = lax.axis_size("slab")
    cross = devices.bit_length() - 1
    source, right = sources[0], v_rows[0]
    levels, rank, width = right.shape
    nleaf, size = leaves.shape[1:3]
    cut = max(nleaf * FIRST_SHARE // 4, 1) * size
    spans = ((0, cut), (cut, width))
    offsets = list(range(1, devices))
    levels_of = [cross - x.bit_length() for x in offsets]

    def moved(x, moves, offset=0):
        route = [(a * devices + h, b * devices + (h ^ offset)) for a, b in moves for h in range(devices)]
        return lax.ppermute(x, ("slab", "hodlr"), route)

    def exchanged(p, moves):
        return [moved(p, moves, x) for x in offsets]

    (coarse_v, fine_v, ahead_v), w = fetch(spans, cross, source, right)
    later = [(k, k - 1) for k in range(IN_PLACE + 1, chain)]
    early = moved(ahead_v, [(1, 0)] + later)
    coarse = moved(coarse_v, later)
    ranks = cross * rank
    whole = ((0, width),)
    p = project(spans, w, [coarse_v, fine_v], ranks, OPEN_FLOPS)
    parts = exchanged(p, [(k, k) for k in range(chain)])
    leaf, u = leaves[0], u_rows[0].reshape(levels * rank, width)
    near_v, sums, projected = first_part(spans, cross, w, leaf, right)

    q = jnp.zeros(p.shape, jnp.float32)
    every = tuple(range(len(spans)))
    far = functools.partial(far_part, rank, size, spans)
    out, q = far(every, sums, projected, q, parts, levels_of, u, False)
    front = [moved(out, [(0, 1)])]
    ahead = [project(whole, [out], [early], ranks)]
    relayed = offsets[1::2]
    parts = [moved(ahead[0], [(0, 1)], x) for x in relayed]
    second = moved(put_behind(coarse_v, ahead[0]), [(2, 1)])
    levels_relayed = [cross - x.bit_length() for x in relayed]
    for k in range(1, chain):
        levels_now = levels_of[::-1]
        for i, span in enumerate(spans):
            behind = projected[i - 1 : i] if i else ahead if k == 1 else []
            if i == 1 and k <= IN_PLACE:
                if k == IN_PLACE:
                    turned = turn(size, [coarse, early[-rank:]])
                nearby = nearby_part(
                    rank,
                    front[0],
                    fine_v,
                    ranks,
                    parts,
                    levels_relayed,
                    behind + (ahead if k == 1 else [turned]),
                    OPEN_FLOPS,
                )
                parts = [moved(nearby, [(k, k)], offsets[0])] + parts
                levels_now = [None] + levels_relayed
                behind = [nearby]
            given, start = (front[0], span[0]) if len(front) == 1 else (front[i], 0)
            w[i], sums[i], projected[i] = near_part(span, start, (levels - cross) * rank, w[i], given, leaf, near_v, behind)
        if k == chain - 1:
            out, _ = far(every, sums, projected, q, parts, levels_now, u, True)
            return out[None]
        split = k >= IN_PLACE and k != WHOLE_HOP
        outs, front = [], []
        for chosen in [(i,) for i in every] if split else [every]:
            sends = [turned, outs[0]] if outs else []
            out, q, *p = far(chosen, sums, projected, q, [] if front else parts, levels_now, u, False, sends)
            outs.append(out)
            front.append(moved(out, [(k, k + 1)]))
        if k < IN_PLACE:
            p = project(whole, outs, [second], ranks)
        else:
            p = p[0] if split else project_turned(whole, outs, turned)
        sent = relayed if k < IN_PLACE else offsets[::-1]
        parts = [moved(p, [(k, k + 1)], x) for x in sent]


def solution(mesh):
    in_specs = (
        P("slab", None, "hodlr"),
        P("slab", "hodlr", None, None),
        P("slab", None, None, "hodlr"),
        P("slab", None, None, "hodlr"),
    )
    out_specs = P("slab", None, "hodlr")
    return jax.shard_map(local, mesh=mesh, in_specs=in_specs, out_specs=out_specs, check_vma=False)
```

```python
import functools

import jax
import jax.numpy as jnp
from jax import lax
from jax.experimental import pallas as pl
from jax.experimental.pallas import tpu as pltpu
from jax.sharding import PartitionSpec as P

VMEM_LIMIT = 24 * 1024 * 1024
FIRST_SHARE = 2
IN_PLACE = 2
WHOLE_HOP = 5
OPEN_FLOPS = 4 * 10**9
ROWS_TIMES_COLUMNS = (((1,), (0,)), ((), ()))
ROWS_TIMES_ROWS = (((1,), (1,)), ((), ()))


def dot(a, b, dims=ROWS_TIMES_COLUMNS):
    return lax.dot_general(a, b, dims, preferred_element_type=jnp.float32)


def call(kernel, outs, args, aliases=None, scratch=(), from_hbm=(), flops=0):
    whole = pl.BlockSpec(memory_space=pltpu.VMEM)
    remote = pl.BlockSpec(memory_space=pl.ANY)
    placed = [
        pltpu.with_memory_space_constraint(a, pltpu.HBM if i in from_hbm else pltpu.VMEM)
        for i, a in enumerate(args)
    ]
    return pl.pallas_call(
        kernel,
        out_shape=outs,
        in_specs=[remote if i in from_hbm else whole for i in range(len(args))],
        out_specs=[whole] * len(outs),
        scratch_shapes=scratch,
        input_output_aliases=aliases or {},
        compiler_params=pltpu.CompilerParams(vmem_limit_bytes=VMEM_LIMIT),
        cost_estimate=pl.CostEstimate(flops=flops, bytes_accessed=0, transcendentals=0),
    )(*placed)


def on_factors(value, v_refs, columns, ranks):
    pieces = [dot(value, ref[:, columns], ROWS_TIMES_ROWS) for ref in v_refs]
    missing = ranks - sum(ref.shape[0] for ref in v_refs)
    if missing:
        pieces.append(jnp.zeros((value.shape[0], missing), jnp.float32))
    return jnp.concatenate(pieces, axis=1)


def fetch_kernel(spans, source_ref, v_ref, *refs):
    v_outs, w_outs, sems = refs[: -1 - len(spans)], refs[-1 - len(spans) : -1], refs[-1]
    copies, level = [], 0
    for out in v_outs[:-1]:
        copies.append((v_ref.at[pl.ds(level, out.shape[0])], out))
        level += out.shape[0]
    first = jnp.where(lax.axis_index("slab") == 1, 0, 1)
    copies.append((v_ref.at[pl.ds(first, v_outs[-1].shape[0])], v_outs[-1]))
    for out, (start, stop) in zip(w_outs, spans):
        copies.append((source_ref.at[:, pl.ds(start, stop - start)], out))
    copies = [pltpu.make_async_copy(a, b, sems.at[i]) for i, (a, b) in enumerate(copies)]
    for copy in copies:
        copy.start()
    for copy in copies:
        copy.wait()


def fetch(spans, cross, source, v):
    _, rank, width = v.shape
    shares = (cross - 1, 1, cross - 1)
    outs = [pltpu.VMEM((n, rank, width), v.dtype) for n in shares]
    outs += [pltpu.VMEM((source.shape[0], stop - start), source.dtype) for start, stop in spans]
    found = call(
        functools.partial(fetch_kernel, spans),
        outs,
        [source, v],
        scratch=[pltpu.SemaphoreType.DMA((len(outs),))],
        from_hbm=(0, 1),
    )
    return [f.reshape(-1, width) for f in found[: len(shares)]], list(found[len(shares) :])


def behind_kernel(x_ref, other_ref, out_ref):
    out_ref[...] = x_ref[...]


def put_behind(x, other):
    return call(behind_kernel, [pltpu.VMEM(x.shape, x.dtype)], [x, other], flops=OPEN_FLOPS)[0]


def project_kernel(spans, factors, *refs):
    v_refs, parts, p_ref = refs[:factors], refs[factors:-1], refs[-1]
    total = None
    for ref, (start, stop) in zip(parts, spans):
        term = on_factors(ref[...], v_refs, slice(start, stop), p_ref.shape[1])
        total = term if total is None else total + term
    p_ref[...] = total.astype(p_ref.dtype)


def project(spans, w, far_v, ranks, flops=0):
    outs = [pltpu.VMEM((w[0].shape[0], ranks), jnp.bfloat16)]
    return call(functools.partial(project_kernel, spans, len(far_v)), outs, [*far_v, *w], flops=flops)[0]


def turn_kernel(size, *refs):
    v_refs, out_ref = refs[:-1], refs[-1]
    for c in range(out_ref.shape[0] // size):
        rows = slice(c * size, (c + 1) * size)
        out_ref[rows, :] = jnp.concatenate([ref[:, rows] for ref in v_refs], axis=0).T


def turn(size, v):
    outs = [pltpu.VMEM((v[0].shape[1], sum(x.shape[0] for x in v)), v[0].dtype)]
    return call(functools.partial(turn_kernel, size), outs, v)[0]


def project_turned_kernel(spans, v_ref, *refs):
    parts, p_ref = refs[:-1], refs[-1]
    total = None
    for ref, (start, stop) in zip(parts, spans):
        term = dot(ref[...], v_ref[start:stop, :])
        total = term if total is None else total + term
    p_ref[...] = total.astype(p_ref.dtype)


def project_turned(spans, w, v):
    outs = [pltpu.VMEM((w[0].shape[0], v.shape[1]), jnp.bfloat16)]
    return call(functools.partial(project_turned_kernel, spans), outs, [v, *w])[0]


def leaves_of(span, size):
    return range(span[0] // size, span[1] // size)


def first_kernel(spans, cross, *refs):
    n = len(spans)
    w_refs, (leaf_ref, v_ref), near_out = refs[:n], refs[n : n + 2], refs[n + 2]
    sum_refs, p_refs = refs[n + 3 : 2 * n + 3], refs[2 * n + 3 :]
    size = leaf_ref.shape[1]
    near = p_refs[0].shape[2]
    for i, span in enumerate(spans):
        for j, c in enumerate(leaves_of(span, size)):
            columns = slice(j * size, (j + 1) * size)
            turned = v_ref[cross:, :, c * size : (c + 1) * size].reshape(near, size).T
            group = near_out.shape[2] // near
            near_out[c // group, :, c % group * near : (c % group + 1) * near] = turned
            p_refs[i][j] = dot(w_refs[i][:, columns], turned)
            sum_refs[i][:, columns] = dot(w_refs[i][:, columns], leaf_ref[c])


def first_part(spans, cross, w, leaf, v):
    levels, rank, width = v.shape
    size = leaf.shape[1]
    rows = w[0].shape[0]
    near = (levels - cross) * rank
    group = 2 if all((stop - start) // size % 2 == 0 for start, stop in spans) else 1
    outs = [pltpu.VMEM((width // size // group, size, group * near), v.dtype)]
    outs += [pltpu.VMEM(x.shape, jnp.float32) for x in w]
    outs += [pltpu.VMEM((x.shape[1] // size, rows, near), jnp.float32) for x in w]
    n = len(w)
    found = call(functools.partial(first_kernel, spans, cross), outs, [*w, leaf, v])
    return found[0], list(found[1 : 1 + n]), list(found[1 + n :])


def nearby_kernel(rank, levels_of, front_ref, v_ref, *refs):
    part_refs, p_ref = refs[: len(levels_of)], refs[-1]
    term = dot(front_ref[...], v_ref[...], ROWS_TIMES_ROWS)
    rows, ranks = p_ref.shape
    before = ranks - term.shape[1]
    if before:
        term = jnp.concatenate([jnp.zeros((rows, before), jnp.float32), term], axis=1)
    lane = lax.broadcasted_iota(jnp.int32, (rows, ranks), 1) // rank
    for ref, level in zip(part_refs, levels_of):
        term = term + jnp.where(lane == level, ref[...].astype(jnp.float32), 0.0)
    p_ref[...] = term.astype(p_ref.dtype)


def nearby_part(rank, front, v, ranks, parts, levels_of, behind, flops=0):
    outs = [pltpu.VMEM((front.shape[0], ranks), jnp.bfloat16)]
    return call(functools.partial(nearby_kernel, rank, tuple(levels_of)), outs, [front, v, *parts, *behind], flops=flops)[0]


def near_kernel(span, start, w_ref, front_ref, leaf_ref, v_ref, *refs):
    w_out, sum_out, p_out = refs[-3:]
    size = leaf_ref.shape[1]
    rows = w_ref.shape[0]
    near = p_out.shape[2]
    group = v_ref.shape[2] // near
    members = []
    for j, c in enumerate(leaves_of(span, size)):
        columns = slice(j * size, (j + 1) * size)
        w = w_ref[:, columns] + front_ref[:, start + j * size : start + (j + 1) * size]
        w_out[:, columns] = w
        members.append(w)
        if len(members) == group:
            both = dot(jnp.concatenate(members, axis=0), v_ref[c // group])
            for i in range(group):
                p_out[j - group + 1 + i] = both[i * rows : (i + 1) * rows, i * near : (i + 1) * near]
            members = []
        sum_out[:, columns] = dot(w, leaf_ref[c])


def near_part(span, start, near, w, front, leaf, near_v, behind):
    outs = [
        pltpu.VMEM(w.shape, w.dtype),
        pltpu.VMEM(w.shape, jnp.float32),
        pltpu.VMEM((w.shape[1] // leaf.shape[1], w.shape[0], near), jnp.float32),
    ]
    return call(functools.partial(near_kernel, span, start), outs, [w, front, leaf, near_v, *behind], {0: 0})


def far_kernel(rank, size, spans, chosen, levels_of, *refs):
    refs = list(refs)
    sum_refs = [refs.pop(0) for _ in chosen]
    p_refs = [refs.pop(0) for _ in spans]
    q_ref = refs.pop(0)
    part_refs = [refs.pop(0) for _ in levels_of]
    u_ref = refs.pop(0)
    out_ref, q_out = refs[:2]
    rows, far = q_ref.shape
    near = u_ref.shape[0] - far

    q = q_ref[...]
    lane = lax.broadcasted_iota(jnp.int32, (rows, far), 1) // rank
    for ref, level in zip(part_refs, levels_of):
        part = ref[...].astype(jnp.float32)
        q = q + (part if level is None else jnp.where(lane == level, part, 0.0))
    q_out[...] = q

    projected = [ref[j] for ref in p_refs for j in range(ref.shape[0])]
    nleaf = len(projected)
    lane = lax.broadcasted_iota(jnp.int32, (rows, near), 1) // rank
    sums = []
    for level in range(near // rank):
        block = nleaf >> (level + 1)
        sums.append(
            [
                functools.reduce(jnp.add, projected[b * block : (b + 1) * block])
                for b in range(nleaf // block)
            ]
        )
    place = 0
    for i, ref in zip(chosen, sum_refs):
        for j, c in enumerate(leaves_of(spans[i], size)):
            swapped = sums[0][(c // (nleaf >> 1)) ^ 1]
            for level in range(1, near // rank):
                swapped = jnp.where(lane == level, sums[level][(c // (nleaf >> (level + 1))) ^ 1], swapped)
            columns = slice(c * size, (c + 1) * size)
            value = ref[:, j * size : (j + 1) * size]
            value = value + dot(q.astype(jnp.bfloat16), u_ref[:far, columns])
            value = value + dot(swapped.astype(jnp.bfloat16), u_ref[far:, columns])
            out_ref[:, place : place + size] = value.astype(jnp.bfloat16)
            place += size


def far_part(rank, size, spans, chosen, sums, projected, q, parts, levels_of, u, last):
    args = [*[sums[i] for i in chosen], *projected, q, *parts, u]
    width = sum(sums[i].shape[1] for i in chosen)
    space = jax.ShapeDtypeStruct if last else pltpu.VMEM
    outs = [space((q.shape[0], width), jnp.bfloat16), pltpu.VMEM(q.shape, jnp.float32)]
    kernel = functools.partial(far_kernel, rank, size, spans, chosen, tuple(levels_of) if parts else ())
    return call(kernel, outs, args, {len(chosen) + len(projected): 1})


def local(sources, leaves, v_rows, u_rows):
    devices = lax.axis_size("hodlr")
    chain = lax.axis_size("slab")
    cross = devices.bit_length() - 1
    source, right = sources[0], v_rows[0]
    levels, rank, width = right.shape
    nleaf, size = leaves.shape[1:3]
    cut = max(nleaf * FIRST_SHARE // 4, 1) * size
    spans = ((0, cut), (cut, width))
    offsets = list(range(1, devices))
    levels_of = [cross - x.bit_length() for x in offsets]

    def moved(x, moves, offset=0):
        route = [(a * devices + h, b * devices + (h ^ offset)) for a, b in moves for h in range(devices)]
        return lax.ppermute(x, ("slab", "hodlr"), route)

    def exchanged(p, moves):
        return [moved(p, moves, x) for x in offsets]

    (coarse_v, fine_v, ahead_v), w = fetch(spans, cross, source, right)
    later = [(k, k - 1) for k in range(IN_PLACE + 1, chain)]
    early = moved(ahead_v, [(1, 0)] + later)
    coarse = moved(coarse_v, later)
    ranks = cross * rank
    whole = ((0, width),)
    p = project(spans, w, [coarse_v, fine_v], ranks, OPEN_FLOPS)
    parts = exchanged(p, [(k, k) for k in range(chain)])
    leaf, u = leaves[0], u_rows[0].reshape(levels * rank, width)
    near_v, sums, projected = first_part(spans, cross, w, leaf, right)

    q = jnp.zeros(p.shape, jnp.float32)
    every = tuple(range(len(spans)))
    far = functools.partial(far_part, rank, size, spans)
    out, q = far(every, sums, projected, q, parts, levels_of, u, False)
    front = [moved(out, [(0, 1)])]
    ahead = [project(whole, [out], [early], ranks)]
    relayed = offsets[1::2]
    parts = [moved(ahead[0], [(0, 1)], x) for x in relayed]
    second = moved(put_behind(coarse_v, ahead[0]), [(2, 1)])
    levels_relayed = [cross - x.bit_length() for x in relayed]
    for k in range(1, chain):
        levels_now = levels_of[::-1]
        for i, span in enumerate(spans):
            behind = projected[i - 1 : i] if i else ahead if k == 1 else []
            if i == 1 and k <= IN_PLACE:
                if k == IN_PLACE:
                    turned = turn(size, [coarse, early[-rank:]])
                nearby = nearby_part(
                    rank,
                    front[0],
                    fine_v,
                    ranks,
                    parts,
                    levels_relayed,
                    behind + (ahead if k == 1 else [turned]),
                    OPEN_FLOPS,
                )
                parts = [moved(nearby, [(k, k)], offsets[0])] + parts
                levels_now = [None] + levels_relayed
                behind = [nearby]
            given, start = (front[0], span[0]) if len(front) == 1 else (front[i], 0)
            w[i], sums[i], projected[i] = near_part(span, start, (levels - cross) * rank, w[i], given, leaf, near_v, behind)
        if k == chain - 1:
            out, _ = far(every, sums, projected, q, parts, levels_now, u, True)
            return out[None]
        split = k >= IN_PLACE and k != WHOLE_HOP
        outs, front = [], []
        for chosen in [(i,) for i in every] if split else [every]:
            out, q = far(chosen, sums, projected, q, [] if front else parts, levels_now, u, False)
            outs.append(out)
            front.append(moved(out, [(k, k + 1)]))
        if k < IN_PLACE:
            p = project(whole, outs, [second], ranks)
        else:
            p = project_turned(spans if split else whole, outs, turned)
        sent = relayed if k < IN_PLACE else offsets[::-1]
        parts = [moved(p, [(k, k + 1)], x) for x in sent]


def solution(mesh):
    in_specs = (
        P("slab", None, "hodlr"),
        P("slab", "hodlr", None, None),
        P("slab", None, None, "hodlr"),
        P("slab", None, None, "hodlr"),
    )
    out_specs = P("slab", None, "hodlr")
    return jax.shard_map(local, mesh=mesh, in_specs=in_specs, out_specs=out_specs, check_vma=False)
```
